32 devices in a mesh: dp: 8 (over y, x, core), ctx: 4 (over z).
Axes of the slice: x: 2, y: 2, z: 4, core: 2. Of those that a mesh axis runs over, the one named last changes fastest.
Arguments:
- tokens: bfloat16 [8192, 2048], P(('dp', 'ctx')), may hold values from -6 to 6
- span_order: int32 [8, 8], P('dp'), may hold values from 0 to 7, each once within a row
- norm_attn: bfloat16 [2048], P(('dp', 'ctx')), may hold values from 0.5 to 1.5
- w_query: bfloat16 [2048, 2048], P(('dp', 'ctx')), may hold values from -0.125 to 0.125
- w_key: bfloat16 [2048, 256], P(('dp', 'ctx')), may hold values from -0.125 to 0.125
- w_value: bfloat16 [2048, 256], P(('dp', 'ctx')), may hold values from -0.125 to 0.125
- w_out: bfloat16 [2048, 2048], P(('dp', 'ctx')), may hold values from -1.5 to 1.5
- norm_mlp: bfloat16 [2048], P(('dp', 'ctx')), may hold values from 0.5 to 1.5
- w_gate: bfloat16 [2048, 5632], P(('dp', 'ctx')), may hold values from -0.125 to 0.125
- w_up: bfloat16 [2048, 5632], P(('dp', 'ctx')), may hold values from -0.125 to 0.125
- w_down: bfloat16 [5632, 2048], P(('dp', 'ctx')), may hold values from -0.15625 to 0.15625
- out_grad: bfloat16 [8192, 2048], P(('dp', 'ctx')), may hold values from -6 to 6
Outputs:
- layer_out: bfloat16 [8192, 2048], P(('dp', 'ctx'))
- input_grad: float32 [8192, 2048], P(('dp', 'ctx'))
- grad_norm_attn: float32 [2048], P(('dp', 'ctx'))
- grad_query: float32 [2048, 2048], P(('dp', 'ctx'))
- grad_key: float32 [2048, 256], P(('dp', 'ctx'))
- grad_value: float32 [2048, 256], P(('dp', 'ctx'))
- grad_out: float32 [2048, 2048], P(('dp', 'ctx'))
- grad_norm_mlp: float32 [2048], P(('dp', 'ctx'))
- grad_gate: float32 [2048, 5632], P(('dp', 'ctx'))
- grad_up: float32 [2048, 5632], P(('dp', 'ctx'))
- grad_down: float32 [5632, 2048], P(('dp', 'ctx'))
The draws below stay inside these ranges and needn't reach their ends.
Inputs may be any that keep to these rules, and one draw needn't show every extreme that they name: `span_order`: each row is a permutation of the 8 block numbers of one sequence.
All inputs are finite; a program needn't handle non-finite values.
Results may differ from the reference program's by a relative error of at most 0.018.
Values may be sent and summed in bfloat16 or wider, within the bound.
No kernel may reach another device: no remote copies, remote signals or barrier semaphores. Data moves between devices by JAX's collectives and lax.ppermute only.
A program may use at most 448 MiB of HBM per device.

```python
import jax
import jax.numpy as jnp
from jax import lax

D = 2048
H = 32
KV = 4
HD = 64
FF = 5632
SPAN = 128
SPANS = 8
SEQ_LEN = 1024
TOKENS = 8192
N_DP = 8


def shard_levels(key, shape, pieces, low, top_value):
    loudness = 1.0
    for position, blocks in pieces:
        draws = jax.random.uniform(jax.random.fold_in(jax.random.fold_in(key, 6), position), (blocks,), jnp.float32, low / len(pieces), top_value / len(pieces))
        loudness = loudness * jnp.repeat(jnp.exp(draws), shape[position] // blocks).reshape((-1,) + (1,) * (len(shape) - 1 - position))
    return loudness


def bell_draw(stream_key, shape, deviation, limit, pieces=(), kind=jnp.bfloat16):
    values = jax.random.normal(stream_key, shape, jnp.float32) * deviation
    if len(pieces) > 0:
        values = shard_levels(stream_key, shape, pieces, -0.22, 0.18) * values
    return jnp.clip(values, min=-limit, max=limit).astype(kind)


def setup_inputs(seed: int = 0) -> dict:
    key_of = jax.random.split(jax.random.key(seed), 13)
    tokens = bell_draw(key_of[0], (TOKENS, D), 1.0, 6.0, ((0, 32),))
    span_order = jax.vmap(lambda own: jax.random.permutation(own, SPANS))(jax.random.split(key_of[1], N_DP)).reshape((N_DP, SPANS)).astype(jnp.int32)
    norm_attn = jnp.clip(1.0 + 0.1 * jax.random.normal(key_of[2], (D,), jnp.float32), 0.5, 1.5).astype(jnp.bfloat16)
    w_query = bell_draw(key_of[3], (D, D), D ** -0.5, 0.125, ((0, 32),))
    w_key = bell_draw(key_of[4], (D, KV * HD), D ** -0.5, 0.125, ((0, 32),))
    w_value = bell_draw(key_of[5], (D, KV * HD), D ** -0.5, 0.125, ((0, 32),))
    w_out = bell_draw(key_of[6], (D, D), (max(1, D * 8 // SEQ_LEN)) ** -0.5, 1.5, ((0, 32),))
    norm_mlp = jnp.clip(1.0 + 0.1 * jax.random.normal(key_of[7], (D,), jnp.float32), 0.5, 1.5).astype(jnp.bfloat16)
    w_gate = bell_draw(key_of[8], (D, FF), D ** -0.5, 0.125, ((0, 32),))
    w_up = bell_draw(key_of[9], (D, FF), D ** -0.5, 0.125, ((0, 32),))
    w_down = bell_draw(key_of[10], (FF, D), (FF // 4) ** -0.5, 0.15625, ((0, 32),))
    out_grad = bell_draw(key_of[11], (TOKENS, D), 1.0, 6.0, ((0, 32),))
    return {"tokens": tokens, "span_order": span_order, "norm_attn": norm_attn, "w_query": w_query, "w_key": w_key, "w_value": w_value, "w_out": w_out, "norm_mlp": norm_mlp, "w_gate": w_gate, "w_up": w_up, "w_down": w_down, "out_grad": out_grad}


epsilon = 1e-05
rope_base = 10000.0
masked_score = -1e+30
highest = lax.Precision.HIGHEST

@jax.custom_vjp
def low(v):
    return lax.optimization_barrier(v.astype(jnp.bfloat16)).astype(jnp.float32)

@jax.custom_vjp
def low_back(v):
    return v

def low_keep(v):
    return (low(v), None)

def low_pass(kept, grad):
    return (grad,)

def back_keep(v):
    return (v, None)

def back_low(kept, grad):
    return (low(grad),)
low.defvjp(low_keep, low_pass)
low_back.defvjp(back_keep, back_low)

def matmul(left, right):
    return jnp.dot(left, right, precision=highest)

def normalize(inputs, gain):
    return inputs * lax.rsqrt(lax.optimization_barrier(jnp.mean(inputs * inputs, axis=-1, keepdims=True)) + epsilon) * gain

def rotate(vectors, positions, head_count):
    half_dim = HD // 2
    frequency = jnp.power(rope_base, -jnp.arange(half_dim, dtype=jnp.float32) / half_dim)
    angles = positions[:, None] * frequency[None, :]
    cosine = jnp.cos(angles)[:, None, :]
    sine_part = jnp.sin(angles)[:, None, :]
    shaped = vectors.reshape(vectors.shape[0], head_count, HD)
    first_half = shaped[..., :half_dim]
    second_half = shaped[..., half_dim:]
    turned = jnp.concatenate([first_half * cosine - second_half * sine_part, second_half * cosine + first_half * sine_part], axis=-1)
    return turned.reshape(vectors.shape[0], head_count * HD)

def layer_forward(inputs, norm_attn, w_query, w_key, w_value, w_out, norm_mlp, w_gate, w_up, w_down, positions, visible):
    seq_rows = inputs.shape[0]
    group_size = H // KV
    normed = low(normalize(inputs, norm_attn))
    queries = low(rotate(low_back(matmul(normed, w_query)), positions, H))
    keys_all = low(rotate(low_back(matmul(normed, w_key)), positions, KV))
    values_all = low(low_back(matmul(normed, w_value)))
    grouped = queries.reshape(seq_rows, KV, group_size, HD)
    key_heads = keys_all.reshape(seq_rows, KV, HD)
    value_heads = values_all.reshape(seq_rows, KV, HD)
    raw_scores = low_back(jnp.einsum('qkgd,tkd->kgqt', grouped, key_heads, precision=highest))
    scores = jnp.where(visible, raw_scores * HD ** (-0.5), masked_score)
    probabilities = low(jax.nn.softmax(scores, axis=-1))
    mixture = jnp.einsum('kgqt,tkd->qkgd', probabilities, value_heads, precision=highest).reshape(seq_rows, H * HD)
    attended = low(low_back(mixture))
    middle = inputs + low_back(matmul(attended, w_out))
    normed_mlp = low(normalize(middle, norm_mlp))
    gate_part = low_back(matmul(normed_mlp, w_gate))
    up_part = low_back(matmul(normed_mlp, w_up))
    hidden = low(jax.nn.silu(gate_part) * up_part)
    return middle + low_back(matmul(hidden, w_down))

def reference(tokens, span_order, norm_attn, w_query, w_key, w_value, w_out, norm_mlp, w_gate, w_up, w_down, out_grad):
    params = tuple((weight_arg.astype(jnp.float32) for weight_arg in (norm_attn, w_query, w_key, w_value, w_out, norm_mlp, w_gate, w_up, w_down)))
    inputs = tokens.astype(jnp.float32).reshape(N_DP, SEQ_LEN, D)
    cotangents = out_grad.astype(jnp.float32).reshape(N_DP, SEQ_LEN, D)
    offsets = jnp.arange(SPAN, dtype=jnp.int32)

    def per_sequence(sums, members):
        sequence, cotangent, ordering = members
        positions = (ordering[:, None] * SPAN + offsets[None, :]).reshape(SEQ_LEN).astype(jnp.int32)
        visible = positions[:, None] >= positions[None, :]
        angles_pos = positions.astype(jnp.float32)

        def forward(inputs_seq, *weights):
            return layer_forward(inputs_seq, *weights, angles_pos, visible)
        result, pullback = jax.vjp(forward, sequence, *params)
        grads = pullback(cotangent)
        sums = tuple((running + part for running, part in zip(sums, grads[1:])))
        return (sums, (result, grads[0]))
    zeros = tuple((jnp.zeros_like(weight_arg) for weight_arg in params))
    sums, (results, input_grads) = lax.scan(per_sequence, zeros, (inputs, cotangents, span_order))
    layer_out = results.reshape(TOKENS, D).astype(jnp.bfloat16)
    input_grad = input_grads.reshape(TOKENS, D)
    return (layer_out, input_grad, sums[0], sums[1], sums[2], sums[3], sums[4], sums[5], sums[6], sums[7], sums[8])
```

```python
import jax
import jax.numpy as jnp
from jax import lax
from jax.sharding import Mesh, PartitionSpec as P

H = 32
KV = 4
HD = 64
TP = 4
GROUP = H // KV

epsilon = 1e-05
rope_base = 10000.0
masked_score = -1e30
bf16 = jnp.bfloat16
f32 = jnp.float32


def dot(left, right):
    return jnp.dot(left, right, preferred_element_type=f32)


def contract_rows(left, right):
    return lax.dot_general(left, right, (((0,), (0,)), ((), ())), preferred_element_type=f32)


def contract_cols(left, right):
    return lax.dot_general(left, right, (((1,), (1,)), ((), ())), preferred_element_type=f32)


def rope_tables(positions):
    half_dim = HD // 2
    frequency = jnp.power(rope_base, -jnp.arange(half_dim, dtype=f32) / half_dim)
    angles = positions.astype(f32)[:, None] * frequency[None, :]
    return jnp.cos(angles)[:, None, :], jnp.sin(angles)[:, None, :]


def rotate(vectors, tables, sign):
    cosine, sine = tables
    sine = sine * sign
    rows, width = vectors.shape
    shaped = vectors.reshape(rows, width // HD, HD)
    first, second = shaped[..., : HD // 2], shaped[..., HD // 2 :]
    turned = jnp.concatenate(
        [first * cosine - second * sine, second * cosine + first * sine], axis=-1
    )
    return turned.reshape(rows, width)


def attend(queries, keys, values, visible):
    rows = queries.shape[0]
    stacked = queries.reshape(rows, GROUP, HD).transpose(1, 0, 2).reshape(GROUP * rows, HD)
    scores = contract_cols(stacked, keys) * HD ** (-0.5)
    scores = jnp.where(visible, scores.reshape(GROUP, rows, -1), masked_score)
    maximum = jnp.max(scores, axis=-1, keepdims=True)
    exponent = jnp.exp(scores - maximum)
    total = jnp.sum(exponent, axis=-1, keepdims=True)
    weights = (exponent / total).astype(bf16).reshape(GROUP * rows, -1)
    mixed = dot(weights, values)
    return mixed, maximum + jnp.log(total)


def attend_back(queries, keys, values, visible, grads, mixed, logsum):
    rows = queries.shape[0]

    def stack(v):
        return v.reshape(rows, GROUP, HD).transpose(1, 0, 2).reshape(GROUP * rows, HD)

    queries, grads = stack(queries), stack(grads)
    scores = contract_cols(queries, keys) * HD ** (-0.5)
    scores = jnp.where(visible, scores.reshape(GROUP, rows, -1), masked_score)
    probabilities = jnp.exp(scores - logsum).reshape(GROUP * rows, -1)
    grad_prob = contract_cols(grads, values)
    delta = jnp.sum(grads.astype(f32) * mixed, axis=-1, keepdims=True)
    grad_score = (probabilities * (grad_prob - delta) * HD ** (-0.5)).astype(bf16)
    grad_queries = dot(grad_score, keys)
    grad_keys = contract_rows(grad_score, queries)
    grad_values = contract_rows(probabilities.astype(bf16), grads)
    return unstack(grad_queries, rows), grad_keys, grad_values


def unstack(v, rows):
    return v.reshape(GROUP, rows, HD).transpose(1, 0, 2).reshape(rows, GROUP * HD)


def make_body(reps, ctxs):
    def swap(v, k):
        if k == 0:
            return v
        if k == 1:
            return lax.ppermute(v, "tx", [(0, 1), (1, 0)])
        if k == 2:
            return lax.ppermute(v, "ty", [(0, 1), (1, 0)])
        return lax.ppermute(v, ("ty", "tx"), [(i, i ^ 3) for i in range(TP)])

    def swap_ctx(v, j):
        if j == 0:
            return v
        return lax.ppermute(v, "ctx", [(i, i ^ j) for i in range(ctxs)])

    def gather(v):
        half = v.shape[0] // 2
        a, b = v[:half], v[half:]
        ax, by = swap(a, 1), swap(b, 2)
        ay, bx = swap(a, 2), swap(b, 1)
        axy, bxy = swap(ax, 2), swap(by, 1)
        return jnp.concatenate([a, b, ax, bx, ay, by, axy, bxy], axis=0)

    def scatter_sum(parts):
        half = parts[0].shape[0] // 2
        a = [p[:half] for p in parts]
        b = [p[half:] for p in parts]
        a3, b3 = swap(a[3].astype(bf16), 2), swap(b[3].astype(bf16), 1)
        a2, b1 = swap(a[2].astype(bf16), 2), swap(b[1].astype(bf16), 1)
        a1 = swap((a[1] + a3).astype(bf16), 1)
        b2 = swap((b[2] + b3).astype(bf16), 2)
        return jnp.concatenate([a[0] + a2 + a1, b[0] + b1 + b2], axis=0)

    def spread_columns(blocks, t):
        out = jnp.zeros_like(blocks)
        for k in range(TP):
            mine = lax.dynamic_index_in_dim(blocks, t ^ k, 0, keepdims=True)
            out = lax.dynamic_update_slice_in_dim(out, swap(mine, k), t ^ k, 0)
        return out.reshape(-1, blocks.shape[2])

    def collect_columns(summed, t):
        blocks = summed.reshape(TP, -1, summed.shape[1])
        out = jnp.zeros_like(blocks)
        for k in range(TP):
            mine = lax.dynamic_index_in_dim(blocks, t ^ k, 0, keepdims=True)
            out = lax.dynamic_update_slice_in_dim(out, swap(mine, k), t ^ k, 0)
        return out.transpose(1, 0, 2)

    def whole(v):
        return lax.all_gather(v, ("rep", "ctx"), axis=0, tiled=True)

    def owned(v):
        v = lax.psum_scatter(v.astype(bf16), "rep", scatter_dimension=0, tiled=True)
        return lax.psum_scatter(v, "ctx", scatter_dimension=0, tiled=True)

    def shuffle(v):
        rows, width = v.shape
        return (
            v.reshape(rows, TP, reps * ctxs, -1).transpose(0, 2, 1, 3).reshape(rows, width)
        )

    def unshuffle(v):
        rows, width = v.shape
        return (
            v.reshape(rows, reps * ctxs, TP, -1).transpose(0, 2, 1, 3).reshape(rows, width)
        )

    def body(
        tokens,
        span_order,
        norm_attn,
        w_query,
        w_key,
        w_value,
        w_out,
        norm_mlp,
        w_gate,
        w_up,
        w_down,
        out_grad,
    ):
        count, width = tokens.shape
        own = w_query.shape[0]
        span = count * ctxs // span_order.shape[1]
        q_cols, kv_cols = GROUP * HD, HD
        t = 2 * lax.axis_index("ty") + lax.axis_index("tx")
        c = lax.axis_index("ctx")

        x_all = gather(shuffle(tokens))
        orders = [swap(span_order, k)[0] for k in range(TP)]
        offsets = jnp.arange(span, dtype=jnp.int32)
        per = count // span

        def block_positions(order, member):
            picked = lax.dynamic_slice_in_dim(order, member * per, per)
            return (picked[:, None] * span + offsets[None, :]).reshape(-1)

        query_positions = [block_positions(order, c) for order in orders]
        key_positions = [
            jnp.concatenate([block_positions(order, c ^ j) for j in range(ctxs)])
            for order in orders
        ]
        visible = [
            q[:, None] >= k[None, :] for q, k in zip(query_positions, key_positions)
        ]
        tables = rope_tables(jnp.concatenate(query_positions))

        gain_attn = norm_attn.astype(f32)[:, None]
        gain_mlp = norm_mlp.astype(f32)[:, None]

        def by_member(w, gain):
            w = (w.astype(f32) * gain).astype(bf16)
            return w.reshape(own, TP, -1).transpose(1, 0, 2)

        blocks = jnp.concatenate(
            [by_member(w, gain_attn) for w in (w_query, w_key, w_value)], axis=2
        )
        qkv = whole(spread_columns(blocks, t))
        out = whole(w_out)
        gate = whole(spread_columns(by_member(w_gate, gain_mlp), t))
        up = whole(spread_columns(by_member(w_up, gain_mlp), t))
        down = whole(w_down)

        g_all = gather(out_grad)

        x32 = x_all.astype(f32)
        inverse_all = lax.rsqrt(jnp.mean(x32 * x32, axis=-1, keepdims=True) + epsilon)
        projected = dot(x_all, qkv) * inverse_all
        queries = rotate(projected[:, :q_cols], tables, 1.0).astype(bf16)
        keys = rotate(projected[:, q_cols : q_cols + kv_cols], tables, 1.0).astype(bf16)
        values = projected[:, q_cols + kv_cols :].astype(bf16)
        pair = jnp.concatenate([keys, values], axis=1).reshape(TP, count, 2 * kv_cols)
        pairs = jnp.concatenate([swap_ctx(pair, j) for j in range(ctxs)], axis=1)
        keys_seq, values_seq = pairs[..., :kv_cols], pairs[..., kv_cols:]
        queries = queries.reshape(TP, count, q_cols)

        kept, parts = [None] * TP, [None] * TP
        for k in (3, 2, 1, 0):
            mixed, logsum = attend(queries[k], keys_seq[k], values_seq[k], visible[k])
            attended = unstack(mixed, count).astype(bf16)
            parts[k] = dot(attended, out)
            kept[k] = (mixed, logsum, attended)
        inputs = tokens.astype(f32)
        middle = inputs + scatter_sum(parts)
        inverse_mid = lax.rsqrt(jnp.mean(middle * middle, axis=-1, keepdims=True) + epsilon)
        normed_mid = middle * inverse_mid
        n2_all = gather(shuffle(normed_mid.astype(bf16)))

        gate_part = dot(n2_all, gate)
        up_part = dot(n2_all, up)
        sigmoid = jax.nn.sigmoid(gate_part)
        hidden = (gate_part * sigmoid * up_part).astype(bf16)
        grad_hidden = contract_cols(g_all, down)
        grad_gate_b = (
            grad_hidden * up_part * sigmoid * (1.0 + gate_part * (1.0 - sigmoid))
        ).astype(bf16)
        grad_up_b = (grad_hidden * gate_part * sigmoid).astype(bf16)
        back_mid = contract_cols(grad_gate_b, gate) + contract_cols(grad_up_b, up)
        e2 = unshuffle(scatter_sum([back_mid[k * count : (k + 1) * count] for k in range(TP)]))
        sum_gate = collect_columns(owned(contract_rows(n2_all, grad_gate_b)), t)
        sum_up = collect_columns(owned(contract_rows(n2_all, grad_up_b)), t)
        grad_down = owned(contract_rows(hidden, g_all)).astype(f32)
        forward = dot(hidden, down)
        layer_out = (
            middle + scatter_sum([forward[k * count : (k + 1) * count] for k in range(TP)])
        ).astype(bf16)

        grad_middle = out_grad.astype(f32) + inverse_mid * (
            e2 - normed_mid * jnp.mean(e2 * normed_mid, axis=-1, keepdims=True)
        )
        db_all = gather(grad_middle.astype(bf16))
        attended_all = jnp.concatenate([kept[k][2] for k in range(TP)], axis=0)
        grad_attended = contract_cols(db_all, out).astype(bf16).reshape(TP, count, q_cols)
        sum_out = owned(contract_rows(attended_all, db_all)).astype(f32)
        grad_queries, grad_pairs = [], []
        for k in range(TP):
            mixed, logsum, _ = kept[k]
            dq, dk, dv = attend_back(
                queries[k], keys_seq[k], values_seq[k], visible[k], grad_attended[k], mixed, logsum
            )
            grad_queries.append(dq)
            grad_pairs.append(jnp.concatenate([dk, dv], axis=1).reshape(ctxs, count, 2 * kv_cols))
        grad_pairs = jnp.stack(grad_pairs, axis=1)
        local = grad_pairs[0]
        for j in range(1, ctxs):
            local = local + swap_ctx(grad_pairs[j].astype(bf16), j).astype(f32)
        local = local.reshape(TP * count, 2 * kv_cols)
        grad_proj = jnp.concatenate(
            [
                rotate(jnp.concatenate(grad_queries, axis=0), tables, -1.0),
                rotate(local[:, :kv_cols], tables, -1.0),
                local[:, kv_cols:],
            ],
            axis=1,
        )
        back = contract_cols(grad_proj.astype(bf16), qkv)
        e1 = unshuffle(scatter_sum([back[k * count : (k + 1) * count] for k in range(TP)]))
        sum_qkv = collect_columns(
            owned(contract_rows(x_all, (grad_proj * inverse_all).astype(bf16))), t
        ).astype(f32)
        inverse = lax.rsqrt(jnp.mean(inputs * inputs, axis=-1, keepdims=True) + epsilon)
        normed = inputs * inverse
        input_grad = grad_middle + inverse * (
            e1 - normed * jnp.mean(e1 * normed, axis=-1, keepdims=True)
        )

        def rows_of(v):
            return v.reshape(own, -1).astype(f32)

        raw_query = rows_of(sum_qkv[..., :q_cols])
        raw_key = rows_of(sum_qkv[..., q_cols : q_cols + kv_cols])
        raw_value = rows_of(sum_qkv[..., q_cols + kv_cols :])
        raw_gate, raw_up = rows_of(sum_gate), rows_of(sum_up)
        grad_norm_attn = (
            jnp.sum(raw_query * w_query.astype(f32), axis=1)
            + jnp.sum(raw_key * w_key.astype(f32), axis=1)
            + jnp.sum(raw_value * w_value.astype(f32), axis=1)
        )
        grad_norm_mlp = jnp.sum(raw_gate * w_gate.astype(f32), axis=1) + jnp.sum(
            raw_up * w_up.astype(f32), axis=1
        )
        return (
            layer_out,
            input_grad,
            grad_norm_attn,
            raw_query * gain_attn,
            raw_key * gain_attn,
            raw_value * gain_attn,
            sum_out,
            grad_norm_mlp,
            raw_gate * gain_mlp,
            raw_up * gain_mlp,
            grad_down,
        )

    return body


def solution(mesh):
    sequences, ctxs = mesh.shape["dp"], mesh.shape["ctx"]
    reps = sequences // TP
    grid = Mesh(mesh.devices.reshape(2, 2, reps, ctxs), ("ty", "tx", "rep", "ctx"))
    rows = ("ty", "tx", "rep", "ctx")
    matrix, vector = P(rows, None), P(rows)
    return jax.shard_map(
        make_body(reps, ctxs),
        mesh=grid,
        in_specs=(
            matrix,
            P(("ty", "tx", "rep"), None),
            vector,
            matrix,
            matrix,
            matrix,
            matrix,
            vector,
            matrix,
            matrix,
            matrix,
            matrix,
        ),
        out_specs=(
            matrix,
            matrix,
            vector,
            matrix,
            matrix,
            matrix,
            matrix,
            vector,
            matrix,
            matrix,
            matrix,
        ),
        check_vma=False,
    )
```

```python
import jax
import jax.numpy as jnp
from jax import lax
from jax.experimental import pallas as pl
from jax.experimental.pallas import tpu as pltpu
from jax.sharding import Mesh, PartitionSpec as P

H = 32
KV = 4
HD = 64
TP = 4
GROUP = H // KV
LANES = 128
ROWS = 64

epsilon = 1e-05
rope_base = 10000.0
masked_score = -1e30
bf16 = jnp.bfloat16
f32 = jnp.float32


def after(value, *others):
    return lax.optimization_barrier((value,) + others)[0]


def phase(*values):
    return lax.optimization_barrier(values)


def nn(left, right):
    return lax.dot_general(left, right, (((1,), (0,)), ((), ())), preferred_element_type=f32)


def nt(left, right):
    return lax.dot_general(left, right, (((1,), (1,)), ((), ())), preferred_element_type=f32)


def tn(left, right):
    return lax.dot_general(left, right, (((0,), (0,)), ((), ())), preferred_element_type=f32)


def turn(vectors, cosine, sine):
    half = HD // 2
    out = []
    for at in range(0, vectors.shape[0], HD):
        first, second = vectors[at : at + half], vectors[at + half : at + HD]
        out += [first * cosine - second * sine, second * cosine + first * sine]
    return jnp.concatenate(out, axis=0)


def project_kernel(x_ref, w_ref, cos_ref, sin_ref, qt_ref, kv_ref, inv_ref):
    x = x_ref[...].astype(f32)
    inverse = lax.rsqrt(jnp.mean(x * x, axis=1, keepdims=True) + epsilon)
    inv_ref[...] = inverse
    flat = (nn(x_ref[...], w_ref[...]) * inverse).T
    cosine, sine = cos_ref[...], sin_ref[...]
    q = GROUP * HD
    qt_ref[...] = (turn(flat[:q], cosine, sine) * HD**-0.5).astype(bf16)
    kv = jnp.concatenate([turn(flat[q : q + HD], cosine, sine), flat[q + HD :]], axis=0)
    kv_ref[...] = kv.T.astype(bf16)


def project(x, w, cosine, sine, rows):
    total, width = x.shape
    n = w.shape[1]
    steps, q = total // rows, GROUP * HD
    return pl.pallas_call(
        project_kernel,
        grid=(steps,),
        in_specs=[
            pl.BlockSpec((rows, width), lambda i: (i, 0)),
            pl.BlockSpec((width, n), lambda i: (0, 0)),
            pl.BlockSpec((HD // 2, rows), lambda i: (0, i)),
            pl.BlockSpec((HD // 2, rows), lambda i: (0, i)),
        ],
        out_specs=[
            pl.BlockSpec((None, q, rows), lambda i: (i, 0, 0)),
            pl.BlockSpec((rows, 2 * HD), lambda i: (i, 0)),
            pl.BlockSpec((rows, 1), lambda i: (i, 0)),
        ],
        out_shape=[
            jax.ShapeDtypeStruct((steps, q, rows), bf16),
            jax.ShapeDtypeStruct((total, 2 * HD), bf16),
            jax.ShapeDtypeStruct((total, 1), f32),
        ],
        compiler_params=pltpu.CompilerParams(vmem_limit_bytes=40 << 20),
        cost_estimate=pl.CostEstimate(
            flops=2 * total * width * n,
            bytes_accessed=2 * (total * width + width * n + total * n),
            transcendentals=0,
        ),
        name="project",
    )(x, w, cosine, sine)


def attend_kernel(qp_ref, kp_ref, qt_ref, kv_ref, wo_ref, ot_ref, lse_ref, part_ref, bias_ref):
    bias_ref[...] = jnp.where(qp_ref[...] >= kp_ref[...], 0.0, masked_score)
    kv = kv_ref[...]
    vt = kv.astype(f32).T[HD:].astype(bf16)
    zero = jnp.zeros((HD, qt_ref.shape[1]), bf16)
    for h in range(GROUP):
        at = slice(h * HD, (h + 1) * HD)
        scores = nn(kv, jnp.concatenate([qt_ref[at, :], zero], axis=0)) + bias_ref[...]
        top = jnp.max(scores, axis=0, keepdims=True)
        exponent = jnp.exp(scores - top)
        total = jnp.sum(exponent, axis=0, keepdims=True)
        ot_ref[at, :] = (nn(vt, exponent.astype(bf16)) / total).astype(bf16)
        lse_ref[h : h + 1, :] = top + jnp.log(total)
    part_ref[...] = tn(ot_ref[...], wo_ref[...]).astype(part_ref.dtype)


def attend(qp, kp, qt, kv, wo, kind):
    n, rows = qt.shape
    keys, width = kv.shape[0], wo.shape[1]
    return pl.pallas_call(
        attend_kernel,
        out_shape=[
            jax.ShapeDtypeStruct((n, rows), bf16),
            jax.ShapeDtypeStruct((GROUP, rows), f32),
            jax.ShapeDtypeStruct((rows, width), kind),
        ],
        scratch_shapes=[pltpu.VMEM((keys, rows), f32)],
        compiler_params=pltpu.CompilerParams(vmem_limit_bytes=40 << 20),
        cost_estimate=pl.CostEstimate(
            flops=2 * rows * n * (keys * 2 * 4 + width),
            bytes_accessed=2 * (n * rows * 2 + keys * 2 * HD + n * width + rows * width),
            transcendentals=GROUP * rows * keys,
        ),
        name="attend",
    )(qp, kp, qt, kv, wo)


def attend_back_kernel(
    qp_ref,
    kp_ref,
    qt_ref,
    kv_ref,
    wo_ref,
    ot_ref,
    lse_ref,
    db_ref,
    inv_ref,
    cos_ref,
    sin_ref,
    dq_ref,
    dqs_ref,
    dkv_ref,
    bias_ref,
    dat_ref,
    dqt_ref,
):
    bias_ref[...] = jnp.where(qp_ref[...] >= kp_ref[...], 0.0, masked_score)
    kv = kv_ref[...]
    kt = kv.astype(f32).T[:HD].astype(bf16)
    zero = jnp.zeros((HD, qt_ref.shape[1]), bf16)
    dat_ref[...] = nt(wo_ref[...], db_ref[...]).astype(bf16)
    for h in range(GROUP):
        at = slice(h * HD, (h + 1) * HD)
        q_low = jnp.concatenate([qt_ref[at, :], zero], axis=0)
        da_high = jnp.concatenate([zero, dat_ref[at, :]], axis=0)
        weights = jnp.exp(nn(kv, q_low) + bias_ref[...] - lse_ref[h : h + 1, :])
        delta = jnp.sum(
            dat_ref[at, :].astype(f32) * ot_ref[at, :].astype(f32), axis=0, keepdims=True
        )
        ds = (weights * (nn(kv, da_high) - delta)).astype(bf16)
        dkv = nt(ds, q_low) + nt(weights.astype(bf16), da_high)
        if h == 0:
            dkv_ref[...] = dkv
        else:
            dkv_ref[...] += dkv
        dqt_ref[at, :] = nn(kt, ds)
    dq = (turn(dqt_ref[...], cos_ref[...], -sin_ref[...]) * HD**-0.5).T
    dq_ref[...] = dq.astype(bf16)
    dqs_ref[...] = (dq * inv_ref[...]).astype(bf16)


def attend_back(qp, kp, qt, kv, wo, ot, lse, db, inv, cosine, sine):
    n, rows = qt.shape
    keys, width = kv.shape[0], wo.shape[1]
    return pl.pallas_call(
        attend_back_kernel,
        out_shape=[
            jax.ShapeDtypeStruct((rows, n), bf16),
            jax.ShapeDtypeStruct((rows, n), bf16),
            jax.ShapeDtypeStruct((keys, 2 * HD), f32),
        ],
        scratch_shapes=[
            pltpu.VMEM((keys, rows), f32),
            pltpu.VMEM((n, rows), bf16),
            pltpu.VMEM((n, rows), f32),
        ],
        compiler_params=pltpu.CompilerParams(vmem_limit_bytes=40 << 20),
        cost_estimate=pl.CostEstimate(
            flops=2 * rows * n * (keys * 5 * 4 + width),
            bytes_accessed=2 * (n * rows * 4 + keys * 6 * HD + n * width + rows * width),
            transcendentals=GROUP * rows * keys,
        ),
        name="attend_back",
    )(qp, kp, qt, kv, wo, ot, lse, db, inv, cosine, sine)


def reorder_lanes(v, ordered):
    shape, size = ordered
    out = []
    for index in shape:
        out.append(v[:, index * size : (index + 1) * size])
    return jnp.concatenate(out, axis=1)


def block_orders(width, holders):
    held = [m * holders + h for h in range(holders) for m in range(TP)]
    natural = [held.index(i) for i in range(len(held))]
    size = width // len(held)
    return (held, size), (natural, size)


def small_call(kernel, name, inputs, outputs):
    size = sum(v.size * v.dtype.itemsize for v in (*inputs, *outputs))
    return pl.pallas_call(
        kernel,
        out_shape=outputs,
        compiler_params=pltpu.CompilerParams(vmem_limit_bytes=40 << 20),
        cost_estimate=pl.CostEstimate(flops=size, bytes_accessed=size, transcendentals=0),
        name=name,
    )(*inputs)


def hold_tokens(tokens, held):
    def kernel(x_ref, out_ref):
        out_ref[...] = reorder_lanes(x_ref[...].astype(f32), held).astype(bf16)

    return small_call(
        kernel, "hold_tokens", [tokens], [jax.ShapeDtypeStruct(tokens.shape, bf16)]
    )[0]


def summed(own_ref, a2_ref, a1_ref, b1_ref, b2_ref, at, half):
    first, second = (a2_ref, a1_ref) if at < half else (b1_ref, b2_ref)
    rows = slice(at, at + ROWS)
    come = slice(at % half, at % half + ROWS)
    return own_ref[rows, :] + first[come, :].astype(f32) + second[come, :].astype(f32)


def finish_middle(tokens, pieces, held):
    rows, width = tokens.shape

    def kernel(x_ref, *refs):
        sums, (mid_ref, inv_ref, n2_ref) = refs[:5], refs[5:]
        for at in range(0, rows, ROWS):
            here = slice(at, at + ROWS)
            middle = x_ref[here, :].astype(f32) + summed(*sums, at, rows // 2)
            inverse = lax.rsqrt(jnp.mean(middle * middle, axis=1, keepdims=True) + epsilon)
            mid_ref[here, :] = middle
            inv_ref[here, :] = inverse
            n2_ref[here, :] = reorder_lanes(middle * inverse, held).astype(bf16)

    return small_call(
        kernel,
        "finish_middle",
        [tokens, *pieces],
        [
            jax.ShapeDtypeStruct((rows, width), f32),
            jax.ShapeDtypeStruct((rows, 1), f32),
            jax.ShapeDtypeStruct((rows, width), bf16),
        ],
    )


def finish_norm_back(grad, normed_from, inverse, pieces, natural, last):
    rows, width = grad.shape

    def kernel(g_ref, x_ref, inv_ref, *refs):
        sums, outs = refs[:5], refs[5:]
        for at in range(0, rows, ROWS):
            here = slice(at, at + ROWS)
            scaled = reorder_lanes(summed(*sums, at, rows // 2), natural)
            inverse = inv_ref[here, :]
            normed = x_ref[here, :].astype(f32) * inverse
            mean = jnp.mean(scaled * normed, axis=1, keepdims=True)
            total = g_ref[here, :].astype(f32) + inverse * (scaled - normed * mean)
            outs[0][here, :] = total
            if not last:
                outs[1][here, :] = total.astype(bf16)

    shapes = [jax.ShapeDtypeStruct((rows, width), f32)]
    if not last:
        shapes.append(jax.ShapeDtypeStruct((rows, width), bf16))
    return small_call(
        kernel, "finish_norm_back", [grad, normed_from, inverse, *pieces], shapes
    )


def interleaved(i):
    return slice(2 * i * LANES, (2 * i + 1) * LANES), slice((2 * i + 1) * LANES, (2 * i + 2) * LANES)


def activate_kernel(n_ref, w_ref, m_ref, slope_ref):
    both = nn(n_ref[...], w_ref[...])
    for i in range(m_ref.shape[1] // LANES):
        gate_at, up_at = interleaved(i)
        gate, up = both[:, gate_at], both[:, up_at]
        sigmoid = jax.nn.sigmoid(gate)
        silu = gate * sigmoid
        m_ref[:, i * LANES : (i + 1) * LANES] = (silu * up).astype(bf16)
        slope_ref[:, gate_at] = (up * (sigmoid + silu * (1.0 - sigmoid))).astype(bf16)
        slope_ref[:, up_at] = silu.astype(bf16)


def activate(n2, gate_up, tile=256):
    total, width = n2.shape
    ff = gate_up.shape[1] // 2
    return pl.pallas_call(
        activate_kernel,
        grid=(pl.cdiv(ff, tile),),
        in_specs=[
            pl.BlockSpec((total, width), lambda j: (0, 0)),
            pl.BlockSpec((width, 2 * tile), lambda j: (0, j)),
        ],
        out_specs=[
            pl.BlockSpec((total, tile), lambda j: (0, j)),
            pl.BlockSpec((total, 2 * tile), lambda j: (0, j)),
        ],
        out_shape=[
            jax.ShapeDtypeStruct((total, ff), bf16),
            jax.ShapeDtypeStruct((total, 2 * ff), bf16),
        ],
        compiler_params=pltpu.CompilerParams(vmem_limit_bytes=48 << 20),
        cost_estimate=pl.CostEstimate(
            flops=4 * total * width * ff,
            bytes_accessed=2 * (total * width + 2 * width * ff + 3 * total * ff),
            transcendentals=total * ff,
        ),
        name="activate",
    )(n2, gate_up)


def activate_back_kernel(g_ref, down_ref, slope_ref, d_ref):
    dm = nt(g_ref[...], down_ref[...])
    for i in range(dm.shape[1] // LANES):
        part = dm[:, i * LANES : (i + 1) * LANES]
        for at in interleaved(i):
            d_ref[:, at] = (part * slope_ref[:, at].astype(f32)).astype(bf16)


def activate_back(g, down, slopes, tile=256):
    total, width = g.shape
    ff = down.shape[0]
    return pl.pallas_call(
        activate_back_kernel,
        grid=(pl.cdiv(ff, tile),),
        in_specs=[
            pl.BlockSpec((total, width), lambda j: (0, 0)),
            pl.BlockSpec((tile, width), lambda j: (j, 0)),
            pl.BlockSpec((total, 2 * tile), lambda j: (0, j)),
        ],
        out_specs=pl.BlockSpec((total, 2 * tile), lambda j: (0, j)),
        out_shape=jax.ShapeDtypeStruct((total, 2 * ff), bf16),
        compiler_params=pltpu.CompilerParams(vmem_limit_bytes=48 << 20),
        cost_estimate=pl.CostEstimate(
            flops=2 * total * width * ff,
            bytes_accessed=2 * (total * width + width * ff + 4 * total * ff),
            transcendentals=0,
        ),
        name="activate_back",
    )(g, down, slopes)


def split_gate_up(w_gate, w_up, gain):
    own, total = w_gate.shape
    ff = total // TP

    def kernel(gate_ref, up_ref, gain_ref, out_ref):
        for g in range(TP):
            for j in range(ff // LANES):
                here = slice(g * ff + j * LANES, g * ff + (j + 1) * LANES)
                for ref, at in zip((gate_ref, up_ref), interleaved(j)):
                    out_ref[g, :, at] = (ref[:, here].astype(f32) * gain_ref[...]).astype(bf16)

    return small_call(
        kernel,
        "split_gate_up",
        [w_gate, w_up, gain],
        [jax.ShapeDtypeStruct((TP, own, 2 * ff), bf16)],
    )[0]


def merge_gate_up(raw, w_gate, w_up, gain):
    own, total = w_gate.shape
    ff = total // TP

    def kernel(in_ref, gate_ref, up_ref, gain_ref, dgate_ref, dup_ref, dgain_ref):
        dgain = jnp.zeros((own, LANES), f32)
        for g in range(TP):
            for j in range(ff // LANES):
                here = slice(g * ff + j * LANES, g * ff + (j + 1) * LANES)
                for ref, out_ref, at in zip(
                    (gate_ref, up_ref), (dgate_ref, dup_ref), interleaved(j)
                ):
                    part = in_ref[g, :, at].astype(f32)
                    dgain += part * ref[:, here].astype(f32)
                    out_ref[:, here] = part * gain_ref[...]
        dgain_ref[...] = jnp.sum(dgain, axis=1, keepdims=True)

    return small_call(
        kernel,
        "merge_gate_up",
        [raw, w_gate, w_up, gain],
        [
            jax.ShapeDtypeStruct((own, total), f32),
            jax.ShapeDtypeStruct((own, total), f32),
            jax.ShapeDtypeStruct((own, 1), f32),
        ],
    )


def make_body(reps, ctxs):
    pair = [(0, 1), (1, 0)]

    def swap(v, k):
        if k == 0:
            return v
        if k == 1:
            return lax.ppermute(v, "tx", pair)
        if k == 2:
            return lax.ppermute(v, "ty", pair)
        return lax.ppermute(v, ("ty", "tx"), [(i, i ^ 3) for i in range(TP)])

    def swap_ctx(v, j):
        return lax.ppermute(v, "ctx", [(i, i ^ j) for i in range(ctxs)]) if j else v

    def halves(v):
        half = v.shape[0] // 2
        return v[:half], v[half:]

    def joined(a, b):
        return jnp.concatenate([p for k in range(TP) for p in (a[k], b[k])], axis=0)

    def gather(v):
        a, b = halves(v)
        ax, by = swap(a, 1), swap(b, 2)
        ay, bx = swap(a, 2), swap(b, 1)
        return joined((a, ax, ay, swap(ax, 2)), (b, bx, by, swap(by, 1)))

    def scatter_far(part):
        a, b = halves(part.astype(bf16))
        return swap(a, 2), swap(b, 1)

    def scatter_near(part_x, part_y, far):
        a1, b1 = halves(part_x)
        a2, b2 = halves(part_y)
        a1 = (a1.astype(f32) + far[0].astype(f32)).astype(bf16)
        b2 = (b2.astype(f32) + far[1].astype(f32)).astype(bf16)
        return [swap(a2.astype(bf16), 2), swap(a1, 1), swap(b1.astype(bf16), 1), swap(b2, 2)]

    def scatter_sum(parts):
        a2, a1, b1, b2 = scatter_near(parts[1], parts[2], scatter_far(parts[3]))
        come = [a2.astype(f32) + a1.astype(f32), b1.astype(f32) + b2.astype(f32)]
        return parts[0].astype(f32) + jnp.concatenate(come, axis=0)

    def exchange(blocks, t):
        out = jnp.zeros_like(blocks)
        for k in range(TP):
            mine = lax.dynamic_index_in_dim(blocks, t ^ k, 0, keepdims=True)
            out = lax.dynamic_update_slice_in_dim(out, swap(mine, k), t ^ k, 0)
        return out

    def spread(blocks, t):
        return exchange(blocks, t).reshape(-1, blocks.shape[2])

    def collect(summed, t):
        return exchange(summed.reshape(TP, -1, summed.shape[1]), t)

    def whole(v):
        return lax.all_gather(v, ("rep", "ctx"), axis=0, tiled=True)

    def over_reps(left, right):
        if reps != 2:
            part = tn(left, right).astype(bf16)
            return lax.psum_scatter(part, "rep", scatter_dimension=0, tiled=True)
        r = lax.axis_index("rep")
        half = left.shape[1] // 2
        other = lax.dynamic_slice_in_dim(left, (1 - r) * half, half, 1)
        sent = lax.ppermute(tn(other, right).astype(bf16), "rep", pair)
        mine = lax.dynamic_slice_in_dim(left, r * half, half, 1)
        return (tn(mine, right) + sent.astype(f32)).astype(bf16)

    def owned(part):
        return lax.psum_scatter(part, "ctx", scatter_dimension=0, tiled=True)

    def body(
        tokens,
        span_order,
        norm_attn,
        w_query,
        w_key,
        w_value,
        w_out,
        norm_mlp,
        w_gate,
        w_up,
        w_down,
        out_grad,
    ):
        count, width = tokens.shape
        own = w_query.shape[0]
        held, natural = block_orders(width, reps * ctxs)
        span = count * ctxs // span_order.shape[1]
        q_cols, kv_cols = GROUP * HD, HD
        t = 2 * lax.axis_index("ty") + lax.axis_index("tx")
        c = lax.axis_index("ctx")

        def part_of(v, k):
            return v[k * count : (k + 1) * count]

        orders = [swap(span_order, k)[0] for k in range(TP)]
        offsets = jnp.arange(span, dtype=jnp.int32)
        per = count // span

        def block_positions(order, member):
            picked = lax.dynamic_slice_in_dim(order, member * per, per)
            return (picked[:, None] * span + offsets[None, :]).reshape(-1)

        query_positions = [block_positions(order, c) for order in orders]
        key_positions = [
            jnp.concatenate([block_positions(order, c ^ j) for j in range(ctxs)])
            for order in orders
        ]
        half_dim = HD // 2
        frequency = jnp.power(rope_base, -jnp.arange(half_dim, dtype=f32) / half_dim)
        angles = frequency[:, None] * jnp.concatenate(query_positions).astype(f32)[None, :]
        cosine, sine = jnp.cos(angles), jnp.sin(angles)

        gain_attn = norm_attn.astype(f32)[:, None]
        gain_mlp = norm_mlp.astype(f32)[:, None]

        def by_group(w):
            w = (w.astype(f32) * gain_attn).astype(bf16)
            return w.reshape(own, TP, -1).transpose(1, 0, 2)

        out = whole(w_out)
        blocks = jnp.concatenate([by_group(w) for w in (w_query, w_key, w_value)], axis=2)
        a, b = halves(hold_tokens(tokens, held))
        qkv_mine, ax, by = phase(spread(blocks, t), swap(a, 1), swap(b, 2))
        qkv = whole(qkv_mine)
        gate_up_blocks = split_gate_up(after(w_gate, qkv_mine), w_up, gain_mlp)
        ay, bx, axy, bxy, gate_up_blocks = phase(
            swap(a, 2), swap(b, 1), swap(ax, 2), swap(by, 1), gate_up_blocks
        )
        x_all = joined((a, ax, ay, axy), (b, bx, by, bxy))
        gate_up_mine = spread(gate_up_blocks, t)
        gate_up = whole(gate_up_mine)
        down = whole(after(w_down, gate_up_mine))

        qt, kv, inverse_all = project(x_all, qkv, cosine, sine, count)
        kv = kv.reshape(TP, count, 2 * kv_cols)
        kv, g_all = phase(
            jnp.stack([swap_ctx(kv, j) for j in range(ctxs)], axis=1),
            gather(after(out_grad, kv)),
        )
        kv_seq = kv.reshape(TP, ctxs * count, 2 * kv_cols)
        mixed, logsum, parts = [None] * TP, [None] * TP, [None] * TP

        def attend_to(k, queries):
            mixed[k], logsum[k], parts[k] = attend(
                query_positions[k][None, :],
                key_positions[k][:, None],
                queries,
                kv_seq[k],
                out,
                bf16 if k else f32,
            )

        attend_to(3, qt[3])
        far = scatter_far(parts[3])
        qt = after(qt, parts[3])
        attend_to(2, qt[2])
        attend_to(1, qt[1])
        far, parts[1], parts[2], qt = phase(far, parts[1], parts[2], qt)
        near = scatter_near(parts[1], parts[2], far)
        attend_to(0, qt[0])
        middle, inverse_mid, n2 = finish_middle(tokens, [parts[0], *near], held)
        n2_all = gather(n2)

        act, slopes = activate(n2_all, gate_up)
        part_down = over_reps(act, g_all)
        slopes, part_down = phase(slopes, part_down)
        sum_down = owned(part_down)
        grad_act = activate_back(g_all, down, slopes)
        back_far = nt(part_of(grad_act, 3), gate_up)
        far = scatter_far(back_far)
        back_near = nt(after(grad_act, back_far)[: 3 * count], gate_up)
        far, back_near = phase(far, back_near)
        near = scatter_near(part_of(back_near, 1), part_of(back_near, 2), far)
        part_gate_up = over_reps(n2_all, after(grad_act, back_near))
        near, part_gate_up = phase(near, part_gate_up)
        sum_gate_up = owned(part_gate_up)
        grad_middle, db = finish_norm_back(
            out_grad, middle, inverse_mid, [part_of(back_near, 0), *near], natural, False
        )

        dq, dqs, dkv = [None] * TP, [None] * TP, [None] * TP

        def attend_back_to(k, grads):
            dq[k], dqs[k], dkv[k] = attend_back(
                query_positions[k][None, :],
                key_positions[k][:, None],
                qt[k],
                kv_seq[k],
                out,
                mixed[k],
                logsum[k],
                grads,
                part_of(inverse_all, k),
                cosine[:, k * count : (k + 1) * count],
                sine[:, k * count : (k + 1) * count],
            )

        a, b = halves(db)
        ax, by = swap(a, 1), swap(b, 2)
        attend_back_to(0, db)
        a, b, ax, by, dq[0] = phase(a, b, ax, by, dq[0])
        ay, bx = swap(a, 2), swap(b, 1)
        forward = nn(after(act, ax), down)
        ay, bx, forward = phase(ay, bx, forward)
        axy, bxy = swap(ax, 2), swap(by, 1)
        attend_back_to(1, jnp.concatenate([ax, bx], axis=0))
        attend_back_to(2, jnp.concatenate([ay, by], axis=0))
        axy, bxy, dq[1], dq[2] = phase(axy, bxy, dq[1], dq[2])
        attend_back_to(3, jnp.concatenate([axy, bxy], axis=0))
        db_all = joined((a, ax, ay, axy), (b, bx, by, bxy))
        layer_out = (
            middle + scatter_sum([part_of(after(forward, axy), k) for k in range(TP)])
        ).astype(bf16)
        dkv = jnp.stack(dkv).reshape(TP, ctxs, count, 2 * kv_cols)
        local = dkv[:, 0]
        for j in range(1, ctxs):
            local = local + swap_ctx(dkv[:, j].astype(bf16), j).astype(f32)
        part_out = over_reps(jnp.concatenate(mixed, axis=1).T, db_all)
        local, part_out = phase(local, part_out)
        sum_out = owned(part_out)
        local = local.reshape(TP * count, 2 * kv_cols)
        first, second = local[:, :half_dim], local[:, half_dim:kv_cols]
        dkv = jnp.concatenate(
            [
                first * cosine.T + second * sine.T,
                second * cosine.T - first * sine.T,
                local[:, kv_cols:],
            ],
            axis=1,
        )
        grad_proj = jnp.concatenate([jnp.concatenate(dq, axis=0), dkv.astype(bf16)], axis=1)
        scaled_proj = jnp.concatenate(
            [jnp.concatenate(dqs, axis=0), (dkv * inverse_all).astype(bf16)], axis=1
        )
        back_far = nt(part_of(grad_proj, 3), qkv)
        far = scatter_far(back_far)
        back_near = nt(after(grad_proj, back_far)[: 3 * count], qkv)
        far, back_near = phase(far, back_near)
        near = scatter_near(part_of(back_near, 1), part_of(back_near, 2), far)
        part_qkv = over_reps(x_all, after(scaled_proj, back_near))
        near, part_qkv = phase(near, part_qkv)
        sum_qkv = owned(part_qkv)
        (input_grad,) = finish_norm_back(
            grad_middle,
            tokens,
            part_of(inverse_all, 0),
            [part_of(back_near, 0), *near],
            natural,
            True,
        )

        sum_gate_up = collect(after(sum_gate_up, input_grad), t)
        grad_gate, grad_up, grad_norm_mlp = merge_gate_up(sum_gate_up, w_gate, w_up, gain_mlp)
        sum_down, sum_out, sum_qkv = after((sum_down, sum_out, sum_qkv), grad_norm_mlp)
        sum_qkv = collect(sum_qkv, t)

        def rows_of(v):
            return v.transpose(1, 0, 2).reshape(own, -1).astype(f32)

        raw_query = rows_of(sum_qkv[..., :q_cols])
        raw_key = rows_of(sum_qkv[..., q_cols : q_cols + kv_cols])
        raw_value = rows_of(sum_qkv[..., q_cols + kv_cols :])
        grad_norm_attn = (
            jnp.sum(raw_query * w_query.astype(f32), axis=1)
            + jnp.sum(raw_key * w_key.astype(f32), axis=1)
            + jnp.sum(raw_value * w_value.astype(f32), axis=1)
        )
        return (
            layer_out,
            input_grad,
            grad_norm_attn,
            raw_query * gain_attn,
            raw_key * gain_attn,
            raw_value * gain_attn,
            sum_out.astype(f32),
            grad_norm_mlp[:, 0],
            grad_gate,
            grad_up,
            sum_down.astype(f32),
        )

    return body


def solution(mesh):
    sequences, ctxs = mesh.shape["dp"], mesh.shape["ctx"]
    reps = sequences // TP
    names = ("ty", "tx", "rep", "ctx")
    grid = Mesh(mesh.devices.reshape(2, 2, reps, ctxs), names)
    matrix, vector = P(names, None), P(names)
    order = P(("ty", "tx", "rep"), None)
    weights = [vector, matrix, matrix, matrix, matrix, vector, matrix, matrix, matrix]
    return jax.shard_map(
        make_body(reps, ctxs),
        mesh=grid,
        in_specs=(matrix, order, *weights, matrix),
        out_specs=(matrix, matrix, *weights),
        check_vma=False,
    )
```

```python
import jax
import jax.numpy as jnp
from jax import lax
from jax.experimental import pallas as pl
from jax.experimental.pallas import tpu as pltpu
from jax.sharding import Mesh, PartitionSpec as P

H = 32
KV = 4
HD = 64
TP = 4
GROUP = H // KV
LANES = 128
ROWS = 64
ROOM = 60 << 20
ATTEND_ROOM = 60 << 20
DOWN_STEPS = 2

epsilon = 1e-05
rope_base = 10000.0
masked_score = -1e30
bf16 = jnp.bfloat16
f32 = jnp.float32


def after(value, *others):
    return lax.optimization_barrier((value,) + others)[0]


def phase(*values):
    return lax.optimization_barrier(values)


def nn(left, right):
    return lax.dot_general(left, right, (((1,), (0,)), ((), ())), preferred_element_type=f32)


def nt(left, right):
    return lax.dot_general(left, right, (((1,), (1,)), ((), ())), preferred_element_type=f32)


def tn(left, right):
    return lax.dot_general(left, right, (((0,), (0,)), ((), ())), preferred_element_type=f32)


def like(shape, kind):
    return jax.ShapeDtypeStruct(shape, kind)


def size_of(values):
    return sum(v.size * v.dtype.itemsize for v in values)


def small_call(
    kernel, name, inputs, outputs, flops=0, scratch=(), scalars=0, transcendentals=0, room=ROOM
):
    specs, arrays = [pl.BlockSpec(memory_space=pltpu.SMEM)] * scalars, list(inputs[:scalars])
    for v in inputs[scalars:]:
        if isinstance(v, tuple):
            specs.append(row_block(*v))
            arrays.append(v[0])
        else:
            specs.append(whole_block(v.shape))
            arrays.append(v)
    size = size_of((*arrays, *outputs))
    return pl.pallas_call(
        kernel,
        grid=(1,),
        in_specs=specs,
        out_specs=[whole_block(v.shape) for v in outputs],
        out_shape=outputs,
        scratch_shapes=list(scratch),
        compiler_params=pltpu.CompilerParams(vmem_limit_bytes=room),
        cost_estimate=pl.CostEstimate(
            flops=max(flops, size), bytes_accessed=size, transcendentals=transcendentals
        ),
        name=name,
    )(*arrays)


def row_block(array, index):
    shape = array.shape[1:]
    return pl.BlockSpec((None,) + shape, lambda i: (index,) + (0,) * len(shape))


def whole_block(shape):
    return pl.BlockSpec(shape, lambda i: (0,) * len(shape))


def turn(vectors, cosine, sine):
    half = HD // 2
    out = []
    for at in range(0, vectors.shape[0], HD):
        first, second = vectors[at : at + half], vectors[at + half : at + HD]
        out += [first * cosine - second * sine, second * cosine + first * sine]
    return jnp.concatenate(out, axis=0)


def project(pieces, w, cosine, sine):
    half, width = pieces[0].shape
    rows, n, q = 2 * half, w.shape[1], GROUP * HD

    def kernel(*refs):
        x_refs, (w_ref, cos_ref, sin_ref, kv_ref), outs = refs[:8], refs[8:12], refs[12:]
        for k in range(TP):
            xb = jnp.concatenate([x_refs[2 * k][...], x_refs[2 * k + 1][...]], axis=0)
            x = xb.astype(f32)
            inverse = lax.rsqrt(jnp.mean(x * x, axis=1, keepdims=True) + epsilon)
            outs[TP + k][...] = inverse
            flat = (nn(xb, w_ref[...]) * inverse).T
            cosine, sine = cos_ref[k], sin_ref[k]
            outs[k][...] = (turn(flat[:q], cosine, sine) * HD**-0.5).astype(bf16)
            kv = jnp.concatenate([turn(flat[q : q + HD], cosine, sine), flat[q + HD :]], axis=0)
            kv_ref[k] = kv.T.astype(bf16)

    kv, *outs = small_call(
        kernel,
        "project",
        [*pieces, w, cosine, sine],
        [like((TP, rows, 2 * HD), bf16)]
        + [like((q, rows), bf16)] * TP
        + [like((rows, 1), f32)] * TP,
        flops=2 * TP * rows * width * n,
    )
    return outs[:TP], kv, outs[TP:]


def set_bias(order_ref, k, bias_ref):
    keys, rows = bias_ref.shape
    span = keys // order_ref.shape[1]
    lane = lax.broadcasted_iota(jnp.int32, (span, rows), 1)
    query = jnp.where(lane < span, order_ref[k, 0], order_ref[k, 1] - 1) * span + lane
    row = lax.broadcasted_iota(jnp.int32, (span, rows), 0)
    for b in range(keys // span):
        key = order_ref[k, b] * span + row
        bias_ref[b * span : (b + 1) * span, :] = jnp.where(query >= key, 0.0, masked_score)


def attend(members, orders, queries, kv_pieces, wo, kind):
    n, rows = queries[0].shape
    holders, width = len(kv_pieces), wo.shape[1]
    keys, count = holders * rows, len(members)

    def kernel(order_ref, wo_ref, *refs):
        for i, k in enumerate(members):
            qt_ref, *kv_refs = refs[i * (1 + holders) : (i + 1) * (1 + holders)]
            outs = refs[count * (1 + holders) :]
            ot_ref, lse_ref, part_ref = outs[3 * i : 3 * i + 3]
            bias_ref = outs[-1]
            set_bias(order_ref, k, bias_ref)
            kv = jnp.concatenate([ref[...] for ref in kv_refs], axis=0)
            vt = kv.astype(f32).T[HD:].astype(bf16)
            zero = jnp.zeros((HD, rows), bf16)
            for h in range(GROUP):
                at = slice(h * HD, (h + 1) * HD)
                scores = nn(kv, jnp.concatenate([qt_ref[at, :], zero], axis=0)) + bias_ref[...]
                top = jnp.max(scores, axis=0, keepdims=True)
                exponent = jnp.exp(scores - top)
                total = jnp.sum(exponent, axis=0, keepdims=True)
                ot_ref[at, :] = (nn(vt, exponent.astype(bf16)) / total).astype(bf16)
                lse_ref[h : h + 1, :] = top + jnp.log(total)
            part_ref[...] = tn(ot_ref[...], wo_ref[...]).astype(part_ref.dtype)

    inputs, outputs = [orders, wo], []
    for i, k in enumerate(members):
        inputs += [queries[i], *[(piece, k) for piece in kv_pieces]]
        outputs += [like((n, rows), bf16), like((GROUP, rows), f32), like((rows, width), kind)]
    results = small_call(
        kernel,
        "attend",
        inputs,
        outputs,
        flops=2 * rows * n * (keys * 2 * 4 + width) * count,
        scratch=[pltpu.VMEM((keys, rows), f32)],
        scalars=1,
        transcendentals=GROUP * rows * keys * count,
        room=ATTEND_ROOM,
    )
    return [results[3 * i : 3 * i + 3] for i in range(count)]


def attend_back(members, orders, wo, kv_pieces, details):
    n, rows = details[0][0].shape
    holders, width = len(kv_pieces), wo.shape[1]
    keys, half, count = holders * rows, rows // 2, len(members)
    step = 8 + holders

    def kernel(order_ref, wo_ref, *refs):
        outs, (bias_ref, dat_ref, dqt_ref, dkv_ref) = refs[count * step : -4], refs[-4:]
        for i, k in enumerate(members):
            own = refs[i * step : (i + 1) * step]
            kv_refs, (qt_ref, ot_ref, lse_ref, a_ref, b_ref) = own[:holders], own[holders:-3]
            inv_ref, cos_ref, sin_ref = own[-3:]
            dq_ref, dqs_ref, own_ref, far_ref = outs[4 * i : 4 * i + 4]
            set_bias(order_ref, k, bias_ref)
            kv = jnp.concatenate([ref[...] for ref in kv_refs], axis=0)
            kt = kv.astype(f32).T[:HD].astype(bf16)
            zero = jnp.zeros((HD, rows), bf16)
            dat_ref[:, :half] = nt(wo_ref[...], a_ref[...]).astype(bf16)
            dat_ref[:, half:] = nt(wo_ref[...], b_ref[...]).astype(bf16)
            for h in range(GROUP):
                at = slice(h * HD, (h + 1) * HD)
                q_low = jnp.concatenate([qt_ref[at, :], zero], axis=0)
                da_high = jnp.concatenate([zero, dat_ref[at, :]], axis=0)
                weights = jnp.exp(nn(kv, q_low) + bias_ref[...] - lse_ref[h : h + 1, :])
                delta = jnp.sum(
                    dat_ref[at, :].astype(f32) * ot_ref[at, :].astype(f32), axis=0, keepdims=True
                )
                ds = (weights * (nn(kv, da_high) - delta)).astype(bf16)
                dkv = nt(ds, q_low) + nt(weights.astype(bf16), da_high)
                if h == 0:
                    dkv_ref[...] = dkv
                else:
                    dkv_ref[...] += dkv
                dqt_ref[at, :] = nn(kt, ds)
            dq = (turn(dqt_ref[...], cos_ref[...], -sin_ref[...]) * HD**-0.5).T
            dq_ref[...] = dq.astype(bf16)
            dqs_ref[...] = (dq * inv_ref[...]).astype(bf16)
            own_ref[...] = dkv_ref[:rows, :]
            far_ref[...] = dkv_ref[rows:, :].astype(bf16)

    inputs, outputs = [orders, wo], []
    for k, detail in zip(members, details):
        inputs += [*[(piece, k) for piece in kv_pieces], *detail]
        outputs += [
            like((rows, n), bf16),
            like((rows, n), bf16),
            like((rows, 2 * HD), f32),
            like((keys - rows, 2 * HD), bf16),
        ]
    results = small_call(
        kernel,
        "attend_back",
        inputs,
        outputs,
        flops=2 * rows * n * (keys * 5 * 4 + width) * count,
        scratch=[
            pltpu.VMEM((keys, rows), f32),
            pltpu.VMEM((n, rows), bf16),
            pltpu.VMEM((n, rows), f32),
            pltpu.VMEM((keys, 2 * HD), f32),
        ],
        scalars=1,
        transcendentals=GROUP * rows * keys * count,
        room=ATTEND_ROOM,
    )
    return [results[4 * i : 4 * i + 4] for i in range(count)]


def out_gradient(mixed, grads):
    n, rows = mixed[0].shape
    width = grads[0].shape[1]

    def kernel(*refs):
        total = 0.0
        for k in range(TP):
            db = jnp.concatenate([refs[TP + 2 * k][...], refs[TP + 2 * k + 1][...]], axis=0)
            total = total + nn(refs[k][...], db)
        refs[-1][...] = total.astype(bf16)

    return small_call(
        kernel,
        "out_gradient",
        [*mixed, *grads],
        [like((n, width), bf16)],
        flops=2 * TP * rows * n * width,
    )[0]


def finish_keys(own, near, last, dq, dqs, inverse, cosine, sine):
    rows, n = dq[0].shape

    def kernel(*refs):
        own_refs, refs = refs[:TP], refs[TP:]
        near_refs, refs = refs[: len(near)], refs[len(near) :]
        last_refs, refs = refs[: len(last)], refs[len(last) :]
        dq_refs, dqs_refs, refs = refs[:TP], refs[TP : 2 * TP], refs[2 * TP :]
        inv_refs, (cos_ref, sin_ref, plain_ref, scaled_ref) = refs[:TP], refs[TP:]
        for k in range(TP):
            total = own_refs[k][...]
            for ref in near_refs if k < TP - 1 else last_refs:
                total = total + ref[k % (TP - 1)].astype(f32)
            total = total.T
            keys = turn(total[:HD], cos_ref[k], -sin_ref[k])
            total = jnp.concatenate([keys, total[HD:]], axis=0).T
            at = slice(k * rows, (k + 1) * rows)
            plain_ref[at, :n] = dq_refs[k][...]
            plain_ref[at, n:] = total.astype(bf16)
            scaled_ref[at, :n] = dqs_refs[k][...]
            scaled_ref[at, n:] = (total * inv_refs[k][...]).astype(bf16)

    shape = like((TP * rows, n + 2 * HD), bf16)
    return small_call(
        kernel,
        "finish_keys",
        [*own, *near, *last, *dq, *dqs, *inverse, cosine, sine],
        [shape, shape],
    )


def join_rows(pieces):
    rows, width = pieces[0].shape

    def kernel(*refs):
        for i, ref in enumerate(refs[:-1]):
            refs[-1][i * rows : (i + 1) * rows, :] = ref[...]

    return small_call(
        kernel, "join_rows", pieces, [like((len(pieces) * rows, width), pieces[0].dtype)]
    )[0]


def reorder_lanes(v, ordered):
    order, size = ordered
    return jnp.concatenate([v[:, i * size : (i + 1) * size] for i in order], axis=1)


def block_orders(width, holders):
    held = [m * holders + h for h in range(holders) for m in range(TP)]
    natural = [held.index(i) for i in range(len(held))]
    size = width // len(held)
    return (held, size), (natural, size)


def hold_tokens(tokens, held):
    half = tokens.shape[0] // 2

    def kernel(x_ref, a_ref, b_ref):
        a_ref[...] = reorder_lanes(x_ref[:half, :].astype(f32), held).astype(bf16)
        b_ref[...] = reorder_lanes(x_ref[half:, :].astype(f32), held).astype(bf16)

    shape = like((half, tokens.shape[1]), bf16)
    return small_call(kernel, "hold_tokens", [tokens], [shape, shape])


def summed(refs, at, half):
    own_ref, a2_ref, a1_ref, b1_ref, b2_ref = refs
    first, second = (a2_ref, a1_ref) if at < half else (b1_ref, b2_ref)
    come = slice(at % half, at % half + ROWS)
    total = own_ref[at : at + ROWS, :].astype(f32)
    return total + first[come, :].astype(f32) + second[come, :].astype(f32)


def finish_middle(tokens, pieces, held):
    rows, width = tokens.shape
    half = rows // 2

    def kernel(x_ref, *refs):
        sums, (mid_ref, inv_ref, a_ref, b_ref) = refs[:5], refs[5:]
        for at in range(0, rows, ROWS):
            here = slice(at, at + ROWS)
            middle = x_ref[here, :].astype(f32) + summed(sums, at, half)
            inverse = lax.rsqrt(jnp.mean(middle * middle, axis=1, keepdims=True) + epsilon)
            mid_ref[here, :] = middle
            inv_ref[here, :] = inverse
            out = a_ref if at < half else b_ref
            come = slice(at % half, at % half + ROWS)
            out[come, :] = reorder_lanes(middle * inverse, held).astype(bf16)

    return small_call(
        kernel,
        "finish_middle",
        [tokens, *pieces],
        [
            like((rows, width), f32),
            like((rows, 1), f32),
            like((half, width), bf16),
            like((half, width), bf16),
        ],
    )


def finish_norm_back(grad, normed_from, inverse, pieces, natural, last):
    rows, width = grad.shape
    half = rows // 2

    def kernel(g_ref, x_ref, inv_ref, *refs):
        sums, outs = refs[:5], refs[5:]
        for at in range(0, rows, ROWS):
            here = slice(at, at + ROWS)
            scaled = reorder_lanes(summed(sums, at, half), natural)
            inverse = inv_ref[here, :]
            normed = x_ref[here, :].astype(f32) * inverse
            mean = jnp.mean(scaled * normed, axis=1, keepdims=True)
            total = g_ref[here, :].astype(f32) + inverse * (scaled - normed * mean)
            outs[0][here, :] = total
            if not last:
                out = outs[1] if at < half else outs[2]
                out[at % half : at % half + ROWS, :] = total.astype(bf16)

    shapes = [like((rows, width), f32)]
    if not last:
        shapes += [like((half, width), bf16)] * 2
    return small_call(
        kernel, "finish_norm_back", [grad, normed_from, inverse, *pieces], shapes
    )


def finish_layer(middle, pieces):
    rows, width = middle.shape

    def kernel(mid_ref, *refs):
        for at in range(0, rows, ROWS):
            here = slice(at, at + ROWS)
            total = mid_ref[here, :] + summed(refs[:5], at, rows // 2)
            refs[5][here, :] = total.astype(bf16)

    return small_call(
        kernel, "finish_layer", [middle, *pieces], [like((rows, width), bf16)]
    )[0]


def interleaved(i):
    return slice(2 * i * LANES, (2 * i + 1) * LANES), slice((2 * i + 1) * LANES, (2 * i + 2) * LANES)


def activate(pieces, gate_up, tile=256):
    half, width = pieces[0].shape
    total, ff = half * len(pieces), gate_up.shape[1] // 2

    def kernel(*refs):
        n_refs, (w_ref, m_ref, slope_ref, n2_ref) = refs[: len(pieces)], refs[len(pieces) :]

        @pl.when(pl.program_id(0) == 0)
        def _():
            for i, ref in enumerate(n_refs):
                n2_ref[i * half : (i + 1) * half, :] = ref[...]

        both = nn(n2_ref[...], w_ref[...])
        for i in range(tile // LANES):
            gate_at, up_at = interleaved(i)
            gate, up = both[:, gate_at], both[:, up_at]
            sigmoid = jax.nn.sigmoid(gate)
            silu = gate * sigmoid
            m_ref[:, i * LANES : (i + 1) * LANES] = (silu * up).astype(bf16)
            slope_ref[:, gate_at] = (up * (sigmoid + silu * (1.0 - sigmoid))).astype(bf16)
            slope_ref[:, up_at] = silu.astype(bf16)

    return pl.pallas_call(
        kernel,
        grid=(pl.cdiv(ff, tile),),
        in_specs=[whole_block(v.shape) for v in pieces]
        + [pl.BlockSpec((width, 2 * tile), lambda j: (0, j))],
        out_specs=[
            pl.BlockSpec((total, tile), lambda j: (0, j)),
            pl.BlockSpec((total, 2 * tile), lambda j: (0, j)),
        ],
        out_shape=[like((total, ff), bf16), like((total, 2 * ff), bf16)],
        scratch_shapes=[pltpu.VMEM((total, width), bf16)],
        compiler_params=pltpu.CompilerParams(vmem_limit_bytes=ROOM),
        cost_estimate=pl.CostEstimate(
            flops=4 * total * width * ff,
            bytes_accessed=2 * (total * width + 2 * width * ff + 3 * total * ff),
            transcendentals=total * ff,
        ),
        name="activate",
    )(*pieces, gate_up)


def activate_back(g, down, slopes, tile=256):
    total, width = g.shape
    ff = down.shape[0]

    def kernel(g_ref, down_ref, slope_ref, d_ref):
        dm = nt(g_ref[...], down_ref[...])
        for i in range(tile // LANES):
            part = dm[:, i * LANES : (i + 1) * LANES]
            for at in interleaved(i):
                d_ref[:, at] = (part * slope_ref[:, at].astype(f32)).astype(bf16)

    return pl.pallas_call(
        kernel,
        grid=(pl.cdiv(ff, tile),),
        in_specs=[
            pl.BlockSpec((total, width), lambda j: (0, 0)),
            pl.BlockSpec((tile, width), lambda j: (j, 0)),
            pl.BlockSpec((total, 2 * tile), lambda j: (0, j)),
        ],
        out_specs=pl.BlockSpec((total, 2 * tile), lambda j: (0, j)),
        out_shape=like((total, 2 * ff), bf16),
        compiler_params=pltpu.CompilerParams(vmem_limit_bytes=ROOM),
        cost_estimate=pl.CostEstimate(
            flops=2 * total * width * ff,
            bytes_accessed=2 * (total * width + width * ff + 4 * total * ff),
            transcendentals=0,
        ),
        name="activate_back",
    )(g, down, slopes)


def weight_grad(left, right, index, come=None):
    total, width = left.shape
    n = right.shape[1]
    rows, columns = width // 4, n // 2 if n % (2 * LANES) == 0 else n

    def kernel(index_ref, left_ref, right_ref, *refs):
        part = tn(left_ref[...], right_ref[...])
        if come is not None:
            part = part + refs[0][...].astype(f32)
        refs[-1][...] = part.astype(bf16)

    out = pl.BlockSpec((rows, columns), lambda i, j, index: (i, j))
    more = [] if come is None else [come]
    return pl.pallas_call(
        kernel,
        grid_spec=pltpu.PrefetchScalarGridSpec(
            num_scalar_prefetch=1,
            grid=(2, n // columns),
            in_specs=[
                pl.BlockSpec((total, rows), lambda i, j, index: (0, 2 * index[0] + i)),
                pl.BlockSpec((total, columns), lambda i, j, index: (0, j)),
            ]
            + [out] * len(more),
            out_specs=out,
        ),
        out_shape=like((width // 2, n), bf16),
        compiler_params=pltpu.CompilerParams(vmem_limit_bytes=ROOM),
        cost_estimate=pl.CostEstimate(
            flops=total * width * n,
            bytes_accessed=total * width + 2 * total * n + 2 * width * n,
            transcendentals=0,
        ),
        name="weight_grad",
    )(index[None], left, right, *more)


def split_qkv(w_query, w_key, w_value, gain):
    own, n = w_query.shape[0], GROUP * HD

    def kernel(q_ref, k_ref, v_ref, gain_ref, out_ref):
        for g in range(TP):
            parts = [ref[:, g * HD : (g + 1) * HD].astype(f32) for ref in (k_ref, v_ref)]
            query = q_ref[:, g * n : (g + 1) * n].astype(f32)
            out_ref[g, :, :n] = (query * gain_ref[...]).astype(bf16)
            out_ref[g, :, n:] = (jnp.concatenate(parts, axis=1) * gain_ref[...]).astype(bf16)

    return small_call(
        kernel,
        "split_qkv",
        [w_query, w_key, w_value, gain],
        [like((TP, own, n + 2 * HD), bf16)],
    )[0]


def merge_qkv(raw, w_query, w_key, w_value, gain):
    own, n = w_query.shape[0], GROUP * HD

    def kernel(in_ref, q_ref, k_ref, v_ref, gain_ref, dq_ref, dk_ref, dv_ref, dgain_ref):
        keys, values = [], []
        dgain = jnp.zeros((own, 1), f32)
        for g in range(TP):
            here = slice(g * n, (g + 1) * n)
            part = in_ref[g, :, :n].astype(f32)
            dgain += jnp.sum(part * q_ref[:, here].astype(f32), axis=1, keepdims=True)
            dq_ref[:, here] = part * gain_ref[...]
            part = in_ref[g, :, n:].astype(f32)
            keys.append(part[:, :HD])
            values.append(part[:, HD:])
        for parts, ref, out_ref in ((keys, k_ref, dk_ref), (values, v_ref, dv_ref)):
            part = jnp.concatenate(parts, axis=1)
            dgain += jnp.sum(part * ref[...].astype(f32), axis=1, keepdims=True)
            out_ref[...] = part * gain_ref[...]
        dgain_ref[...] = dgain

    return small_call(
        kernel,
        "merge_qkv",
        [raw, w_query, w_key, w_value, gain],
        [like(w.shape, f32) for w in (w_query, w_key, w_value)] + [like((own, 1), f32)],
    )


def split_gate_up(w_gate, w_up, gain):
    own, total = w_gate.shape
    ff = total // TP

    def kernel(gate_ref, up_ref, gain_ref, out_ref):
        for g in range(TP):
            for j in range(ff // LANES):
                here = slice(g * ff + j * LANES, g * ff + (j + 1) * LANES)
                for ref, at in zip((gate_ref, up_ref), interleaved(j)):
                    out_ref[g, :, at] = (ref[:, here].astype(f32) * gain_ref[...]).astype(bf16)

    return small_call(
        kernel,
        "split_gate_up",
        [w_gate, w_up, gain],
        [jax.ShapeDtypeStruct((TP, own, 2 * ff), bf16)],
    )[0]


def merge_gate_up(raw, w_gate, w_up, gain):
    own, total = w_gate.shape
    ff = total // TP

    def kernel(in_ref, gate_ref, up_ref, gain_ref, dgate_ref, dup_ref, dgain_ref):
        dgain = jnp.zeros((own, LANES), f32)
        for g in range(TP):
            for j in range(ff // LANES):
                here = slice(g * ff + j * LANES, g * ff + (j + 1) * LANES)
                for ref, out_ref, at in zip(
                    (gate_ref, up_ref), (dgate_ref, dup_ref), interleaved(j)
                ):
                    part = in_ref[g, :, at].astype(f32)
                    dgain += part * ref[:, here].astype(f32)
                    out_ref[:, here] = part * gain_ref[...]
        dgain_ref[...] = jnp.sum(dgain, axis=1, keepdims=True)

    return small_call(
        kernel,
        "merge_gate_up",
        [raw, w_gate, w_up, gain],
        [
            jax.ShapeDtypeStruct((own, total), f32),
            jax.ShapeDtypeStruct((own, total), f32),
            jax.ShapeDtypeStruct((own, 1), f32),
        ],
    )


def make_body(reps, ctxs):
    pair = [(0, 1), (1, 0)]

    def swap(v, k):
        if k == 0:
            return v
        if k == 1:
            return lax.ppermute(v, "tx", pair)
        if k == 2:
            return lax.ppermute(v, "ty", pair)
        return lax.ppermute(v, ("ty", "tx"), [(i, i ^ 3) for i in range(TP)])

    def swap_ctx(v, j):
        return lax.ppermute(v, "ctx", [(i, i ^ j) for i in range(ctxs)]) if j else v

    def halves(v):
        half = v.shape[0] // 2
        return v[:half], v[half:]

    def in_order(a, b):
        return [p for k in range(TP) for p in (a[k], b[k])]

    def gather(a, b):
        ax, by = swap(a, 1), swap(b, 2)
        ay, bx = swap(a, 2), swap(b, 1)
        return in_order((a, ax, ay, swap(ax, 2)), (b, bx, by, swap(by, 1)))

    def scatter_far(parts):
        a, b = halves(parts[3])
        return swap(a, 2), swap(b, 1)

    def scatter_near(parts, far):
        a1, b1 = halves(parts[1])
        a2, b2 = halves(parts[2])
        a1 = (a1.astype(f32) + far[0].astype(f32)).astype(bf16)
        b2 = (b2.astype(f32) + far[1].astype(f32)).astype(bf16)
        return [swap(a2, 2), swap(a1, 1), swap(b1, 1), swap(b2, 2)]

    def by_member(v):
        return v.reshape(TP, -1, v.shape[1])

    def exchange(blocks, t, *first):
        out = jnp.zeros_like(blocks)
        for k in range(TP):
            come = swap(lax.dynamic_index_in_dim(blocks, t ^ k, 0, keepdims=True), k)
            come = after(come, *first) if first else come
            out = lax.dynamic_update_slice_in_dim(out, come, t ^ k, 0)
        return out

    def spread(blocks, t, *first):
        return exchange(blocks, t, *first).reshape(-1, blocks.shape[2])

    def collect(summed_rows, t, *first):
        return exchange(summed_rows.reshape(TP, -1, summed_rows.shape[1]), t, *first)

    def whole(v):
        return lax.all_gather(v, ("rep", "ctx"), axis=0, tiled=True)

    def split_reps(full):
        if reps != 2:
            return lax.psum_scatter(full, "rep", scatter_dimension=0, tiled=True)
        r = lax.axis_index("rep")
        half = full.shape[0] // 2
        sent = lax.dynamic_slice_in_dim(full, (1 - r) * half, half, 0)
        mine = lax.dynamic_slice_in_dim(full, r * half, half, 0)
        sent = lax.ppermute(sent, "rep", pair)
        return (mine.astype(f32) + sent.astype(f32)).astype(bf16)

    def over_reps_first(left, right):
        if reps != 2:
            return tn(left, right).astype(bf16)
        index = 1 - lax.axis_index("rep")
        half = left.shape[1] // 2
        if half % (2 * LANES) == 0:
            return weight_grad(left, right, index)
        return tn(lax.dynamic_slice_in_dim(left, index * half, half, 1), right).astype(bf16)

    def over_reps_last(left, right, first):
        if reps != 2:
            return lax.psum_scatter(first, "rep", scatter_dimension=0, tiled=True)
        index = lax.axis_index("rep")
        half = left.shape[1] // 2
        come = lax.ppermute(first, "rep", pair)
        if half % (2 * LANES) == 0:
            return weight_grad(left, right, index, come)
        mine = lax.dynamic_slice_in_dim(left, index * half, half, 1)
        return (tn(mine, right) + come.astype(f32)).astype(bf16)

    def over_reps(left, right):
        return over_reps_last(left, right, over_reps_first(left, right))

    def owned(part):
        return lax.psum_scatter(part, "ctx", scatter_dimension=0, tiled=True)

    def half_of(v, j, other):
        index = lax.axis_index("ctx") // j % 2
        v = v.reshape(2, -1, v.shape[1])
        return lax.dynamic_index_in_dim(v, 1 - index if other else index, 0, False)

    def body(
        tokens,
        span_order,
        norm_attn,
        w_query,
        w_key,
        w_value,
        w_out,
        norm_mlp,
        w_gate,
        w_up,
        w_down,
        out_grad,
    ):
        count, width = tokens.shape
        held, natural = block_orders(width, reps * ctxs)
        span = count * ctxs // span_order.shape[1]
        per = count // span
        t = 2 * lax.axis_index("ty") + lax.axis_index("tx")
        c = lax.axis_index("ctx")
        gain_attn = norm_attn.astype(f32)[:, None]
        gain_mlp = norm_mlp.astype(f32)[:, None]

        out = whole(w_out)
        qkv_blocks = split_qkv(w_query, w_key, w_value, gain_attn)
        a, b = hold_tokens(after(tokens, qkv_blocks), held)
        qkv_mine, a, b = phase(spread(after(qkv_blocks, a), t), a, b)
        ax, by = swap(a, 1), swap(b, 2)
        ay, bx, axy, bxy = swap(a, 2), swap(b, 1), swap(ax, 2), swap(by, 1)
        qkv = whole(after(qkv_mine, out, ax, by))
        gate_up_blocks = split_gate_up(after(w_gate, qkv_mine), w_up, gain_mlp)
        orders = [swap(after(span_order, qkv_mine), k) for k in range(TP)]
        ay, bx, axy, bxy, gate_up_blocks = phase(ay, bx, axy, bxy, gate_up_blocks)
        x_pieces = in_order((a, ax, ay, axy), (b, bx, by, bxy))

        orders = jnp.concatenate(orders, axis=0).reshape(TP, ctxs, per)
        orders = jnp.concatenate(
            [lax.dynamic_slice_in_dim(orders, c ^ j, 1, 1) for j in range(ctxs)], axis=1
        ).reshape(TP, ctxs * per)
        positions = orders[:, :per, None] * span + jnp.arange(span, dtype=jnp.int32)
        half_dim = HD // 2
        frequency = jnp.power(rope_base, -jnp.arange(half_dim, dtype=f32) / half_dim)
        angles = frequency[:, None] * positions.reshape(TP, 1, count).astype(f32)
        cosine, sine = jnp.cos(angles), jnp.sin(angles)

        qt, kv, inverse = project(x_pieces, qkv, cosine, sine)
        gate_up_mine = spread(after(gate_up_blocks, axy, bxy), t, kv)
        kv_far = [swap_ctx(kv, j) for j in range(1, ctxs)]
        ga, gb = halves(after(out_grad, kv))
        kv, kv_far, gate_up_mine, gax, gby, x_all = phase(
            kv, kv_far, gate_up_mine, swap(ga, 1), swap(gb, 2), join_rows(after(x_pieces, kv))
        )
        kv_pieces = [kv, *kv_far]
        gate_up = whole(gate_up_mine)
        down = whole(after(w_down, gate_up_mine))
        mixed, logsum, parts = [None] * TP, [None] * TP, [None] * TP

        def attend_to(members, queries):
            results = attend(
                members,
                orders,
                [queries[k] for k in members],
                kv_pieces,
                out,
                f32 if 0 in members else bf16,
            )
            for k, (mixed[k], logsum[k], parts[k]) in zip(members, results):
                pass

        attend_to((3,), qt)
        queries, gay, gbx = phase(qt, swap(ga, 2), swap(gb, 1), parts[3])[:3]
        far = scatter_far(parts)
        attend_to((2, 1), queries)
        far, parts[1], parts[2], queries, gaxy, gbxy = phase(
            far, parts[1], parts[2], queries, swap(gax, 2), swap(gby, 1)
        )
        near = scatter_near(parts, far)
        attend_to((0,), queries)
        g_all = join_rows(in_order((ga, gax, gay, gaxy), (gb, gbx, gby, gbxy)))
        near, parts[0], g_all = phase(near, parts[0], g_all)
        middle, inverse_mid, a, b = finish_middle(tokens, [parts[0], *near], held)
        n2_pieces = gather(a, b)

        act, slopes = activate(n2_pieces, gate_up)
        n2_all = join_rows(after(n2_pieces, act))
        part_down = over_reps(act, g_all)
        slopes, part_down, n2_all = phase(slopes, part_down, n2_all)
        down_sent = jnp.split(half_of(part_down, ctxs // 2, True), DOWN_STEPS, axis=1)
        down_come = []

        def send_down(*first):
            piece = after(down_sent[len(down_come)], *first)
            down_come.append(swap_ctx(piece, ctxs // 2))
            return down_come[-1]

        grad_act = activate_back(g_all, down, slopes)
        sent = over_reps_first(n2_all, grad_act)
        sent, down_come[-1] = phase(sent, send_down(down))
        part_gate_up = over_reps_last(n2_all, after(grad_act, sent), sent)
        sum_gate_up = owned(part_gate_up)
        parts = by_member(nt(after(grad_act, part_gate_up), gate_up).astype(bf16))
        parts, down_come[-1] = phase(parts, send_down(sent))
        far = scatter_far(parts)
        near = scatter_near(parts, far)
        forward = nn(after(act, far), down).astype(bf16)
        near, forward = phase(near, forward)
        grad_middle, a, b = finish_norm_back(
            out_grad, middle, inverse_mid, [(parts, 0), *near], natural, False
        )
        part_down = half_of(part_down, ctxs // 2, False).astype(f32)
        part_down = part_down + jnp.concatenate(down_come, axis=1).astype(f32)

        back_of = [None] * TP

        def attend_back_to(members, *grads):
            results = attend_back(
                members,
                orders,
                out,
                kv_pieces,
                [
                    (qt[k], mixed[k], logsum[k], *g, inverse[k], (cosine, k), (sine, k))
                    for k, g in zip(members, grads)
                ],
            )
            for k, back_of[k] in zip(members, results):
                pass

        attend_back_to((0,), (a, b))
        ax, by, ay, bx, back_of[0] = phase(
            swap(a, 1), swap(b, 2), swap(a, 2), swap(b, 1), back_of[0]
        )
        forward = by_member(forward)
        attend_back_to((1, 2), (ax, bx), (ay, by))
        axy, bxy, far, back_of[1], back_of[2] = phase(
            swap(ax, 2), swap(by, 1), scatter_far(forward), back_of[1], back_of[2]
        )
        keys_near = [
            swap_ctx(jnp.stack([back_of[k][3][(j - 1) * count : j * count] for k in range(3)]), j)
            for j in range(1, ctxs)
        ]
        attend_back_to((3,), (axy, bxy))
        keys_near, back_of[3] = phase(keys_near, back_of[3])
        keys_last = [
            swap_ctx(back_of[3][3][None, (j - 1) * count : j * count], j) for j in range(1, ctxs)
        ]
        db_pieces = in_order((a, ax, ay, axy), (b, bx, by, bxy))
        part_out = out_gradient(mixed, after(db_pieces, back_of[3]))
        forward_near = scatter_near(after(forward, keys_near), far)
        keys_last, part_out = phase(keys_last, split_reps(part_out))
        sum_out = owned(part_out)
        grad_proj, scaled_proj = finish_keys(
            [v[2] for v in back_of],
            keys_near,
            keys_last,
            [v[0] for v in back_of],
            [v[1] for v in back_of],
            inverse,
            cosine,
            sine,
        )
        parts = by_member(nt(grad_proj, qkv).astype(bf16))
        down_come = swap_ctx(
            half_of(after(part_down, keys_last).astype(bf16), ctxs // 4, True), ctxs // 4
        )
        parts, sum_gate_up, down_come = phase(parts, sum_gate_up, down_come)
        far = scatter_far(parts)
        sent = over_reps_first(x_all, after(scaled_proj, parts))
        far, sent, forward_near = phase(far, sent, forward_near)
        near = scatter_near(parts, far)
        part_qkv = over_reps_last(x_all, after(scaled_proj, sent), sent)
        sum_qkv = owned(part_qkv)
        layer_out = finish_layer(middle, [(forward, 0), *forward_near])
        near, layer_out = phase(near, layer_out, part_qkv)[:2]
        sum_down = half_of(part_down, ctxs // 4, False) + down_come.astype(f32)
        (input_grad,) = finish_norm_back(
            grad_middle, tokens, inverse[0], [(parts, 0), *near], natural, True
        )
        raw_gate_up = collect(after(sum_gate_up, input_grad), t)

        grad_gate, grad_up, grad_norm_mlp = merge_gate_up(
            raw_gate_up, w_gate, w_up, gain_mlp
        )
        sum_out, sum_qkv = after((sum_out, sum_qkv), input_grad)
        grad_query, grad_key, grad_value, grad_norm_attn = merge_qkv(
            collect(sum_qkv, t), w_query, w_key, w_value, gain_attn
        )
        return (
            layer_out,
            input_grad,
            grad_norm_attn[:, 0],
            grad_query,
            grad_key,
            grad_value,
            sum_out.astype(f32),
            grad_norm_mlp[:, 0],
            grad_gate,
            grad_up,
            sum_down,
        )

    return body


def solution(mesh):
    sequences, ctxs = mesh.shape["dp"], mesh.shape["ctx"]
    reps = sequences // TP
    names = ("ty", "tx", "rep", "ctx")
    grid = Mesh(mesh.devices.reshape(2, 2, reps, ctxs), names)
    matrix, vector = P(names, None), P(names)
    order = P(("ty", "tx", "rep"), None)
    weights = [vector, matrix, matrix, matrix, matrix, vector, matrix, matrix, matrix]
    return jax.shard_map(
        make_body(reps, ctxs),
        mesh=grid,
        in_specs=(matrix, order, *weights, matrix),
        out_specs=(matrix, matrix, *weights),
        check_vma=False,
    )
```

```python
import jax
import jax.numpy as jnp
from jax import lax
from jax.experimental import pallas as pl
from jax.experimental.pallas import tpu as pltpu
from jax.sharding import Mesh, PartitionSpec as P

H = 32
KV = 4
HD = 64
TP = 4
GROUP = H // KV
LANES = 128
ROWS = 64
ROOM = 60 << 20
ATTEND_ROOM = 60 << 20
DOWN_STEPS = 4

epsilon = 1e-05
rope_base = 10000.0
masked_score = -1e30
bf16 = jnp.bfloat16
f32 = jnp.float32


def after(value, *others):
    return lax.optimization_barrier((value,) + others)[0]


def phase(*values):
    return lax.optimization_barrier(values)


def nn(left, right):
    return lax.dot_general(left, right, (((1,), (0,)), ((), ())), preferred_element_type=f32)


def nt(left, right):
    return lax.dot_general(left, right, (((1,), (1,)), ((), ())), preferred_element_type=f32)


def tn(left, right):
    return lax.dot_general(left, right, (((0,), (0,)), ((), ())), preferred_element_type=f32)


def like(shape, kind):
    return jax.ShapeDtypeStruct(shape, kind)


def size_of(values):
    return sum(v.size * v.dtype.itemsize for v in values)


def small_call(
    kernel, name, inputs, outputs, flops=0, scratch=(), scalars=0, transcendentals=0, room=ROOM
):
    specs, arrays = [pl.BlockSpec(memory_space=pltpu.SMEM)] * scalars, list(inputs[:scalars])
    for v in inputs[scalars:]:
        if isinstance(v, tuple):
            specs.append(row_block(*v))
            arrays.append(v[0])
        else:
            specs.append(whole_block(v.shape))
            arrays.append(v)
    size = size_of((*arrays, *outputs))
    return pl.pallas_call(
        kernel,
        grid=(1,),
        in_specs=specs,
        out_specs=[whole_block(v.shape) for v in outputs],
        out_shape=outputs,
        scratch_shapes=list(scratch),
        compiler_params=pltpu.CompilerParams(vmem_limit_bytes=room),
        cost_estimate=pl.CostEstimate(
            flops=max(flops, size), bytes_accessed=size, transcendentals=transcendentals
        ),
        name=name,
    )(*arrays)


def row_block(array, index):
    shape = array.shape[1:]
    return pl.BlockSpec((None,) + shape, lambda i: (index,) + (0,) * len(shape))


def whole_block(shape):
    return pl.BlockSpec(shape, lambda i: (0,) * len(shape))


def turn(vectors, cosine, sine):
    half = HD // 2
    out = []
    for at in range(0, vectors.shape[0], HD):
        first, second = vectors[at : at + half], vectors[at + half : at + HD]
        out += [first * cosine - second * sine, second * cosine + first * sine]
    return jnp.concatenate(out, axis=0)


def project(pieces, w, cosine, sine):
    half, width = pieces[0].shape
    rows, n, q = 2 * half, w.shape[1], GROUP * HD

    def kernel(*refs):
        x_refs, (w_ref, cos_ref, sin_ref, kv_ref), outs = refs[:8], refs[8:12], refs[12:]
        for k in range(TP):
            xb = jnp.concatenate([x_refs[2 * k][...], x_refs[2 * k + 1][...]], axis=0)
            x = xb.astype(f32)
            inverse = lax.rsqrt(jnp.mean(x * x, axis=1, keepdims=True) + epsilon)
            outs[TP + k][...] = inverse
            flat = (nn(xb, w_ref[...]) * inverse).T
            cosine, sine = cos_ref[k], sin_ref[k]
            outs[k][...] = (turn(flat[:q], cosine, sine) * HD**-0.5).astype(bf16)
            kv = jnp.concatenate([turn(flat[q : q + HD], cosine, sine), flat[q + HD :]], axis=0)
            kv_ref[k] = kv.T.astype(bf16)

    kv, *outs = small_call(
        kernel,
        "project",
        [*pieces, w, cosine, sine],
        [like((TP, rows, 2 * HD), bf16)]
        + [like((q, rows), bf16)] * TP
        + [like((rows, 1), f32)] * TP,
        flops=2 * TP * rows * width * n,
    )
    return outs[:TP], kv, outs[TP:]


def set_bias(order_ref, k, bias_ref):
    keys, rows = bias_ref.shape
    span = keys // order_ref.shape[1]
    lane = lax.broadcasted_iota(jnp.int32, (span, rows), 1)
    query = jnp.where(lane < span, order_ref[k, 0], order_ref[k, 1] - 1) * span + lane
    row = lax.broadcasted_iota(jnp.int32, (span, rows), 0)
    for b in range(keys // span):
        key = order_ref[k, b] * span + row
        bias_ref[b * span : (b + 1) * span, :] = jnp.where(query >= key, 0.0, masked_score)


def attend(members, orders, queries, kv_pieces, wo, kind):
    n, rows = queries[0].shape
    holders, width = len(kv_pieces), wo.shape[1]
    keys, count = holders * rows, len(members)

    def kernel(order_ref, wo_ref, *refs):
        for i, k in enumerate(members):
            qt_ref, *kv_refs = refs[i * (1 + holders) : (i + 1) * (1 + holders)]
            outs = refs[count * (1 + holders) :]
            ot_ref, lse_ref, part_ref = outs[3 * i : 3 * i + 3]
            bias_ref = outs[-1]
            set_bias(order_ref, k, bias_ref)
            kv = jnp.concatenate([ref[...] for ref in kv_refs], axis=0)
            vt = kv.astype(f32).T[HD:].astype(bf16)
            zero = jnp.zeros((HD, rows), bf16)
            for h in range(GROUP):
                at = slice(h * HD, (h + 1) * HD)
                scores = nn(kv, jnp.concatenate([qt_ref[at, :], zero], axis=0)) + bias_ref[...]
                top = jnp.max(scores, axis=0, keepdims=True)
                exponent = jnp.exp(scores - top)
                total = jnp.sum(exponent, axis=0, keepdims=True)
                ot_ref[at, :] = (nn(vt, exponent.astype(bf16)) / total).astype(bf16)
                lse_ref[h : h + 1, :] = top + jnp.log(total)
            part_ref[...] = tn(ot_ref[...], wo_ref[...]).astype(part_ref.dtype)

    inputs, outputs = [orders, wo], []
    for i, k in enumerate(members):
        inputs += [queries[i], *[(piece, k) for piece in kv_pieces]]
        outputs += [like((n, rows), bf16), like((GROUP, rows), f32), like((rows, width), kind)]
    results = small_call(
        kernel,
        "attend",
        inputs,
        outputs,
        flops=2 * rows * n * (keys * 2 * 4 + width) * count,
        scratch=[pltpu.VMEM((keys, rows), f32)],
        scalars=1,
        transcendentals=GROUP * rows * keys * count,
        room=ATTEND_ROOM,
    )
    return [results[3 * i : 3 * i + 3] for i in range(count)]


def attend_back(members, orders, wo, kv_pieces, details):
    n, rows = details[0][0].shape
    holders, width = len(kv_pieces), wo.shape[1]
    keys, half, count = holders * rows, rows // 2, len(members)
    step = 8 + holders

    def kernel(order_ref, wo_ref, *refs):
        outs, (bias_ref, dat_ref, dqt_ref, dkv_ref) = refs[count * step : -4], refs[-4:]
        for i, k in enumerate(members):
            own = refs[i * step : (i + 1) * step]
            kv_refs, (qt_ref, ot_ref, lse_ref, a_ref, b_ref) = own[:holders], own[holders:-3]
            inv_ref, cos_ref, sin_ref = own[-3:]
            dq_ref, dqs_ref, own_ref, far_ref = outs[4 * i : 4 * i + 4]
            set_bias(order_ref, k, bias_ref)
            kv = jnp.concatenate([ref[...] for ref in kv_refs], axis=0)
            kt = kv.astype(f32).T[:HD].astype(bf16)
            zero = jnp.zeros((HD, rows), bf16)
            dat_ref[:, :half] = nt(wo_ref[...], a_ref[...]).astype(bf16)
            dat_ref[:, half:] = nt(wo_ref[...], b_ref[...]).astype(bf16)
            for h in range(GROUP):
                at = slice(h * HD, (h + 1) * HD)
                q_low = jnp.concatenate([qt_ref[at, :], zero], axis=0)
                da_high = jnp.concatenate([zero, dat_ref[at, :]], axis=0)
                weights = jnp.exp(nn(kv, q_low) + bias_ref[...] - lse_ref[h : h + 1, :])
                delta = jnp.sum(
                    dat_ref[at, :].astype(f32) * ot_ref[at, :].astype(f32), axis=0, keepdims=True
                )
                ds = (weights * (nn(kv, da_high) - delta)).astype(bf16)
                dkv = nt(ds, q_low) + nt(weights.astype(bf16), da_high)
                if h == 0:
                    dkv_ref[...] = dkv
                else:
                    dkv_ref[...] += dkv
                dqt_ref[at, :] = nn(kt, ds)
            dq = (turn(dqt_ref[...], cos_ref[...], -sin_ref[...]) * HD**-0.5).T
            dq_ref[...] = dq.astype(bf16)
            dqs_ref[...] = (dq * inv_ref[...]).astype(bf16)
            own_ref[...] = dkv_ref[:rows, :]
            far_ref[...] = dkv_ref[rows:, :].astype(bf16)

    inputs, outputs = [orders, wo], []
    for k, detail in zip(members, details):
        inputs += [*[(piece, k) for piece in kv_pieces], *detail]
        outputs += [
            like((rows, n), bf16),
            like((rows, n), bf16),
            like((rows, 2 * HD), f32),
            like((keys - rows, 2 * HD), bf16),
        ]
    results = small_call(
        kernel,
        "attend_back",
        inputs,
        outputs,
        flops=2 * rows * n * (keys * 5 * 4 + width) * count,
        scratch=[
            pltpu.VMEM((keys, rows), f32),
            pltpu.VMEM((n, rows), bf16),
            pltpu.VMEM((n, rows), f32),
            pltpu.VMEM((keys, 2 * HD), f32),
        ],
        scalars=1,
        transcendentals=GROUP * rows * keys * count,
        room=ATTEND_ROOM,
    )
    return [results[4 * i : 4 * i + 4] for i in range(count)]


def out_gradient(mixed, grads):
    n, rows = mixed[0].shape
    width = grads[0].shape[1]

    def kernel(*refs):
        total = 0.0
        for k in range(TP):
            db = jnp.concatenate([refs[TP + 2 * k][...], refs[TP + 2 * k + 1][...]], axis=0)
            total = total + nn(refs[k][...], db)
        refs[-1][...] = total.astype(bf16)

    return small_call(
        kernel,
        "out_gradient",
        [*mixed, *grads],
        [like((n, width), bf16)],
        flops=2 * TP * rows * n * width,
    )[0]


def finish_keys(own, near, last, dq, dqs, inverse, cosine, sine):
    rows, n = dq[0].shape

    def kernel(*refs):
        own_refs, refs = refs[:TP], refs[TP:]
        near_refs, refs = refs[: len(near)], refs[len(near) :]
        last_refs, refs = refs[: len(last)], refs[len(last) :]
        dq_refs, dqs_refs, refs = refs[:TP], refs[TP : 2 * TP], refs[2 * TP :]
        inv_refs, (cos_ref, sin_ref, plain_ref, scaled_ref) = refs[:TP], refs[TP:]
        for k in range(TP):
            total = own_refs[k][...]
            for ref in near_refs if k < TP - 1 else last_refs:
                total = total + ref[k % (TP - 1)].astype(f32)
            total = total.T
            keys = turn(total[:HD], cos_ref[k], -sin_ref[k])
            total = jnp.concatenate([keys, total[HD:]], axis=0).T
            at = slice(k * rows, (k + 1) * rows)
            plain_ref[at, :n] = dq_refs[k][...]
            plain_ref[at, n:] = total.astype(bf16)
            scaled_ref[at, :n] = dqs_refs[k][...]
            scaled_ref[at, n:] = (total * inv_refs[k][...]).astype(bf16)

    shape = like((TP * rows, n + 2 * HD), bf16)
    return small_call(
        kernel,
        "finish_keys",
        [*own, *near, *last, *dq, *dqs, *inverse, cosine, sine],
        [shape, shape],
    )


def join_rows(pieces):
    rows, width = pieces[0].shape

    def kernel(*refs):
        for i, ref in enumerate(refs[:-1]):
            refs[-1][i * rows : (i + 1) * rows, :] = ref[...]

    return small_call(
        kernel, "join_rows", pieces, [like((len(pieces) * rows, width), pieces[0].dtype)]
    )[0]


def reorder_lanes(v, ordered):
    order, size = ordered
    return jnp.concatenate([v[:, i * size : (i + 1) * size] for i in order], axis=1)


def block_orders(width, holders):
    held = [m * holders + h for h in range(holders) for m in range(TP)]
    natural = [held.index(i) for i in range(len(held))]
    size = width // len(held)
    return (held, size), (natural, size)


def hold_tokens(tokens, held):
    half = tokens.shape[0] // 2

    def kernel(x_ref, a_ref, b_ref):
        a_ref[...] = reorder_lanes(x_ref[:half, :].astype(f32), held).astype(bf16)
        b_ref[...] = reorder_lanes(x_ref[half:, :].astype(f32), held).astype(bf16)

    shape = like((half, tokens.shape[1]), bf16)
    return small_call(kernel, "hold_tokens", [tokens], [shape, shape])


def summed(refs, at, half):
    own_ref, a2_ref, a1_ref, b1_ref, b2_ref = refs
    first, second = (a2_ref, a1_ref) if at < half else (b1_ref, b2_ref)
    come = slice(at % half, at % half + ROWS)
    total = own_ref[at : at + ROWS, :].astype(f32)
    return total + first[come, :].astype(f32) + second[come, :].astype(f32)


def finish_middle(tokens, pieces, held):
    rows, width = tokens.shape
    half = rows // 2

    def kernel(x_ref, *refs):
        sums, (mid_ref, inv_ref, a_ref, b_ref) = refs[:5], refs[5:]
        for at in range(0, rows, ROWS):
            here = slice(at, at + ROWS)
            middle = x_ref[here, :].astype(f32) + summed(sums, at, half)
            inverse = lax.rsqrt(jnp.mean(middle * middle, axis=1, keepdims=True) + epsilon)
            mid_ref[here, :] = middle
            inv_ref[here, :] = inverse
            out = a_ref if at < half else b_ref
            come = slice(at % half, at % half + ROWS)
            out[come, :] = reorder_lanes(middle * inverse, held).astype(bf16)

    return small_call(
        kernel,
        "finish_middle",
        [tokens, *pieces],
        [
            like((rows, width), f32),
            like((rows, 1), f32),
            like((half, width), bf16),
            like((half, width), bf16),
        ],
    )


def finish_norm_back(grad, normed_from, inverse, pieces, natural, last):
    rows, width = grad.shape
    half = rows // 2

    def kernel(g_ref, x_ref, inv_ref, *refs):
        sums, outs = refs[:5], refs[5:]
        for at in range(0, rows, ROWS):
            here = slice(at, at + ROWS)
            scaled = reorder_lanes(summed(sums, at, half), natural)
            inverse = inv_ref[here, :]
            normed = x_ref[here, :].astype(f32) * inverse
            mean = jnp.mean(scaled * normed, axis=1, keepdims=True)
            total = g_ref[here, :].astype(f32) + inverse * (scaled - normed * mean)
            outs[0][here, :] = total
            if not last:
                out = outs[1] if at < half else outs[2]
                out[at % half : at % half + ROWS, :] = total.astype(bf16)

    shapes = [like((rows, width), f32)]
    if not last:
        shapes += [like((half, width), bf16)] * 2
    return small_call(
        kernel, "finish_norm_back", [grad, normed_from, inverse, *pieces], shapes
    )


def finish_layer(middle, pieces):
    rows, width = middle.shape

    def kernel(mid_ref, *refs):
        for at in range(0, rows, ROWS):
            here = slice(at, at + ROWS)
            total = mid_ref[here, :] + summed(refs[:5], at, rows // 2)
            refs[5][here, :] = total.astype(bf16)

    return small_call(
        kernel, "finish_layer", [middle, *pieces], [like((rows, width), bf16)]
    )[0]


def interleaved(i):
    return slice(2 * i * LANES, (2 * i + 1) * LANES), slice((2 * i + 1) * LANES, (2 * i + 2) * LANES)


def activate(pieces, gate_up, tile=256):
    half, width = pieces[0].shape
    total, ff = half * len(pieces), gate_up.shape[1] // 2

    def kernel(*refs):
        n_refs, (w_ref, m_ref, slope_ref, n2_ref) = refs[: len(pieces)], refs[len(pieces) :]

        @pl.when(pl.program_id(0) == 0)
        def _():
            for i, ref in enumerate(n_refs):
                n2_ref[i * half : (i + 1) * half, :] = ref[...]

        both = nn(n2_ref[...], w_ref[...])
        for i in range(tile // LANES):
            gate_at, up_at = interleaved(i)
            gate, up = both[:, gate_at], both[:, up_at]
            sigmoid = jax.nn.sigmoid(gate)
            silu = gate * sigmoid
            m_ref[:, i * LANES : (i + 1) * LANES] = (silu * up).astype(bf16)
            slope_ref[:, gate_at] = (up * (sigmoid + silu * (1.0 - sigmoid))).astype(bf16)
            slope_ref[:, up_at] = silu.astype(bf16)

    return pl.pallas_call(
        kernel,
        grid=(pl.cdiv(ff, tile),),
        in_specs=[whole_block(v.shape) for v in pieces]
        + [pl.BlockSpec((width, 2 * tile), lambda j: (0, j))],
        out_specs=[
            pl.BlockSpec((total, tile), lambda j: (0, j)),
            pl.BlockSpec((total, 2 * tile), lambda j: (0, j)),
        ],
        out_shape=[like((total, ff), bf16), like((total, 2 * ff), bf16)],
        scratch_shapes=[pltpu.VMEM((total, width), bf16)],
        compiler_params=pltpu.CompilerParams(vmem_limit_bytes=ROOM),
        cost_estimate=pl.CostEstimate(
            flops=4 * total * width * ff,
            bytes_accessed=2 * (total * width + 2 * width * ff + 3 * total * ff),
            transcendentals=total * ff,
        ),
        name="activate",
    )(*pieces, gate_up)


def activate_back(g, down, slopes, tile=256):
    total, width = g.shape
    ff = down.shape[0]

    def kernel(g_ref, down_ref, slope_ref, d_ref):
        dm = nt(g_ref[...], down_ref[...])
        for i in range(tile // LANES):
            part = dm[:, i * LANES : (i + 1) * LANES]
            for at in interleaved(i):
                d_ref[:, at] = (part * slope_ref[:, at].astype(f32)).astype(bf16)

    return pl.pallas_call(
        kernel,
        grid=(pl.cdiv(ff, tile),),
        in_specs=[
            pl.BlockSpec((total, width), lambda j: (0, 0)),
            pl.BlockSpec((tile, width), lambda j: (j, 0)),
            pl.BlockSpec((total, 2 * tile), lambda j: (0, j)),
        ],
        out_specs=pl.BlockSpec((total, 2 * tile), lambda j: (0, j)),
        out_shape=like((total, 2 * ff), bf16),
        compiler_params=pltpu.CompilerParams(vmem_limit_bytes=ROOM),
        cost_estimate=pl.CostEstimate(
            flops=2 * total * width * ff,
            bytes_accessed=2 * (total * width + width * ff + 4 * total * ff),
            transcendentals=0,
        ),
        name="activate_back",
    )(g, down, slopes)


def weight_grad(left, right, index, come=None):
    total, width = left.shape
    n = right.shape[1]
    rows, columns = width // 4, n // 2 if n % (2 * LANES) == 0 else n

    def kernel(index_ref, left_ref, right_ref, *refs):
        part = tn(left_ref[...], right_ref[...])
        if come is not None:
            part = part + refs[0][...].astype(f32)
        refs[-1][...] = part.astype(bf16)

    out = pl.BlockSpec((rows, columns), lambda i, j, index: (i, j))
    more = [] if come is None else [come]
    return pl.pallas_call(
        kernel,
        grid_spec=pltpu.PrefetchScalarGridSpec(
            num_scalar_prefetch=1,
            grid=(2, n // columns),
            in_specs=[
                pl.BlockSpec((total, rows), lambda i, j, index: (0, 2 * index[0] + i)),
                pl.BlockSpec((total, columns), lambda i, j, index: (0, j)),
            ]
            + [out] * len(more),
            out_specs=out,
        ),
        out_shape=like((width // 2, n), bf16),
        compiler_params=pltpu.CompilerParams(vmem_limit_bytes=ROOM),
        cost_estimate=pl.CostEstimate(
            flops=total * width * n,
            bytes_accessed=total * width + 2 * total * n + 2 * width * n,
            transcendentals=0,
        ),
        name="weight_grad",
    )(index[None], left, right, *more)


def split_qkv(w_query, w_key, w_value, gain):
    own, n = w_query.shape[0], GROUP * HD

    def kernel(q_ref, k_ref, v_ref, gain_ref, out_ref):
        for g in range(TP):
            parts = [ref[:, g * HD : (g + 1) * HD].astype(f32) for ref in (k_ref, v_ref)]
            query = q_ref[:, g * n : (g + 1) * n].astype(f32)
            out_ref[g, :, :n] = (query * gain_ref[...]).astype(bf16)
            out_ref[g, :, n:] = (jnp.concatenate(parts, axis=1) * gain_ref[...]).astype(bf16)

    return small_call(
        kernel,
        "split_qkv",
        [w_query, w_key, w_value, gain],
        [like((TP, own, n + 2 * HD), bf16)],
    )[0]


def merge_qkv(raw, w_query, w_key, w_value, gain):
    own, n = w_query.shape[0], GROUP * HD

    def kernel(in_ref, q_ref, k_ref, v_ref, gain_ref, dq_ref, dk_ref, dv_ref, dgain_ref):
        keys, values = [], []
        dgain = jnp.zeros((own, 1), f32)
        for g in range(TP):
            here = slice(g * n, (g + 1) * n)
            part = in_ref[g, :, :n].astype(f32)
            dgain += jnp.sum(part * q_ref[:, here].astype(f32), axis=1, keepdims=True)
            dq_ref[:, here] = part * gain_ref[...]
            part = in_ref[g, :, n:].astype(f32)
            keys.append(part[:, :HD])
            values.append(part[:, HD:])
        for parts, ref, out_ref in ((keys, k_ref, dk_ref), (values, v_ref, dv_ref)):
            part = jnp.concatenate(parts, axis=1)
            dgain += jnp.sum(part * ref[...].astype(f32), axis=1, keepdims=True)
            out_ref[...] = part * gain_ref[...]
        dgain_ref[...] = dgain

    return small_call(
        kernel,
        "merge_qkv",
        [raw, w_query, w_key, w_value, gain],
        [like(w.shape, f32) for w in (w_query, w_key, w_value)] + [like((own, 1), f32)],
    )


def split_gate_up(w_gate, w_up, gain):
    own, total = w_gate.shape
    ff = total // TP

    def kernel(gate_ref, up_ref, gain_ref, out_ref):
        for g in range(TP):
            for j in range(ff // LANES):
                here = slice(g * ff + j * LANES, g * ff + (j + 1) * LANES)
                for ref, at in zip((gate_ref, up_ref), interleaved(j)):
                    out_ref[g, :, at] = (ref[:, here].astype(f32) * gain_ref[...]).astype(bf16)

    return small_call(
        kernel,
        "split_gate_up",
        [w_gate, w_up, gain],
        [jax.ShapeDtypeStruct((TP, own, 2 * ff), bf16)],
    )[0]


def merge_gate_up(raw, w_gate, w_up, gain):
    own, total = w_gate.shape
    ff = total // TP

    def kernel(in_ref, gate_ref, up_ref, gain_ref, dgate_ref, dup_ref, dgain_ref):
        dgain = jnp.zeros((own, LANES), f32)
        for g in range(TP):
            for j in range(ff // LANES):
                here = slice(g * ff + j * LANES, g * ff + (j + 1) * LANES)
                for ref, out_ref, at in zip(
                    (gate_ref, up_ref), (dgate_ref, dup_ref), interleaved(j)
                ):
                    part = in_ref[g, :, at].astype(f32)
                    dgain += part * ref[:, here].astype(f32)
                    out_ref[:, here] = part * gain_ref[...]
        dgain_ref[...] = jnp.sum(dgain, axis=1, keepdims=True)

    return small_call(
        kernel,
        "merge_gate_up",
        [raw, w_gate, w_up, gain],
        [
            jax.ShapeDtypeStruct((own, total), f32),
            jax.ShapeDtypeStruct((own, total), f32),
            jax.ShapeDtypeStruct((own, 1), f32),
        ],
    )


def make_body(reps, ctxs):
    pair = [(0, 1), (1, 0)]

    def swap(v, k):
        if k == 0:
            return v
        if k == 1:
            return lax.ppermute(v, "tx", pair)
        if k == 2:
            return lax.ppermute(v, "ty", pair)
        return lax.ppermute(v, ("ty", "tx"), [(i, i ^ 3) for i in range(TP)])

    def swap_ctx(v, j):
        return lax.ppermute(v, "ctx", [(i, i ^ j) for i in range(ctxs)]) if j else v

    def halves(v):
        half = v.shape[0] // 2
        return v[:half], v[half:]

    def in_order(a, b):
        return [p for k in range(TP) for p in (a[k], b[k])]

    def gather(a, b):
        ax, by = swap(a, 1), swap(b, 2)
        ay, bx = swap(a, 2), swap(b, 1)
        return in_order((a, ax, ay, swap(ax, 2)), (b, bx, by, swap(by, 1)))

    def scatter_far(parts):
        a, b = halves(parts[3])
        return swap(a, 2), swap(b, 1)

    def scatter_near(parts, far):
        a1, b1 = halves(parts[1])
        a2, b2 = halves(parts[2])
        a1 = (a1.astype(f32) + far[0].astype(f32)).astype(bf16)
        b2 = (b2.astype(f32) + far[1].astype(f32)).astype(bf16)
        return [swap(a2, 2), swap(a1, 1), swap(b1, 1), swap(b2, 2)]

    def by_member(v):
        return v.reshape(TP, -1, v.shape[1])

    def exchange(blocks, t, *first):
        out = jnp.zeros_like(blocks)
        for k in range(TP):
            come = swap(lax.dynamic_index_in_dim(blocks, t ^ k, 0, keepdims=True), k)
            come = after(come, *first) if first else come
            out = lax.dynamic_update_slice_in_dim(out, come, t ^ k, 0)
        return out

    def spread(blocks, t, *first):
        return exchange(blocks, t, *first).reshape(-1, blocks.shape[2])

    def collect(summed_rows, t, *first):
        return exchange(summed_rows.reshape(TP, -1, summed_rows.shape[1]), t, *first)

    def whole(v):
        return lax.all_gather(v, ("rep", "ctx"), axis=0, tiled=True)

    def split_reps(full):
        if reps != 2:
            return lax.psum_scatter(full, "rep", scatter_dimension=0, tiled=True)
        r = lax.axis_index("rep")
        half = full.shape[0] // 2
        sent = lax.dynamic_slice_in_dim(full, (1 - r) * half, half, 0)
        mine = lax.dynamic_slice_in_dim(full, r * half, half, 0)
        sent = lax.ppermute(sent, "rep", pair)
        return (mine.astype(f32) + sent.astype(f32)).astype(bf16)

    def over_reps_first(left, right):
        if reps != 2:
            return tn(left, right).astype(bf16)
        index = 1 - lax.axis_index("rep")
        half = left.shape[1] // 2
        if half % (2 * LANES) == 0:
            return weight_grad(left, right, index)
        return tn(lax.dynamic_slice_in_dim(left, index * half, half, 1), right).astype(bf16)

    def over_reps_last(left, right, first):
        if reps != 2:
            return lax.psum_scatter(first, "rep", scatter_dimension=0, tiled=True)
        index = lax.axis_index("rep")
        half = left.shape[1] // 2
        come = lax.ppermute(first, "rep", pair)
        if half % (2 * LANES) == 0:
            return weight_grad(left, right, index, come)
        mine = lax.dynamic_slice_in_dim(left, index * half, half, 1)
        return (tn(mine, right) + come.astype(f32)).astype(bf16)

    def over_reps(left, right):
        return over_reps_last(left, right, over_reps_first(left, right))

    def owned(part):
        return lax.psum_scatter(part, "ctx", scatter_dimension=0, tiled=True)

    def half_of(v, j, other):
        index = lax.axis_index("ctx") // j % 2
        v = v.reshape(2, -1, v.shape[1])
        return lax.dynamic_index_in_dim(v, 1 - index if other else index, 0, False)

    def body(
        tokens,
        span_order,
        norm_attn,
        w_query,
        w_key,
        w_value,
        w_out,
        norm_mlp,
        w_gate,
        w_up,
        w_down,
        out_grad,
    ):
        count, width = tokens.shape
        held, natural = block_orders(width, reps * ctxs)
        span = count * ctxs // span_order.shape[1]
        per = count // span
        t = 2 * lax.axis_index("ty") + lax.axis_index("tx")
        c = lax.axis_index("ctx")
        gain_attn = norm_attn.astype(f32)[:, None]
        gain_mlp = norm_mlp.astype(f32)[:, None]

        out = whole(w_out)
        qkv_blocks = split_qkv(w_query, w_key, w_value, gain_attn)
        a, b = hold_tokens(after(tokens, qkv_blocks), held)
        qkv_mine, a, b = phase(spread(after(qkv_blocks, a), t), a, b)
        ax, by = swap(a, 1), swap(b, 2)
        ay, bx, axy, bxy = swap(a, 2), swap(b, 1), swap(ax, 2), swap(by, 1)
        qkv = whole(after(qkv_mine, out, ax, by))
        gate_up_blocks = split_gate_up(after(w_gate, qkv_mine), w_up, gain_mlp)
        orders = [swap(after(span_order, qkv_mine), k) for k in range(TP)]
        ay, bx, axy, bxy, gate_up_blocks = phase(ay, bx, axy, bxy, gate_up_blocks)
        x_pieces = in_order((a, ax, ay, axy), (b, bx, by, bxy))

        orders = jnp.concatenate(orders, axis=0).reshape(TP, ctxs, per)
        orders = jnp.concatenate(
            [lax.dynamic_slice_in_dim(orders, c ^ j, 1, 1) for j in range(ctxs)], axis=1
        ).reshape(TP, ctxs * per)
        positions = orders[:, :per, None] * span + jnp.arange(span, dtype=jnp.int32)
        half_dim = HD // 2
        frequency = jnp.power(rope_base, -jnp.arange(half_dim, dtype=f32) / half_dim)
        angles = frequency[:, None] * positions.reshape(TP, 1, count).astype(f32)
        cosine, sine = jnp.cos(angles), jnp.sin(angles)

        qt, kv, inverse = project(x_pieces, qkv, cosine, sine)
        gate_up_mine = spread(after(gate_up_blocks, axy, bxy), t, kv)
        kv_far = [swap_ctx(kv, j) for j in range(1, ctxs)]
        ga, gb = halves(after(out_grad, kv))
        kv, kv_far, gate_up_mine, gax, gby, x_all = phase(
            kv, kv_far, gate_up_mine, swap(ga, 1), swap(gb, 2), join_rows(after(x_pieces, kv))
        )
        kv_pieces = [kv, *kv_far]
        gate_up = whole(gate_up_mine)
        down = whole(after(w_down, gate_up_mine))
        mixed, logsum, parts = [None] * TP, [None] * TP, [None] * TP

        def attend_to(members, queries):
            results = attend(
                members,
                orders,
                [queries[k] for k in members],
                kv_pieces,
                out,
                f32 if 0 in members else bf16,
            )
            for k, (mixed[k], logsum[k], parts[k]) in zip(members, results):
                pass

        attend_to((3,), qt)
        queries, gay, gbx = phase(qt, swap(ga, 2), swap(gb, 1), parts[3])[:3]
        far = scatter_far(parts)
        attend_to((2, 1), queries)
        far, parts[1], parts[2], queries, gaxy, gbxy = phase(
            far, parts[1], parts[2], queries, swap(gax, 2), swap(gby, 1)
        )
        near = scatter_near(parts, far)
        attend_to((0,), queries)
        g_all = join_rows(in_order((ga, gax, gay, gaxy), (gb, gbx, gby, gbxy)))
        near, parts[0], g_all = phase(near, parts[0], g_all)
        middle, inverse_mid, a, b = finish_middle(tokens, [parts[0], *near], held)
        n2_pieces = gather(a, b)

        act, slopes = activate(n2_pieces, gate_up)
        n2_all = join_rows(after(n2_pieces, act))
        part_down = over_reps(act, g_all)
        slopes, part_down, n2_all = phase(slopes, part_down, n2_all)
        down_sent = jnp.split(half_of(part_down, ctxs // 2, True), DOWN_STEPS, axis=1)
        down_come = []

        def send_down(*first):
            piece = after(down_sent[len(down_come)], *first)
            down_come.append(swap_ctx(piece, ctxs // 2))
            return down_come[-1]

        grad_act = activate_back(g_all, down, slopes)
        sent = over_reps_first(n2_all, grad_act)
        sent, down_come[-1] = phase(sent, send_down(down))
        parts = by_member(nt(after(grad_act, sent), gate_up).astype(bf16))
        parts, down_come[-1] = phase(parts, send_down(grad_act))
        part_gate_up = over_reps_last(n2_all, after(grad_act, parts), sent)
        part_gate_up, down_come[-1] = phase(part_gate_up, send_down(sent))
        sum_gate_up = owned(part_gate_up)
        far = scatter_far(after(parts, part_gate_up))
        near = scatter_near(parts, far)
        forward = nn(after(act, far), down).astype(bf16)
        near, forward = phase(near, forward)
        grad_middle, a, b = finish_norm_back(
            out_grad, middle, inverse_mid, [(parts, 0), *near], natural, False
        )
        back_of = [None] * TP

        def attend_back_to(members, *grads):
            results = attend_back(
                members,
                orders,
                out,
                kv_pieces,
                [
                    (qt[k], mixed[k], logsum[k], *g, inverse[k], (cosine, k), (sine, k))
                    for k, g in zip(members, grads)
                ],
            )
            for k, back_of[k] in zip(members, results):
                pass

        attend_back_to((0,), (a, b))
        ax, by, ay, bx, back_of[0] = phase(
            swap(a, 1), swap(b, 2), swap(a, 2), swap(b, 1), back_of[0]
        )
        forward = by_member(forward)
        attend_back_to((1, 2), (ax, bx), (ay, by))
        axy, bxy, far, back_of[1], back_of[2] = phase(
            swap(ax, 2), swap(by, 1), scatter_far(forward), back_of[1], back_of[2]
        )
        keys_near = [
            swap_ctx(jnp.stack([back_of[k][3][(j - 1) * count : j * count] for k in range(3)]), j)
            for j in range(1, ctxs)
        ]
        attend_back_to((3,), (axy, bxy))
        keys_near, back_of[3] = phase(keys_near, back_of[3])
        keys_last = [
            swap_ctx(back_of[3][3][None, (j - 1) * count : j * count], j) for j in range(1, ctxs)
        ]
        db_pieces = in_order((a, ax, ay, axy), (b, bx, by, bxy))
        part_out = out_gradient(mixed, after(db_pieces, back_of[3]))
        forward_near = scatter_near(after(forward, keys_near), far)
        keys_last, part_out, forward_near[0], forward_near[2] = phase(
            keys_last, part_out, forward_near[0], forward_near[2]
        )
        grad_proj, scaled_proj = finish_keys(
            [v[2] for v in back_of],
            keys_near,
            keys_last,
            [v[0] for v in back_of],
            [v[1] for v in back_of],
            inverse,
            cosine,
            sine,
        )
        parts = by_member(nt(grad_proj, qkv).astype(bf16))
        parts, down_come[-1], forward_near, sum_gate_up = phase(
            parts, send_down(keys_near), forward_near, sum_gate_up
        )
        across = phase(*halves(parts[3]))
        far_back = swap(across[0], 2), swap(across[1], 1)
        sent = over_reps_first(x_all, after(scaled_proj, across))
        part_qkv = over_reps_last(x_all, after(scaled_proj, sent), sent)
        far_back, part_qkv = phase(far_back, part_qkv)
        sum_qkv = owned(part_qkv)
        near = scatter_near(parts, far_back)
        layer_out = finish_layer(after(middle, far_back), [(forward, 0), *forward_near])
        sum_out = owned(split_reps(after(part_out, far_back)))
        near, layer_out = phase(near, layer_out)
        (input_grad,) = finish_norm_back(
            grad_middle, tokens, inverse[0], [(parts, 0), *near], natural, True
        )
        raw_gate_up = collect(after(sum_gate_up, near), t)
        grad_gate, grad_up, grad_norm_mlp = merge_gate_up(
            after(raw_gate_up, input_grad), w_gate, w_up, gain_mlp
        )
        sum_qkv = after(sum_qkv, near)
        grad_query, grad_key, grad_value, grad_norm_attn = merge_qkv(
            collect(sum_qkv, t), w_query, w_key, w_value, gain_attn
        )
        part_down = half_of(after(part_down, input_grad), ctxs // 2, False).astype(f32)
        part_down = part_down + jnp.concatenate(down_come, axis=1).astype(f32)
        down_come = swap_ctx(
            half_of(part_down.astype(bf16), ctxs // 4, True), ctxs // 4
        )
        down_come = after(down_come, grad_query)
        sum_down = half_of(part_down, ctxs // 4, False) + down_come.astype(f32)
        return (
            layer_out,
            input_grad,
            grad_norm_attn[:, 0],
            grad_query,
            grad_key,
            grad_value,
            after(sum_out, grad_query).astype(f32),
            grad_norm_mlp[:, 0],
            grad_gate,
            grad_up,
            sum_down,
        )

    return body


def solution(mesh):
    sequences, ctxs = mesh.shape["dp"], mesh.shape["ctx"]
    reps = sequences // TP
    names = ("ty", "tx", "rep", "ctx")
    grid = Mesh(mesh.devices.reshape(2, 2, reps, ctxs), names)
    matrix, vector = P(names, None), P(names)
    order = P(("ty", "tx", "rep"), None)
    weights = [vector, matrix, matrix, matrix, matrix, vector, matrix, matrix, matrix]
    return jax.shard_map(
        make_body(reps, ctxs),
        mesh=grid,
        in_specs=(matrix, order, *weights, matrix),
        out_specs=(matrix, matrix, *weights),
        check_vma=False,
    )
```

```python
import jax
import jax.numpy as jnp
from jax import lax
from jax.experimental import pallas as pl
from jax.experimental.pallas import tpu as pltpu
from jax.sharding import Mesh, PartitionSpec as P

H = 32
KV = 4
HD = 64
TP = 4
GROUP = H // KV
LANES = 128
ROWS = 64
ROOM = 60 << 20
ATTEND_ROOM = 60 << 20
DOWN_STEPS = 4

epsilon = 1e-05
rope_base = 10000.0
masked_score = -1e30
bf16 = jnp.bfloat16
f32 = jnp.float32


def after(value, *others):
    return lax.optimization_barrier((value,) + others)[0]


def phase(*values):
    return lax.optimization_barrier(values)


def nn(left, right):
    return lax.dot_general(left, right, (((1,), (0,)), ((), ())), preferred_element_type=f32)


def nt(left, right):
    return lax.dot_general(left, right, (((1,), (1,)), ((), ())), preferred_element_type=f32)


def tn(left, right):
    return lax.dot_general(left, right, (((0,), (0,)), ((), ())), preferred_element_type=f32)


def like(shape, kind):
    return jax.ShapeDtypeStruct(shape, kind)


def size_of(values):
    return sum(v.size * v.dtype.itemsize for v in values)


def small_call(
    kernel, name, inputs, outputs, flops=0, scratch=(), scalars=0, transcendentals=0, room=ROOM
):
    specs, arrays = [pl.BlockSpec(memory_space=pltpu.SMEM)] * scalars, list(inputs[:scalars])
    for v in inputs[scalars:]:
        if isinstance(v, tuple):
            specs.append(row_block(*v))
            arrays.append(v[0])
        else:
            specs.append(whole_block(v.shape))
            arrays.append(v)
    size = size_of((*arrays, *outputs))
    return pl.pallas_call(
        kernel,
        grid=(1,),
        in_specs=specs,
        out_specs=[whole_block(v.shape) for v in outputs],
        out_shape=outputs,
        scratch_shapes=list(scratch),
        compiler_params=pltpu.CompilerParams(vmem_limit_bytes=room),
        cost_estimate=pl.CostEstimate(
            flops=max(flops, size), bytes_accessed=size, transcendentals=transcendentals
        ),
        name=name,
    )(*arrays)


def row_block(array, index):
    shape = array.shape[1:]
    return pl.BlockSpec((None,) + shape, lambda i: (index,) + (0,) * len(shape))


def whole_block(shape):
    return pl.BlockSpec(shape, lambda i: (0,) * len(shape))


def turn(vectors, cosine, sine):
    half = HD // 2
    out = []
    for at in range(0, vectors.shape[0], HD):
        first, second = vectors[at : at + half], vectors[at + half : at + HD]
        out += [first * cosine - second * sine, second * cosine + first * sine]
    return jnp.concatenate(out, axis=0)


def project(pieces, w, cosine, sine):
    half, width = pieces[0].shape
    rows, n, q = 2 * half, w.shape[1], GROUP * HD

    def kernel(*refs):
        x_refs, (w_ref, cos_ref, sin_ref, kv_ref), outs = refs[:8], refs[8:12], refs[12:]
        for k in range(TP):
            xb = jnp.concatenate([x_refs[2 * k][...], x_refs[2 * k + 1][...]], axis=0)
            x = xb.astype(f32)
            inverse = lax.rsqrt(jnp.mean(x * x, axis=1, keepdims=True) + epsilon)
            outs[TP + k][...] = inverse
            flat = (nn(xb, w_ref[...]) * inverse).T
            cosine, sine = cos_ref[k], sin_ref[k]
            outs[k][...] = (turn(flat[:q], cosine, sine) * HD**-0.5).astype(bf16)
            kv = jnp.concatenate([turn(flat[q : q + HD], cosine, sine), flat[q + HD :]], axis=0)
            kv_ref[k] = kv.T.astype(bf16)

    kv, *outs = small_call(
        kernel,
        "project",
        [*pieces, w, cosine, sine],
        [like((TP, rows, 2 * HD), bf16)]
        + [like((q, rows), bf16)] * TP
        + [like((rows, 1), f32)] * TP,
        flops=2 * TP * rows * width * n,
    )
    return outs[:TP], kv, outs[TP:]


def set_bias(order_ref, k, bias_ref):
    keys, rows = bias_ref.shape
    span = keys // order_ref.shape[1]
    lane = lax.broadcasted_iota(jnp.int32, (span, rows), 1)
    query = jnp.where(lane < span, order_ref[k, 0], order_ref[k, 1] - 1) * span + lane
    row = lax.broadcasted_iota(jnp.int32, (span, rows), 0)
    for b in range(keys // span):
        key = order_ref[k, b] * span + row
        bias_ref[b * span : (b + 1) * span, :] = jnp.where(query >= key, 0.0, masked_score)


def attend(members, orders, queries, kv_pieces, wo, kind):
    n, rows = queries[0].shape
    holders, width = len(kv_pieces), wo.shape[1]
    keys, count = holders * rows, len(members)

    def kernel(order_ref, wo_ref, *refs):
        for i, k in enumerate(members):
            qt_ref, *kv_refs = refs[i * (1 + holders) : (i + 1) * (1 + holders)]
            outs = refs[count * (1 + holders) :]
            ot_ref, lse_ref, part_ref = outs[3 * i : 3 * i + 3]
            bias_ref = outs[-1]
            set_bias(order_ref, k, bias_ref)
            kv = jnp.concatenate([ref[...] for ref in kv_refs], axis=0)
            vt = kv.astype(f32).T[HD:].astype(bf16)
            zero = jnp.zeros((HD, rows), bf16)
            for h in range(GROUP):
                at = slice(h * HD, (h + 1) * HD)
                scores = nn(kv, jnp.concatenate([qt_ref[at, :], zero], axis=0)) + bias_ref[...]
                top = jnp.max(scores, axis=0, keepdims=True)
                exponent = jnp.exp(scores - top)
                total = jnp.sum(exponent, axis=0, keepdims=True)
                ot_ref[at, :] = (nn(vt, exponent.astype(bf16)) / total).astype(bf16)
                lse_ref[h : h + 1, :] = top + jnp.log(total)
            part_ref[...] = tn(ot_ref[...], wo_ref[...]).astype(part_ref.dtype)

    inputs, outputs = [orders, wo], []
    for i, k in enumerate(members):
        inputs += [queries[i], *[(piece, k) for piece in kv_pieces]]
        outputs += [like((n, rows), bf16), like((GROUP, rows), f32), like((rows, width), kind)]
    results = small_call(
        kernel,
        "attend",
        inputs,
        outputs,
        flops=2 * rows * n * (keys * 2 * 4 + width) * count,
        scratch=[pltpu.VMEM((keys, rows), f32)],
        scalars=1,
        transcendentals=GROUP * rows * keys * count,
        room=ATTEND_ROOM,
    )
    return [results[3 * i : 3 * i + 3] for i in range(count)]


def attend_back(members, orders, wo, kv_pieces, details):
    n, rows = details[0][0].shape
    holders, width = len(kv_pieces), wo.shape[1]
    keys, half, count = holders * rows, rows // 2, len(members)
    step = 8 + holders

    def kernel(order_ref, wo_ref, *refs):
        outs, (bias_ref, dat_ref, dqt_ref, dkv_ref) = refs[count * step : -4], refs[-4:]
        for i, k in enumerate(members):
            own = refs[i * step : (i + 1) * step]
            kv_refs, (qt_ref, ot_ref, lse_ref, a_ref, b_ref) = own[:holders], own[holders:-3]
            inv_ref, cos_ref, sin_ref = own[-3:]
            dq_ref, dqs_ref, own_ref, far_ref = outs[4 * i : 4 * i + 4]
            set_bias(order_ref, k, bias_ref)
            kv = jnp.concatenate([ref[...] for ref in kv_refs], axis=0)
            kt = kv.astype(f32).T[:HD].astype(bf16)
            zero = jnp.zeros((HD, rows), bf16)
            dat_ref[:, :half] = nt(wo_ref[...], a_ref[...]).astype(bf16)
            dat_ref[:, half:] = nt(wo_ref[...], b_ref[...]).astype(bf16)
            for h in range(GROUP):
                at = slice(h * HD, (h + 1) * HD)
                q_low = jnp.concatenate([qt_ref[at, :], zero], axis=0)
                da_high = jnp.concatenate([zero, dat_ref[at, :]], axis=0)
                weights = jnp.exp(nn(kv, q_low) + bias_ref[...] - lse_ref[h : h + 1, :])
                delta = jnp.sum(
                    dat_ref[at, :].astype(f32) * ot_ref[at, :].astype(f32), axis=0, keepdims=True
                )
                ds = (weights * (nn(kv, da_high) - delta)).astype(bf16)
                dkv = nt(ds, q_low) + nt(weights.astype(bf16), da_high)
                if h == 0:
                    dkv_ref[...] = dkv
                else:
                    dkv_ref[...] += dkv
                dqt_ref[at, :] = nn(kt, ds)
            dq = (turn(dqt_ref[...], cos_ref[...], -sin_ref[...]) * HD**-0.5).T
            dq_ref[...] = dq.astype(bf16)
            dqs_ref[...] = (dq * inv_ref[...]).astype(bf16)
            own_ref[...] = dkv_ref[:rows, :]
            far_ref[...] = dkv_ref[rows:, :].astype(bf16)

    inputs, outputs = [orders, wo], []
    for k, detail in zip(members, details):
        inputs += [*[(piece, k) for piece in kv_pieces], *detail]
        outputs += [
            like((rows, n), bf16),
            like((rows, n), bf16),
            like((rows, 2 * HD), f32),
            like((keys - rows, 2 * HD), bf16),
        ]
    results = small_call(
        kernel,
        "attend_back",
        inputs,
        outputs,
        flops=2 * rows * n * (keys * 5 * 4 + width) * count,
        scratch=[
            pltpu.VMEM((keys, rows), f32),
            pltpu.VMEM((n, rows), bf16),
            pltpu.VMEM((n, rows), f32),
            pltpu.VMEM((keys, 2 * HD), f32),
        ],
        scalars=1,
        transcendentals=GROUP * rows * keys * count,
        room=ATTEND_ROOM,
    )
    return [results[4 * i : 4 * i + 4] for i in range(count)]


def out_gradient(mixed, grads, parts, index, come=None):
    n, width = mixed[0].shape[0] // parts, grads[0].shape[1]

    def kernel(index_ref, *refs):
        at = pl.ds(pl.multiple_of(index_ref[0] * n, n), n)
        total = 0.0 if come is None else refs[3 * TP][...].astype(f32)
        for k in range(TP):
            db = jnp.concatenate([refs[TP + 2 * k][...], refs[TP + 2 * k + 1][...]], axis=0)
            total = total + nn(refs[k][at, :], db)
        refs[-1][...] = total.astype(bf16)

    return small_call(
        kernel,
        "out_gradient",
        [index[None], *mixed, *grads] + ([] if come is None else [come]),
        [like((n, width), bf16)],
        flops=2 * TP * mixed[0].shape[1] * n * width,
        scalars=1,
    )[0]


def finish_keys(own, near, last, dq, dqs, inverse, cosine, sine):
    rows, n = dq[0].shape

    def kernel(*refs):
        own_refs, refs = refs[:TP], refs[TP:]
        near_refs, refs = refs[: len(near)], refs[len(near) :]
        last_refs, refs = refs[: len(last)], refs[len(last) :]
        dq_refs, dqs_refs, refs = refs[:TP], refs[TP : 2 * TP], refs[2 * TP :]
        inv_refs, (cos_ref, sin_ref, plain_ref, scaled_ref) = refs[:TP], refs[TP:]
        for k in range(TP):
            total = own_refs[k][...]
            for ref in near_refs if k < TP - 1 else last_refs:
                total = total + ref[k % (TP - 1)].astype(f32)
            total = total.T
            keys = turn(total[:HD], cos_ref[k], -sin_ref[k])
            total = jnp.concatenate([keys, total[HD:]], axis=0).T
            at = slice(k * rows, (k + 1) * rows)
            plain_ref[at, :n] = dq_refs[k][...]
            plain_ref[at, n:] = total.astype(bf16)
            scaled_ref[at, :n] = dqs_refs[k][...]
            scaled_ref[at, n:] = (total * inv_refs[k][...]).astype(bf16)

    shape = like((TP * rows, n + 2 * HD), bf16)
    return small_call(
        kernel,
        "finish_keys",
        [*own, *near, *last, *dq, *dqs, *inverse, cosine, sine],
        [shape, shape],
    )


def join_rows(pieces):
    rows, width = pieces[0].shape

    def kernel(*refs):
        for i, ref in enumerate(refs[:-1]):
            refs[-1][i * rows : (i + 1) * rows, :] = ref[...]

    return small_call(
        kernel, "join_rows", pieces, [like((len(pieces) * rows, width), pieces[0].dtype)]
    )[0]


def reorder_lanes(v, ordered):
    order, size = ordered
    return jnp.concatenate([v[:, i * size : (i + 1) * size] for i in order], axis=1)


def block_orders(width, holders):
    held = [m * holders + h for h in range(holders) for m in range(TP)]
    natural = [held.index(i) for i in range(len(held))]
    size = width // len(held)
    return (held, size), (natural, size)


def hold_tokens(tokens, held):
    half = tokens.shape[0] // 2

    def kernel(x_ref, a_ref, b_ref):
        a_ref[...] = reorder_lanes(x_ref[:half, :].astype(f32), held).astype(bf16)
        b_ref[...] = reorder_lanes(x_ref[half:, :].astype(f32), held).astype(bf16)

    shape = like((half, tokens.shape[1]), bf16)
    return small_call(kernel, "hold_tokens", [tokens], [shape, shape])


def summed(refs, at, half):
    own_ref, a2_ref, a1_ref, b1_ref, b2_ref = refs
    first, second = (a2_ref, a1_ref) if at < half else (b1_ref, b2_ref)
    come = slice(at % half, at % half + ROWS)
    total = own_ref[at : at + ROWS, :].astype(f32)
    return total + first[come, :].astype(f32) + second[come, :].astype(f32)


def finish_middle(tokens, pieces, held):
    rows, width = tokens.shape
    half = rows // 2

    def kernel(x_ref, *refs):
        sums, (mid_ref, inv_ref, a_ref, b_ref) = refs[:5], refs[5:]
        for at in range(0, rows, ROWS):
            here = slice(at, at + ROWS)
            middle = x_ref[here, :].astype(f32) + summed(sums, at, half)
            inverse = lax.rsqrt(jnp.mean(middle * middle, axis=1, keepdims=True) + epsilon)
            mid_ref[here, :] = middle
            inv_ref[here, :] = inverse
            out = a_ref if at < half else b_ref
            come = slice(at % half, at % half + ROWS)
            out[come, :] = reorder_lanes(middle * inverse, held).astype(bf16)

    return small_call(
        kernel,
        "finish_middle",
        [tokens, *pieces],
        [
            like((rows, width), f32),
            like((rows, 1), f32),
            like((half, width), bf16),
            like((half, width), bf16),
        ],
    )


def finish_norm_back(grad, normed_from, inverse, pieces, natural, last):
    rows, width = grad.shape
    half = rows // 2

    def kernel(g_ref, x_ref, inv_ref, *refs):
        sums, outs = refs[:5], refs[5:]
        for at in range(0, rows, ROWS):
            here = slice(at, at + ROWS)
            scaled = reorder_lanes(summed(sums, at, half), natural)
            inverse = inv_ref[here, :]
            normed = x_ref[here, :].astype(f32) * inverse
            mean = jnp.mean(scaled * normed, axis=1, keepdims=True)
            total = g_ref[here, :].astype(f32) + inverse * (scaled - normed * mean)
            outs[0][here, :] = total
            if not last:
                out = outs[1] if at < half else outs[2]
                out[at % half : at % half + ROWS, :] = total.astype(bf16)

    shapes = [like((rows, width), f32)]
    if not last:
        shapes += [like((half, width), bf16)] * 2
    return small_call(
        kernel, "finish_norm_back", [grad, normed_from, inverse, *pieces], shapes
    )


def finish_layer(middle, pieces):
    rows, width = middle.shape

    def kernel(mid_ref, *refs):
        for at in range(0, rows, ROWS):
            here = slice(at, at + ROWS)
            total = mid_ref[here, :] + summed(refs[:5], at, rows // 2)
            refs[5][here, :] = total.astype(bf16)

    return small_call(
        kernel, "finish_layer", [middle, *pieces], [like((rows, width), bf16)]
    )[0]


def interleaved(i):
    return slice(2 * i * LANES, (2 * i + 1) * LANES), slice((2 * i + 1) * LANES, (2 * i + 2) * LANES)


def activate(pieces, gate_up, tile=256):
    half, width = pieces[0].shape
    total, ff = half * len(pieces), gate_up.shape[1] // 2

    def kernel(*refs):
        n_refs, (w_ref, m_ref, slope_ref, n2_ref) = refs[: len(pieces)], refs[len(pieces) :]

        @pl.when(pl.program_id(0) == 0)
        def _():
            for i, ref in enumerate(n_refs):
                n2_ref[i * half : (i + 1) * half, :] = ref[...]

        both = nn(n2_ref[...], w_ref[...])
        for i in range(tile // LANES):
            gate_at, up_at = interleaved(i)
            gate, up = both[:, gate_at], both[:, up_at]
            sigmoid = jax.nn.sigmoid(gate)
            silu = gate * sigmoid
            m_ref[:, i * LANES : (i + 1) * LANES] = (silu * up).astype(bf16)
            slope_ref[:, gate_at] = (up * (sigmoid + silu * (1.0 - sigmoid))).astype(bf16)
            slope_ref[:, up_at] = silu.astype(bf16)

    return pl.pallas_call(
        kernel,
        grid=(pl.cdiv(ff, tile),),
        in_specs=[whole_block(v.shape) for v in pieces]
        + [pl.BlockSpec((width, 2 * tile), lambda j: (0, j))],
        out_specs=[
            pl.BlockSpec((total, tile), lambda j: (0, j)),
            pl.BlockSpec((total, 2 * tile), lambda j: (0, j)),
        ],
        out_shape=[like((total, ff), bf16), like((total, 2 * ff), bf16)],
        scratch_shapes=[pltpu.VMEM((total, width), bf16)],
        compiler_params=pltpu.CompilerParams(vmem_limit_bytes=ROOM),
        cost_estimate=pl.CostEstimate(
            flops=4 * total * width * ff,
            bytes_accessed=2 * (total * width + 2 * width * ff + 3 * total * ff),
            transcendentals=total * ff,
        ),
        name="activate",
    )(*pieces, gate_up)


def activate_back(g, down, slopes, tile=256):
    total, width = g.shape
    ff = down.shape[0]

    def kernel(g_ref, down_ref, slope_ref, d_ref):
        dm = nt(g_ref[...], down_ref[...])
        for i in range(tile // LANES):
            part = dm[:, i * LANES : (i + 1) * LANES]
            for at in interleaved(i):
                d_ref[:, at] = (part * slope_ref[:, at].astype(f32)).astype(bf16)

    return pl.pallas_call(
        kernel,
        grid=(pl.cdiv(ff, tile),),
        in_specs=[
            pl.BlockSpec((total, width), lambda j: (0, 0)),
            pl.BlockSpec((tile, width), lambda j: (j, 0)),
            pl.BlockSpec((total, 2 * tile), lambda j: (0, j)),
        ],
        out_specs=pl.BlockSpec((total, 2 * tile), lambda j: (0, j)),
        out_shape=like((total, 2 * ff), bf16),
        compiler_params=pltpu.CompilerParams(vmem_limit_bytes=ROOM),
        cost_estimate=pl.CostEstimate(
            flops=2 * total * width * ff,
            bytes_accessed=2 * (total * width + width * ff + 4 * total * ff),
            transcendentals=0,
        ),
        name="activate_back",
    )(g, down, slopes)


def weight_grad(left, right, index, come=None):
    total, width = left.shape
    n = right.shape[1]
    rows, columns = width // 4, n // 2 if n % (2 * LANES) == 0 else n

    def kernel(index_ref, left_ref, right_ref, *refs):
        part = tn(left_ref[...], right_ref[...])
        if come is not None:
            part = part + refs[0][...].astype(f32)
        refs[-1][...] = part.astype(bf16)

    out = pl.BlockSpec((rows, columns), lambda i, j, index: (i, j))
    more = [] if come is None else [come]
    return pl.pallas_call(
        kernel,
        grid_spec=pltpu.PrefetchScalarGridSpec(
            num_scalar_prefetch=1,
            grid=(2, n // columns),
            in_specs=[
                pl.BlockSpec((total, rows), lambda i, j, index: (0, 2 * index[0] + i)),
                pl.BlockSpec((total, columns), lambda i, j, index: (0, j)),
            ]
            + [out] * len(more),
            out_specs=out,
        ),
        out_shape=like((width // 2, n), bf16),
        compiler_params=pltpu.CompilerParams(vmem_limit_bytes=ROOM),
        cost_estimate=pl.CostEstimate(
            flops=total * width * n,
            bytes_accessed=total * width + 2 * total * n + 2 * width * n,
            transcendentals=0,
        ),
        name="weight_grad",
    )(index[None], left, right, *more)


def split_qkv(w_query, w_key, w_value, gain):
    own, n = w_query.shape[0], GROUP * HD

    def kernel(q_ref, k_ref, v_ref, gain_ref, out_ref):
        for g in range(TP):
            parts = [ref[:, g * HD : (g + 1) * HD].astype(f32) for ref in (k_ref, v_ref)]
            query = q_ref[:, g * n : (g + 1) * n].astype(f32)
            out_ref[g, :, :n] = (query * gain_ref[...]).astype(bf16)
            out_ref[g, :, n:] = (jnp.concatenate(parts, axis=1) * gain_ref[...]).astype(bf16)

    return small_call(
        kernel,
        "split_qkv",
        [w_query, w_key, w_value, gain],
        [like((TP, own, n + 2 * HD), bf16)],
    )[0]


def merge_qkv(t, pieces, w_query, w_key, w_value, gain):
    own, n = w_query.shape[0], GROUP * HD

    def kernel(t_ref, *refs):
        in_refs, (q_ref, k_ref, v_ref, gain_ref, dq_ref, dk_ref, dv_ref, dgain_ref) = (
            refs[:TP],
            refs[TP:],
        )
        slot = lax.broadcasted_iota(jnp.int32, (own, TP * HD), 1) // HD
        dgain = jnp.zeros((own, 1), f32)
        keys, values = 0.0, 0.0
        for k, ref in enumerate(in_refs):
            group = t_ref[0] ^ k
            here = pl.ds(pl.multiple_of(group * n, n), n)
            part = ref[:, :n].astype(f32)
            dgain += jnp.sum(part * q_ref[:, here].astype(f32), axis=1, keepdims=True)
            dq_ref[:, here] = part * gain_ref[...]
            part = ref[:, n:].astype(f32)
            mine = slot == group
            keys += jnp.where(mine, jnp.concatenate([part[:, :HD]] * TP, axis=1), 0.0)
            values += jnp.where(mine, jnp.concatenate([part[:, HD:]] * TP, axis=1), 0.0)
        for part, ref, out_ref in ((keys, k_ref, dk_ref), (values, v_ref, dv_ref)):
            dgain += jnp.sum(part * ref[...].astype(f32), axis=1, keepdims=True)
            out_ref[...] = part * gain_ref[...]
        dgain_ref[...] = dgain.T

    return small_call(
        kernel,
        "merge_qkv",
        [t[None], *pieces, w_query, w_key, w_value, gain],
        [like(w.shape, f32) for w in (w_query, w_key, w_value)] + [like((1, own), f32)],
        scalars=1,
    )


def split_gate_up(w_gate, w_up, gain):
    own, total = w_gate.shape
    ff = total // TP

    def kernel(gate_ref, up_ref, gain_ref, out_ref):
        for g in range(TP):
            for j in range(ff // LANES):
                here = slice(g * ff + j * LANES, g * ff + (j + 1) * LANES)
                for ref, at in zip((gate_ref, up_ref), interleaved(j)):
                    out_ref[g, :, at] = (ref[:, here].astype(f32) * gain_ref[...]).astype(bf16)

    return small_call(
        kernel,
        "split_gate_up",
        [w_gate, w_up, gain],
        [jax.ShapeDtypeStruct((TP, own, 2 * ff), bf16)],
    )[0]


def merge_gate_up(t, pieces, w_gate, w_up, gain):
    own, total = w_gate.shape
    ff = total // TP

    def kernel(t_ref, *refs):
        in_refs, (gate_ref, up_ref, gain_ref, dgate_ref, dup_ref, dgain_ref) = refs[:TP], refs[TP:]
        dgain = jnp.zeros((own, LANES), f32)
        for k, in_ref in enumerate(in_refs):
            base = (t_ref[0] ^ k) * ff
            for j in range(ff // LANES):
                here = pl.ds(pl.multiple_of(base + j * LANES, LANES), LANES)
                for ref, out_ref, at in zip(
                    (gate_ref, up_ref), (dgate_ref, dup_ref), interleaved(j)
                ):
                    part = in_ref[:, at].astype(f32)
                    dgain += part * ref[:, here].astype(f32)
                    out_ref[:, here] = part * gain_ref[...]
        dgain_ref[...] = jnp.sum(dgain, axis=1, keepdims=True).T

    return small_call(
        kernel,
        "merge_gate_up",
        [t[None], *pieces, w_gate, w_up, gain],
        [like((own, total), f32), like((own, total), f32), like((1, own), f32)],
        scalars=1,
    )


def make_body(reps, ctxs):
    pair = [(0, 1), (1, 0)]

    def swap(v, k):
        if k == 0:
            return v
        if k == 1:
            return lax.ppermute(v, "tx", pair)
        if k == 2:
            return lax.ppermute(v, "ty", pair)
        return lax.ppermute(v, ("ty", "tx"), [(i, i ^ 3) for i in range(TP)])

    def swap_ctx(v, j):
        return lax.ppermute(v, "ctx", [(i, i ^ j) for i in range(ctxs)]) if j else v

    def halves(v):
        half = v.shape[0] // 2
        return v[:half], v[half:]

    def in_order(a, b):
        return [p for k in range(TP) for p in (a[k], b[k])]

    def gather(a, b):
        ax, by = swap(a, 1), swap(b, 2)
        ay, bx = swap(a, 2), swap(b, 1)
        return in_order((a, ax, ay, swap(ax, 2)), (b, bx, by, swap(by, 1)))

    def scatter_far(parts):
        a, b = halves(parts[3])
        return swap(a, 2), swap(b, 1)

    def scatter_near(parts, far):
        a1, b1 = halves(parts[1])
        a2, b2 = halves(parts[2])
        a1 = (a1.astype(f32) + far[0].astype(f32)).astype(bf16)
        b2 = (b2.astype(f32) + far[1].astype(f32)).astype(bf16)
        return [swap(a2, 2), swap(a1, 1), swap(b1, 1), swap(b2, 2)]

    def by_member(v):
        return v.reshape(TP, -1, v.shape[1])

    def exchange(blocks, t, *first):
        out = jnp.zeros_like(blocks)
        for k in range(TP):
            come = swap(lax.dynamic_index_in_dim(blocks, t ^ k, 0, keepdims=True), k)
            come = after(come, *first) if first else come
            out = lax.dynamic_update_slice_in_dim(out, come, t ^ k, 0)
        return out

    def spread(blocks, t, *first):
        return exchange(blocks, t, *first).reshape(-1, blocks.shape[2])

    def collect(summed_rows, t):
        blocks = summed_rows.reshape(TP, -1, summed_rows.shape[1])
        return [swap(lax.dynamic_index_in_dim(blocks, t ^ k, 0, False), k) for k in range(TP)]

    def whole(v):
        return lax.all_gather(v, ("rep", "ctx"), axis=0, tiled=True)

    def over_reps_first(left, right):
        if reps != 2:
            return tn(left, right).astype(bf16)
        index = 1 - lax.axis_index("rep")
        half = left.shape[1] // 2
        if half % (2 * LANES) == 0:
            return weight_grad(left, right, index)
        return tn(lax.dynamic_slice_in_dim(left, index * half, half, 1), right).astype(bf16)

    def over_reps_last(left, right, first):
        if reps != 2:
            return lax.psum_scatter(first, "rep", scatter_dimension=0, tiled=True)
        index = lax.axis_index("rep")
        half = left.shape[1] // 2
        come = lax.ppermute(first, "rep", pair)
        if half % (2 * LANES) == 0:
            return weight_grad(left, right, index, come)
        mine = lax.dynamic_slice_in_dim(left, index * half, half, 1)
        return (tn(mine, right) + come.astype(f32)).astype(bf16)

    def over_reps(left, right):
        return over_reps_last(left, right, over_reps_first(left, right))

    def owned(part):
        return lax.psum_scatter(part, "ctx", scatter_dimension=0, tiled=True)

    def half_of(v, j, other):
        index = lax.axis_index("ctx") // j % 2
        v = v.reshape(2, -1, v.shape[1])
        return lax.dynamic_index_in_dim(v, 1 - index if other else index, 0, False)

    def body(
        tokens,
        span_order,
        norm_attn,
        w_query,
        w_key,
        w_value,
        w_out,
        norm_mlp,
        w_gate,
        w_up,
        w_down,
        out_grad,
    ):
        count, width = tokens.shape
        held, natural = block_orders(width, reps * ctxs)
        span = count * ctxs // span_order.shape[1]
        per = count // span
        t = 2 * lax.axis_index("ty") + lax.axis_index("tx")
        c = lax.axis_index("ctx")
        gain_attn = norm_attn.astype(f32)[:, None]
        gain_mlp = norm_mlp.astype(f32)[:, None]

        qkv_blocks = split_qkv(w_query, w_key, w_value, gain_attn)
        a, b = hold_tokens(after(tokens, qkv_blocks), held)
        qkv_mine, a, b = phase(spread(after(qkv_blocks, a), t), a, b)
        qkv = whole(qkv_mine)
        out = whole(after(w_out, qkv_mine))
        ax, by = swap(a, 1), swap(b, 2)
        ax, by, a, b = phase(ax, by, a, b)
        gate_up_blocks = split_gate_up(after(w_gate, ax), w_up, gain_mlp)
        orders = [swap(after(span_order, qkv_mine), k) for k in range(TP)]
        ay, bx, axy, bxy = swap(a, 2), swap(b, 1), swap(ax, 2), swap(by, 1)
        ay, bx, axy, bxy, gate_up_blocks = phase(ay, bx, axy, bxy, gate_up_blocks)
        x_pieces = in_order((a, ax, ay, axy), (b, bx, by, bxy))

        orders = jnp.concatenate(orders, axis=0).reshape(TP, ctxs, per)
        orders = jnp.concatenate(
            [lax.dynamic_slice_in_dim(orders, c ^ j, 1, 1) for j in range(ctxs)], axis=1
        ).reshape(TP, ctxs * per)
        positions = orders[:, :per, None] * span + jnp.arange(span, dtype=jnp.int32)
        half_dim = HD // 2
        frequency = jnp.power(rope_base, -jnp.arange(half_dim, dtype=f32) / half_dim)
        angles = frequency[:, None] * positions.reshape(TP, 1, count).astype(f32)
        cosine, sine = jnp.cos(angles), jnp.sin(angles)

        qt, kv, inverse = project(x_pieces, qkv, cosine, sine)
        gate_up_mine = spread(after(gate_up_blocks, axy, bxy), t, kv)
        kv_far = [swap_ctx(kv, j) for j in range(1, ctxs)]
        ga, gb = halves(after(out_grad, kv))
        kv, kv_far, gate_up_mine, gax, gby, x_all = phase(
            kv, kv_far, gate_up_mine, swap(ga, 1), swap(gb, 2), join_rows(after(x_pieces, kv))
        )
        kv_pieces = [kv, *kv_far]
        gate_up = whole(gate_up_mine)
        down = whole(after(w_down, gate_up_mine))
        mixed, logsum, parts = [None] * TP, [None] * TP, [None] * TP

        def attend_to(members, queries):
            results = attend(
                members,
                orders,
                [queries[k] for k in members],
                kv_pieces,
                out,
                f32 if 0 in members else bf16,
            )
            for k, (mixed[k], logsum[k], parts[k]) in zip(members, results):
                pass

        attend_to((3,), qt)
        queries, gay, gbx = phase(qt, swap(ga, 2), swap(gb, 1), parts[3])[:3]
        far = scatter_far(parts)
        attend_to((2, 1), queries)
        far, parts[1], parts[2], queries, gaxy, gbxy = phase(
            far, parts[1], parts[2], queries, swap(gax, 2), swap(gby, 1)
        )
        near = scatter_near(parts, far)
        attend_to((0,), queries)
        g_all = join_rows(in_order((ga, gax, gay, gaxy), (gb, gbx, gby, gbxy)))
        near, parts[0], g_all = phase(near, parts[0], g_all)
        middle, inverse_mid, a, b = finish_middle(tokens, [parts[0], *near], held)
        n2_pieces = gather(a, b)

        act, slopes = activate(n2_pieces, gate_up)
        n2_all = join_rows(after(n2_pieces, act))
        part_down = over_reps(act, g_all)
        slopes, part_down, n2_all = phase(slopes, part_down, n2_all)
        down_sent = jnp.split(half_of(part_down, ctxs // 2, True), DOWN_STEPS, axis=1)
        down_come = []

        def send_down(*first):
            piece = after(down_sent[len(down_come)], *first)
            down_come.append(swap_ctx(piece, ctxs // 2))
            return down_come[-1]

        grad_act = activate_back(g_all, down, slopes)
        sent = over_reps_first(n2_all, grad_act)
        sent, down_come[-1] = phase(sent, send_down(down))
        parts = by_member(nt(after(grad_act, sent), gate_up).astype(bf16))
        parts, down_come[-1] = phase(parts, send_down(grad_act))
        far = scatter_far(parts)
        part_gate_up = over_reps_last(n2_all, after(grad_act, parts), sent)
        far, part_gate_up, down_come[-1] = phase(far, part_gate_up, send_down(sent))
        sum_gate_up = owned(part_gate_up)
        near = scatter_near(parts, far)
        forward = nn(after(act, far), down).astype(bf16)
        near, forward = phase(near, forward)
        grad_middle, a, b = finish_norm_back(
            out_grad, middle, inverse_mid, [(parts, 0), *near], natural, False
        )
        back_of = [None] * TP

        def attend_back_to(members, *grads):
            results = attend_back(
                members,
                orders,
                out,
                kv_pieces,
                [
                    (qt[k], mixed[k], logsum[k], *g, inverse[k], (cosine, k), (sine, k))
                    for k, g in zip(members, grads)
                ],
            )
            for k, back_of[k] in zip(members, results):
                pass

        attend_back_to((0,), (a, b))
        ax, by, ay, bx, back_of[0] = phase(
            swap(a, 1), swap(b, 2), swap(a, 2), swap(b, 1), back_of[0]
        )
        forward = by_member(forward)
        attend_back_to((1, 2), (ax, bx), (ay, by))
        axy, bxy, far, back_of[1], back_of[2] = phase(
            swap(ax, 2), swap(by, 1), scatter_far(forward), back_of[1], back_of[2]
        )
        keys_near = [
            swap_ctx(jnp.stack([back_of[k][3][(j - 1) * count : j * count] for k in range(3)]), j)
            for j in range(1, ctxs)
        ]
        db_pieces = in_order((a, ax, ay, axy), (b, bx, by, bxy))
        r = lax.axis_index("rep")
        if reps == 2:
            part_out = out_gradient(mixed, db_pieces, 2, 1 - r)
            part_out, axy, bxy = phase(part_out, axy, bxy)
            part_out = lax.ppermute(part_out, "rep", pair)
        attend_back_to((3,), (axy, bxy))
        keys_near, back_of[3] = phase(keys_near, back_of[3])
        keys_last = [
            swap_ctx(back_of[3][3][None, (j - 1) * count : j * count], j) for j in range(1, ctxs)
        ]
        db_pieces = after(db_pieces, back_of[3])
        if reps == 2:
            part_out = out_gradient(mixed, db_pieces, 2, r, part_out)
        else:
            part_out = out_gradient(mixed, db_pieces, 1, jnp.zeros((), jnp.int32))
            part_out = lax.psum_scatter(part_out, "rep", scatter_dimension=0, tiled=True)
        forward_near = scatter_near(after(forward, keys_near), far)
        keys_last, part_out, forward_near[0], forward_near[2] = phase(
            keys_last, part_out, forward_near[0], forward_near[2]
        )
        grad_proj, scaled_proj = finish_keys(
            [v[2] for v in back_of],
            keys_near,
            keys_last,
            [v[0] for v in back_of],
            [v[1] for v in back_of],
            inverse,
            cosine,
            sine,
        )
        parts = by_member(nt(grad_proj, qkv).astype(bf16))
        parts, down_come[-1], forward_near, sum_gate_up = phase(
            parts, send_down(keys_near), forward_near, sum_gate_up
        )
        across = phase(*halves(parts[3]))
        far_back = swap(across[0], 2), swap(across[1], 1)
        sent = over_reps_first(x_all, after(scaled_proj, across))
        part_qkv = over_reps_last(x_all, after(scaled_proj, sent), sent)
        sum_out = owned(after(part_out, across))
        far_back, part_qkv, sum_out = phase(far_back, part_qkv, sum_out)
        sum_qkv = owned(part_qkv)
        near = scatter_near(parts, far_back)
        layer_out = finish_layer(after(middle, far_back), [(forward, 0), *forward_near])
        raw_gate_up = collect(after(sum_gate_up, far_back), t)
        part_down = half_of(after(part_down, far_back), ctxs // 2, False).astype(f32)
        part_down = part_down + jnp.concatenate(down_come, axis=1).astype(f32)
        near, layer_out, part_down = phase(near, layer_out, part_down)
        (input_grad,) = finish_norm_back(
            grad_middle, tokens, inverse[0], [(parts, 0), *near], natural, True
        )
        grad_gate, grad_up, grad_norm_mlp = merge_gate_up(
            t, after(raw_gate_up, near), w_gate, w_up, gain_mlp
        )
        sum_qkv = after(sum_qkv, input_grad)
        grad_query, grad_key, grad_value, grad_norm_attn = merge_qkv(
            t, collect(sum_qkv, t), w_query, w_key, w_value, gain_attn
        )
        down_come = swap_ctx(
            half_of(part_down.astype(bf16), ctxs // 4, True), ctxs // 4
        )
        down_come = after(down_come, grad_query)
        sum_down = half_of(part_down, ctxs // 4, False) + down_come.astype(f32)
        return (
            layer_out,
            input_grad,
            grad_norm_attn[0],
            grad_query,
            grad_key,
            grad_value,
            after(sum_out, grad_query).astype(f32),
            grad_norm_mlp[0],
            grad_gate,
            grad_up,
            sum_down,
        )

    return body


def solution(mesh):
    sequences, ctxs = mesh.shape["dp"], mesh.shape["ctx"]
    reps = sequences // TP
    names = ("ty", "tx", "rep", "ctx")
    grid = Mesh(mesh.devices.reshape(2, 2, reps, ctxs), names)
    matrix, vector = P(names, None), P(names)
    order = P(("ty", "tx", "rep"), None)
    weights = [vector, matrix, matrix, matrix, matrix, vector, matrix, matrix, matrix]
    return jax.shard_map(
        make_body(reps, ctxs),
        mesh=grid,
        in_specs=(matrix, order, *weights, matrix),
        out_specs=(matrix, matrix, *weights),
        check_vma=False,
    )
```

```python
import jax
import jax.numpy as jnp
from jax import lax
from jax.experimental import pallas as pl
from jax.experimental.pallas import tpu as pltpu
from jax.sharding import Mesh, PartitionSpec as P

H = 32
KV = 4
HD = 64
TP = 4
GROUP = H // KV
LANES = 128
ROWS = 64
ROOM = 60 << 20
ATTEND_ROOM = 60 << 20
DOWN_STEPS = 4

epsilon = 1e-05
rope_base = 10000.0
masked_score = -1e30
bf16 = jnp.bfloat16
f32 = jnp.float32


def after(value, *others):
    return lax.optimization_barrier((value,) + others)[0]


def phase(*values):
    return lax.optimization_barrier(values)


def nn(left, right):
    return lax.dot_general(left, right, (((1,), (0,)), ((), ())), preferred_element_type=f32)


def nt(left, right):
    return lax.dot_general(left, right, (((1,), (1,)), ((), ())), preferred_element_type=f32)


def tn(left, right):
    return lax.dot_general(left, right, (((0,), (0,)), ((), ())), preferred_element_type=f32)


def like(shape, kind):
    return jax.ShapeDtypeStruct(shape, kind)


def size_of(values):
    return sum(v.size * v.dtype.itemsize for v in values)


def small_call(
    kernel, name, inputs, outputs, flops=0, scratch=(), scalars=0, transcendentals=0, room=ROOM
):
    specs, arrays = [pl.BlockSpec(memory_space=pltpu.SMEM)] * scalars, list(inputs[:scalars])
    for v in inputs[scalars:]:
        if isinstance(v, tuple):
            specs.append(row_block(*v))
            arrays.append(v[0])
        else:
            specs.append(whole_block(v.shape))
            arrays.append(v)
    size = size_of((*arrays, *outputs))
    return pl.pallas_call(
        kernel,
        grid=(1,),
        in_specs=specs,
        out_specs=[whole_block(v.shape) for v in outputs],
        out_shape=outputs,
        scratch_shapes=list(scratch),
        compiler_params=pltpu.CompilerParams(vmem_limit_bytes=room),
        cost_estimate=pl.CostEstimate(
            flops=max(flops, size), bytes_accessed=size, transcendentals=transcendentals
        ),
        name=name,
    )(*arrays)


def row_block(array, index):
    shape = array.shape[1:]
    return pl.BlockSpec((None,) + shape, lambda i: (index,) + (0,) * len(shape))


def whole_block(shape):
    return pl.BlockSpec(shape, lambda i: (0,) * len(shape))


def turn(vectors, cosine, sine):
    half = HD // 2
    out = []
    for at in range(0, vectors.shape[0], HD):
        first, second = vectors[at : at + half], vectors[at + half : at + HD]
        out += [first * cosine - second * sine, second * cosine + first * sine]
    return jnp.concatenate(out, axis=0)


def project(pieces, w, cosine, sine):
    half, width = pieces[0].shape
    rows, n, q = 2 * half, w.shape[1], GROUP * HD

    def kernel(*refs):
        x_refs, (w_ref, cos_ref, sin_ref, kv_ref), outs = refs[:8], refs[8:12], refs[12:]
        for k in range(TP):
            xb = jnp.concatenate([x_refs[2 * k][...], x_refs[2 * k + 1][...]], axis=0)
            x = xb.astype(f32)
            inverse = lax.rsqrt(jnp.mean(x * x, axis=1, keepdims=True) + epsilon)
            outs[TP + k][...] = inverse
            flat = (nn(xb, w_ref[...]) * inverse).T
            cosine, sine = cos_ref[k], sin_ref[k]
            outs[k][...] = (turn(flat[:q], cosine, sine) * HD**-0.5).astype(bf16)
            kv = jnp.concatenate([turn(flat[q : q + HD], cosine, sine), flat[q + HD :]], axis=0)
            kv_ref[k] = kv.T.astype(bf16)

    kv, *outs = small_call(
        kernel,
        "project",
        [*pieces, w, cosine, sine],
        [like((TP, rows, 2 * HD), bf16)]
        + [like((q, rows), bf16)] * TP
        + [like((rows, 1), f32)] * TP,
        flops=2 * TP * rows * width * n,
    )
    return outs[:TP], kv, outs[TP:]


def set_bias(order_ref, k, bias_ref):
    keys, rows = bias_ref.shape
    span = keys // order_ref.shape[1]
    lane = lax.broadcasted_iota(jnp.int32, (span, rows), 1)
    query = jnp.where(lane < span, order_ref[k, 0], order_ref[k, 1] - 1) * span + lane
    row = lax.broadcasted_iota(jnp.int32, (span, rows), 0)
    for b in range(keys // span):
        key = order_ref[k, b] * span + row
        bias_ref[b * span : (b + 1) * span, :] = jnp.where(query >= key, 0.0, masked_score)


def attend(members, orders, queries, kv_pieces, wo, kind):
    n, rows = queries[0].shape
    holders, width = len(kv_pieces), wo.shape[1]
    keys, count = holders * rows, len(members)

    def kernel(order_ref, wo_ref, *refs):
        for i, k in enumerate(members):
            qt_ref, *kv_refs = refs[i * (1 + holders) : (i + 1) * (1 + holders)]
            outs = refs[count * (1 + holders) :]
            ot_ref, lse_ref, part_ref = outs[3 * i : 3 * i + 3]
            bias_ref = outs[-1]
            set_bias(order_ref, k, bias_ref)
            kv = jnp.concatenate([ref[...] for ref in kv_refs], axis=0)
            vt = kv.astype(f32).T[HD:].astype(bf16)
            zero = jnp.zeros((HD, rows), bf16)
            for h in range(GROUP):
                at = slice(h * HD, (h + 1) * HD)
                scores = nn(kv, jnp.concatenate([qt_ref[at, :], zero], axis=0)) + bias_ref[...]
                top = jnp.max(scores, axis=0, keepdims=True)
                exponent = jnp.exp(scores - top)
                total = jnp.sum(exponent, axis=0, keepdims=True)
                ot_ref[at, :] = (nn(vt, exponent.astype(bf16)) / total).astype(bf16)
                lse_ref[h : h + 1, :] = top + jnp.log(total)
            part_ref[...] = tn(ot_ref[...], wo_ref[...]).astype(part_ref.dtype)

    inputs, outputs = [orders, wo], []
    for i, k in enumerate(members):
        inputs += [queries[i], *[(piece, k) for piece in kv_pieces]]
        outputs += [like((n, rows), bf16), like((GROUP, rows), f32), like((rows, width), kind)]
    results = small_call(
        kernel,
        "attend",
        inputs,
        outputs,
        flops=2 * rows * n * (keys * 2 * 4 + width) * count,
        scratch=[pltpu.VMEM((keys, rows), f32)],
        scalars=1,
        transcendentals=GROUP * rows * keys * count,
        room=ATTEND_ROOM,
    )
    return [results[3 * i : 3 * i + 3] for i in range(count)]


def attend_back(members, orders, wo, kv_pieces, details):
    n, rows = details[0][0].shape
    holders, width = len(kv_pieces), wo.shape[1]
    keys, half, count = holders * rows, rows // 2, len(members)
    step = 8 + holders

    def kernel(order_ref, wo_ref, *refs):
        outs, (bias_ref, dat_ref, dqt_ref, dkv_ref) = refs[count * step : -4], refs[-4:]
        for i, k in enumerate(members):
            own = refs[i * step : (i + 1) * step]
            kv_refs, (qt_ref, ot_ref, lse_ref, a_ref, b_ref) = own[:holders], own[holders:-3]
            inv_ref, cos_ref, sin_ref = own[-3:]
            dq_ref, dqs_ref, own_ref, far_ref = outs[4 * i : 4 * i + 4]
            set_bias(order_ref, k, bias_ref)
            kv = jnp.concatenate([ref[...] for ref in kv_refs], axis=0)
            kt = kv.astype(f32).T[:HD].astype(bf16)
            zero = jnp.zeros((HD, rows), bf16)
            dat_ref[:, :half] = nt(wo_ref[...], a_ref[...]).astype(bf16)
            dat_ref[:, half:] = nt(wo_ref[...], b_ref[...]).astype(bf16)
            for h in range(GROUP):
                at = slice(h * HD, (h + 1) * HD)
                q_low = jnp.concatenate([qt_ref[at, :], zero], axis=0)
                da_high = jnp.concatenate([zero, dat_ref[at, :]], axis=0)
                weights = jnp.exp(nn(kv, q_low) + bias_ref[...] - lse_ref[h : h + 1, :])
                delta = jnp.sum(
                    dat_ref[at, :].astype(f32) * ot_ref[at, :].astype(f32), axis=0, keepdims=True
                )
                ds = (weights * (nn(kv, da_high) - delta)).astype(bf16)
                dkv = nt(ds, q_low) + nt(weights.astype(bf16), da_high)
                if h == 0:
                    dkv_ref[...] = dkv
                else:
                    dkv_ref[...] += dkv
                dqt_ref[at, :] = nn(kt, ds)
            dq = (turn(dqt_ref[...], cos_ref[...], -sin_ref[...]) * HD**-0.5).T
            dq_ref[...] = dq.astype(bf16)
            dqs_ref[...] = (dq * inv_ref[...]).astype(bf16)
            own_ref[...] = dkv_ref[:rows, :]
            far_ref[...] = dkv_ref[rows:, :].astype(bf16)

    inputs, outputs = [orders, wo], []
    for k, detail in zip(members, details):
        inputs += [*[(piece, k) for piece in kv_pieces], *detail]
        outputs += [
            like((rows, n), bf16),
            like((rows, n), bf16),
            like((rows, 2 * HD), f32),
            like((keys - rows, 2 * HD), bf16),
        ]
    results = small_call(
        kernel,
        "attend_back",
        inputs,
        outputs,
        flops=2 * rows * n * (keys * 5 * 4 + width) * count,
        scratch=[
            pltpu.VMEM((keys, rows), f32),
            pltpu.VMEM((n, rows), bf16),
            pltpu.VMEM((n, rows), f32),
            pltpu.VMEM((keys, 2 * HD), f32),
        ],
        scalars=1,
        transcendentals=GROUP * rows * keys * count,
        room=ATTEND_ROOM,
    )
    return [results[4 * i : 4 * i + 4] for i in range(count)]


def out_gradient(mixed, grads, parts, index, come=None):
    n, width = mixed[0].shape[0] // parts, grads[0].shape[1]

    def kernel(index_ref, *refs):
        at = pl.ds(pl.multiple_of(index_ref[0] * n, n), n)
        total = 0.0 if come is None else refs[3 * TP][...].astype(f32)
        for k in range(TP):
            db = jnp.concatenate([refs[TP + 2 * k][...], refs[TP + 2 * k + 1][...]], axis=0)
            total = total + nn(refs[k][at, :], db)
        refs[-1][...] = total.astype(bf16)

    return small_call(
        kernel,
        "out_gradient",
        [index[None], *mixed, *grads] + ([] if come is None else [come]),
        [like((n, width), bf16)],
        flops=2 * TP * mixed[0].shape[1] * n * width,
        scalars=1,
    )[0]


def finish_keys(own, near, last, dq, dqs, inverse, cosine, sine):
    rows, n = dq[0].shape

    def kernel(*refs):
        own_refs, refs = refs[:TP], refs[TP:]
        near_refs, refs = refs[: len(near)], refs[len(near) :]
        last_refs, refs = refs[: len(last)], refs[len(last) :]
        dq_refs, dqs_refs, refs = refs[:TP], refs[TP : 2 * TP], refs[2 * TP :]
        inv_refs, (cos_ref, sin_ref, plain_ref, scaled_ref) = refs[:TP], refs[TP:]
        for k in range(TP):
            total = own_refs[k][...]
            for ref in near_refs if k < TP - 1 else last_refs:
                total = total + ref[k % (TP - 1)].astype(f32)
            total = total.T
            keys = turn(total[:HD], cos_ref[k], -sin_ref[k])
            total = jnp.concatenate([keys, total[HD:]], axis=0).T
            at = slice(k * rows, (k + 1) * rows)
            plain_ref[at, :n] = dq_refs[k][...]
            plain_ref[at, n:] = total.astype(bf16)
            scaled_ref[at, :n] = dqs_refs[k][...]
            scaled_ref[at, n:] = (total * inv_refs[k][...]).astype(bf16)

    shape = like((TP * rows, n + 2 * HD), bf16)
    return small_call(
        kernel,
        "finish_keys",
        [*own, *near, *last, *dq, *dqs, *inverse, cosine, sine],
        [shape, shape],
    )


def join_rows(pieces):
    rows, width = pieces[0].shape

    def kernel(*refs):
        for i, ref in enumerate(refs[:-1]):
            refs[-1][i * rows : (i + 1) * rows, :] = ref[...]

    return small_call(
        kernel, "join_rows", pieces, [like((len(pieces) * rows, width), pieces[0].dtype)]
    )[0]


def reorder_lanes(v, ordered):
    order, size = ordered
    return jnp.concatenate([v[:, i * size : (i + 1) * size] for i in order], axis=1)


def block_orders(width, holders):
    held = [m * holders + h for h in range(holders) for m in range(TP)]
    natural = [held.index(i) for i in range(len(held))]
    size = width // len(held)
    return (held, size), (natural, size)


def hold_tokens(tokens, held):
    half = tokens.shape[0] // 2

    def kernel(x_ref, a_ref, b_ref):
        a_ref[...] = reorder_lanes(x_ref[:half, :].astype(f32), held).astype(bf16)
        b_ref[...] = reorder_lanes(x_ref[half:, :].astype(f32), held).astype(bf16)

    shape = like((half, tokens.shape[1]), bf16)
    return small_call(kernel, "hold_tokens", [tokens], [shape, shape])


def summed(refs, at, half):
    own_ref, a2_ref, a1_ref, b1_ref, b2_ref = refs
    first, second = (a2_ref, a1_ref) if at < half else (b1_ref, b2_ref)
    come = slice(at % half, at % half + ROWS)
    total = own_ref[at : at + ROWS, :].astype(f32)
    return total + first[come, :].astype(f32) + second[come, :].astype(f32)


def finish_middle(tokens, pieces, held):
    rows, width = tokens.shape
    half = rows // 2

    def kernel(x_ref, *refs):
        sums, (mid_ref, inv_ref, a_ref, b_ref) = refs[:5], refs[5:]
        for at in range(0, rows, ROWS):
            here = slice(at, at + ROWS)
            middle = x_ref[here, :].astype(f32) + summed(sums, at, half)
            inverse = lax.rsqrt(jnp.mean(middle * middle, axis=1, keepdims=True) + epsilon)
            mid_ref[here, :] = middle
            inv_ref[here, :] = inverse
            out = a_ref if at < half else b_ref
            come = slice(at % half, at % half + ROWS)
            out[come, :] = reorder_lanes(middle * inverse, held).astype(bf16)

    return small_call(
        kernel,
        "finish_middle",
        [tokens, *pieces],
        [
            like((rows, width), f32),
            like((rows, 1), f32),
            like((half, width), bf16),
            like((half, width), bf16),
        ],
    )


def finish_norm_back(grad, normed_from, inverse, pieces, natural, last):
    rows, width = grad.shape
    half = rows // 2

    def kernel(g_ref, x_ref, inv_ref, *refs):
        sums, outs = refs[:5], refs[5:]
        for at in range(0, rows, ROWS):
            here = slice(at, at + ROWS)
            scaled = reorder_lanes(summed(sums, at, half), natural)
            inverse = inv_ref[here, :]
            normed = x_ref[here, :].astype(f32) * inverse
            mean = jnp.mean(scaled * normed, axis=1, keepdims=True)
            total = g_ref[here, :].astype(f32) + inverse * (scaled - normed * mean)
            outs[0][here, :] = total
            if not last:
                out = outs[1] if at < half else outs[2]
                out[at % half : at % half + ROWS, :] = total.astype(bf16)

    shapes = [like((rows, width), f32)]
    if not last:
        shapes += [like((half, width), bf16)] * 2
    return small_call(
        kernel, "finish_norm_back", [grad, normed_from, inverse, *pieces], shapes
    )


def finish_layer(middle, pieces):
    rows, width = middle.shape

    def kernel(mid_ref, *refs):
        for at in range(0, rows, ROWS):
            here = slice(at, at + ROWS)
            total = mid_ref[here, :] + summed(refs[:5], at, rows // 2)
            refs[5][here, :] = total.astype(bf16)

    return small_call(
        kernel, "finish_layer", [middle, *pieces], [like((rows, width), bf16)]
    )[0]


def interleaved(i):
    return slice(2 * i * LANES, (2 * i + 1) * LANES), slice((2 * i + 1) * LANES, (2 * i + 2) * LANES)


def activate(pieces, gate_up, tile=256):
    half, width = pieces[0].shape
    total, ff = half * len(pieces), gate_up.shape[1] // 2

    def kernel(*refs):
        n_refs, (w_ref, m_ref, slope_ref, n2_ref) = refs[: len(pieces)], refs[len(pieces) :]

        @pl.when(pl.program_id(0) == 0)
        def _():
            for i, ref in enumerate(n_refs):
                n2_ref[i * half : (i + 1) * half, :] = ref[...]

        both = nn(n2_ref[...], w_ref[...])
        for i in range(tile // LANES):
            gate_at, up_at = interleaved(i)
            gate, up = both[:, gate_at], both[:, up_at]
            sigmoid = jax.nn.sigmoid(gate)
            silu = gate * sigmoid
            m_ref[:, i * LANES : (i + 1) * LANES] = (silu * up).astype(bf16)
            slope_ref[:, gate_at] = (up * (sigmoid + silu * (1.0 - sigmoid))).astype(bf16)
            slope_ref[:, up_at] = silu.astype(bf16)

    return pl.pallas_call(
        kernel,
        grid=(pl.cdiv(ff, tile),),
        in_specs=[whole_block(v.shape) for v in pieces]
        + [pl.BlockSpec((width, 2 * tile), lambda j: (0, j))],
        out_specs=[
            pl.BlockSpec((total, tile), lambda j: (0, j)),
            pl.BlockSpec((total, 2 * tile), lambda j: (0, j)),
        ],
        out_shape=[like((total, ff), bf16), like((total, 2 * ff), bf16)],
        scratch_shapes=[pltpu.VMEM((total, width), bf16)],
        compiler_params=pltpu.CompilerParams(vmem_limit_bytes=ROOM),
        cost_estimate=pl.CostEstimate(
            flops=4 * total * width * ff,
            bytes_accessed=2 * (total * width + 2 * width * ff + 3 * total * ff),
            transcendentals=total * ff,
        ),
        name="activate",
    )(*pieces, gate_up)


def activate_back(g, down, slopes, tile=256):
    total, width = g.shape
    ff = down.shape[0]

    def kernel(g_ref, down_ref, slope_ref, d_ref):
        dm = nt(g_ref[...], down_ref[...])
        for i in range(tile // LANES):
            part = dm[:, i * LANES : (i + 1) * LANES]
            for at in interleaved(i):
                d_ref[:, at] = (part * slope_ref[:, at].astype(f32)).astype(bf16)

    return pl.pallas_call(
        kernel,
        grid=(pl.cdiv(ff, tile),),
        in_specs=[
            pl.BlockSpec((total, width), lambda j: (0, 0)),
            pl.BlockSpec((tile, width), lambda j: (j, 0)),
            pl.BlockSpec((total, 2 * tile), lambda j: (0, j)),
        ],
        out_specs=pl.BlockSpec((total, 2 * tile), lambda j: (0, j)),
        out_shape=like((total, 2 * ff), bf16),
        compiler_params=pltpu.CompilerParams(vmem_limit_bytes=ROOM),
        cost_estimate=pl.CostEstimate(
            flops=2 * total * width * ff,
            bytes_accessed=2 * (total * width + width * ff + 4 * total * ff),
            transcendentals=0,
        ),
        name="activate_back",
    )(g, down, slopes)


def weight_grad(left, right, index, come=None):
    total, width = left.shape
    n = right.shape[1]
    rows, columns = width // 4, n // 2 if n % (2 * LANES) == 0 else n

    def kernel(index_ref, left_ref, right_ref, *refs):
        part = tn(left_ref[...], right_ref[...])
        if come is not None:
            part = part + refs[0][...].astype(f32)
        refs[-1][...] = part.astype(bf16)

    out = pl.BlockSpec((rows, columns), lambda i, j, index: (i, j))
    more = [] if come is None else [come]
    return pl.pallas_call(
        kernel,
        grid_spec=pltpu.PrefetchScalarGridSpec(
            num_scalar_prefetch=1,
            grid=(2, n // columns),
            in_specs=[
                pl.BlockSpec((total, rows), lambda i, j, index: (0, 2 * index[0] + i)),
                pl.BlockSpec((total, columns), lambda i, j, index: (0, j)),
            ]
            + [out] * len(more),
            out_specs=out,
        ),
        out_shape=like((width // 2, n), bf16),
        compiler_params=pltpu.CompilerParams(vmem_limit_bytes=ROOM),
        cost_estimate=pl.CostEstimate(
            flops=total * width * n,
            bytes_accessed=total * width + 2 * total * n + 2 * width * n,
            transcendentals=0,
        ),
        name="weight_grad",
    )(index[None], left, right, *more)


def split_qkv(w_query, w_key, w_value, gain):
    own, n = w_query.shape[0], GROUP * HD

    def kernel(q_ref, k_ref, v_ref, gain_ref, out_ref):
        for g in range(TP):
            parts = [ref[:, g * HD : (g + 1) * HD].astype(f32) for ref in (k_ref, v_ref)]
            query = q_ref[:, g * n : (g + 1) * n].astype(f32)
            out_ref[g, :, :n] = (query * gain_ref[...]).astype(bf16)
            out_ref[g, :, n:] = (jnp.concatenate(parts, axis=1) * gain_ref[...]).astype(bf16)

    return small_call(
        kernel,
        "split_qkv",
        [w_query, w_key, w_value, gain],
        [like((TP, own, n + 2 * HD), bf16)],
    )[0]


def merge_qkv(t, pieces, w_query, w_key, w_value, gain):
    own, n = w_query.shape[0], GROUP * HD

    def kernel(t_ref, *refs):
        in_refs, (q_ref, k_ref, v_ref, gain_ref, dq_ref, dk_ref, dv_ref, dgain_ref) = (
            refs[:TP],
            refs[TP:],
        )
        slot = lax.broadcasted_iota(jnp.int32, (own, TP * HD), 1) // HD
        dgain = jnp.zeros((own, 1), f32)
        keys, values = 0.0, 0.0
        for k, ref in enumerate(in_refs):
            group = t_ref[0] ^ k
            here = pl.ds(pl.multiple_of(group * n, n), n)
            part = ref[:, :n].astype(f32)
            dgain += jnp.sum(part * q_ref[:, here].astype(f32), axis=1, keepdims=True)
            dq_ref[:, here] = part * gain_ref[...]
            part = ref[:, n:].astype(f32)
            mine = slot == group
            keys += jnp.where(mine, jnp.concatenate([part[:, :HD]] * TP, axis=1), 0.0)
            values += jnp.where(mine, jnp.concatenate([part[:, HD:]] * TP, axis=1), 0.0)
        for part, ref, out_ref in ((keys, k_ref, dk_ref), (values, v_ref, dv_ref)):
            dgain += jnp.sum(part * ref[...].astype(f32), axis=1, keepdims=True)
            out_ref[...] = part * gain_ref[...]
        dgain_ref[...] = dgain.T

    return small_call(
        kernel,
        "merge_qkv",
        [t[None], *pieces, w_query, w_key, w_value, gain],
        [like(w.shape, f32) for w in (w_query, w_key, w_value)] + [like((1, own), f32)],
        scalars=1,
    )


def split_gate_up(w_gate, w_up, gain):
    own, total = w_gate.shape
    ff = total // TP

    def kernel(gate_ref, up_ref, gain_ref, out_ref):
        for g in range(TP):
            for j in range(ff // LANES):
                here = slice(g * ff + j * LANES, g * ff + (j + 1) * LANES)
                for ref, at in zip((gate_ref, up_ref), interleaved(j)):
                    out_ref[g, :, at] = (ref[:, here].astype(f32) * gain_ref[...]).astype(bf16)

    return small_call(
        kernel,
        "split_gate_up",
        [w_gate, w_up, gain],
        [jax.ShapeDtypeStruct((TP, own, 2 * ff), bf16)],
    )[0]


def merge_gate_up(t, pieces, w_gate, w_up, gain):
    own, total = w_gate.shape
    ff = total // TP

    def kernel(t_ref, *refs):
        in_refs, (gate_ref, up_ref, gain_ref, dgate_ref, dup_ref, dgain_ref) = refs[:TP], refs[TP:]
        dgain = jnp.zeros((own, LANES), f32)
        for k, in_ref in enumerate(in_refs):
            base = (t_ref[0] ^ k) * ff
            for j in range(ff // LANES):
                here = pl.ds(pl.multiple_of(base + j * LANES, LANES), LANES)
                for ref, out_ref, at in zip(
                    (gate_ref, up_ref), (dgate_ref, dup_ref), interleaved(j)
                ):
                    part = in_ref[:, at].astype(f32)
                    dgain += part * ref[:, here].astype(f32)
                    out_ref[:, here] = part * gain_ref[...]
        dgain_ref[...] = jnp.sum(dgain, axis=1, keepdims=True).T

    return small_call(
        kernel,
        "merge_gate_up",
        [t[None], *pieces, w_gate, w_up, gain],
        [like((own, total), f32), like((own, total), f32), like((1, own), f32)],
        scalars=1,
    )


def make_body(reps, ctxs):
    pair = [(0, 1), (1, 0)]

    def swap(v, k):
        if k == 0:
            return v
        if k == 1:
            return lax.ppermute(v, "tx", pair)
        if k == 2:
            return lax.ppermute(v, "ty", pair)
        return lax.ppermute(v, ("ty", "tx"), [(i, i ^ 3) for i in range(TP)])

    def swap_ctx(v, j):
        return lax.ppermute(v, "ctx", [(i, i ^ j) for i in range(ctxs)]) if j else v

    def halves(v):
        half = v.shape[0] // 2
        return v[:half], v[half:]

    def in_order(a, b):
        return [p for k in range(TP) for p in (a[k], b[k])]

    def gather(a, b):
        ax, by = swap(a, 1), swap(b, 2)
        ay, bx = swap(a, 2), swap(b, 1)
        return in_order((a, ax, ay, swap(ax, 2)), (b, bx, by, swap(by, 1)))

    def scatter_far(parts):
        a, b = halves(parts[3])
        return swap(a, 2), swap(b, 1)

    def scatter_near(parts, far):
        a1, b1 = halves(parts[1])
        a2, b2 = halves(parts[2])
        a1 = (a1.astype(f32) + far[0].astype(f32)).astype(bf16)
        b2 = (b2.astype(f32) + far[1].astype(f32)).astype(bf16)
        return [swap(a2, 2), swap(a1, 1), swap(b1, 1), swap(b2, 2)]

    def by_member(v):
        return v.reshape(TP, -1, v.shape[1])

    def exchange(blocks, t, *first):
        out = jnp.zeros_like(blocks)
        for k in range(TP):
            come = swap(lax.dynamic_index_in_dim(blocks, t ^ k, 0, keepdims=True), k)
            come = after(come, *first) if first else come
            out = lax.dynamic_update_slice_in_dim(out, come, t ^ k, 0)
        return out

    def spread(blocks, t, *first):
        return exchange(blocks, t, *first).reshape(-1, blocks.shape[2])

    def collect(summed_rows, t):
        blocks = summed_rows.reshape(TP, -1, summed_rows.shape[1])
        return [swap(lax.dynamic_index_in_dim(blocks, t ^ k, 0, False), k) for k in range(TP)]

    def whole(v):
        return lax.all_gather(v, ("rep", "ctx"), axis=0, tiled=True)

    def over_reps_first(left, right):
        if reps != 2:
            return tn(left, right).astype(bf16)
        index = 1 - lax.axis_index("rep")
        half = left.shape[1] // 2
        if half % (2 * LANES) == 0:
            return weight_grad(left, right, index)
        return tn(lax.dynamic_slice_in_dim(left, index * half, half, 1), right).astype(bf16)

    def over_reps_last(left, right, first):
        if reps != 2:
            return lax.psum_scatter(first, "rep", scatter_dimension=0, tiled=True)
        index = lax.axis_index("rep")
        half = left.shape[1] // 2
        come = lax.ppermute(first, "rep", pair)
        if half % (2 * LANES) == 0:
            return weight_grad(left, right, index, come)
        mine = lax.dynamic_slice_in_dim(left, index * half, half, 1)
        return (tn(mine, right) + come.astype(f32)).astype(bf16)

    def over_reps(left, right):
        return over_reps_last(left, right, over_reps_first(left, right))

    def owned(part):
        return lax.psum_scatter(part, "ctx", scatter_dimension=0, tiled=True)

    def half_of(v, j, other):
        index = lax.axis_index("ctx") // j % 2
        v = v.reshape(2, -1, v.shape[1])
        return lax.dynamic_index_in_dim(v, 1 - index if other else index, 0, False)

    def body(
        tokens,
        span_order,
        norm_attn,
        w_query,
        w_key,
        w_value,
        w_out,
        norm_mlp,
        w_gate,
        w_up,
        w_down,
        out_grad,
    ):
        count, width = tokens.shape
        held, natural = block_orders(width, reps * ctxs)
        span = count * ctxs // span_order.shape[1]
        per = count // span
        t = 2 * lax.axis_index("ty") + lax.axis_index("tx")
        c = lax.axis_index("ctx")
        gain_attn = norm_attn.astype(f32)[:, None]
        gain_mlp = norm_mlp.astype(f32)[:, None]

        qkv_blocks = split_qkv(w_query, w_key, w_value, gain_attn)
        a, b = hold_tokens(after(tokens, qkv_blocks), held)
        qkv_mine, a, b = phase(spread(after(qkv_blocks, a), t), a, b)
        qkv = whole(qkv_mine)
        out = whole(after(w_out, qkv_mine))
        ax, by = swap(a, 1), swap(b, 2)
        ax, by, a, b = phase(ax, by, a, b)
        gate_up_blocks = split_gate_up(after(w_gate, ax), w_up, gain_mlp)
        orders = [swap(after(span_order, qkv_mine), k) for k in range(TP)]
        ay, bx, axy, bxy = swap(a, 2), swap(b, 1), swap(ax, 2), swap(by, 1)
        ay, bx, axy, bxy, gate_up_blocks = phase(ay, bx, axy, bxy, gate_up_blocks)
        x_pieces = in_order((a, ax, ay, axy), (b, bx, by, bxy))

        orders = jnp.concatenate(orders, axis=0).reshape(TP, ctxs, per)
        orders = jnp.concatenate(
            [lax.dynamic_slice_in_dim(orders, c ^ j, 1, 1) for j in range(ctxs)], axis=1
        ).reshape(TP, ctxs * per)
        positions = orders[:, :per, None] * span + jnp.arange(span, dtype=jnp.int32)
        half_dim = HD // 2
        frequency = jnp.power(rope_base, -jnp.arange(half_dim, dtype=f32) / half_dim)
        angles = frequency[:, None] * positions.reshape(TP, 1, count).astype(f32)
        cosine, sine = jnp.cos(angles), jnp.sin(angles)

        qt, kv, inverse = project(x_pieces, qkv, cosine, sine)
        gate_up_mine = spread(after(gate_up_blocks, axy, bxy), t, kv)
        kv_far = [swap_ctx(kv, j) for j in range(1, ctxs)]
        ga, gb = halves(after(out_grad, kv))
        kv, kv_far, gate_up_mine, gax, gby, x_all = phase(
            kv, kv_far, gate_up_mine, swap(ga, 1), swap(gb, 2), join_rows(after(x_pieces, kv))
        )
        kv_pieces = [kv, *kv_far]
        gate_up = whole(gate_up_mine)
        down = whole(after(w_down, gate_up_mine))
        mixed, logsum, parts = [None] * TP, [None] * TP, [None] * TP

        def attend_to(members, queries):
            results = attend(
                members,
                orders,
                [queries[k] for k in members],
                kv_pieces,
                out,
                f32 if 0 in members else bf16,
            )
            for k, (mixed[k], logsum[k], parts[k]) in zip(members, results):
                pass

        attend_to((3,), qt)
        queries, gay, gbx = phase(qt, swap(ga, 2), swap(gb, 1), parts[3])[:3]
        far = scatter_far(parts)
        attend_to((2, 1), queries)
        far, parts[1], parts[2], queries, gaxy, gbxy = phase(
            far, parts[1], parts[2], queries, swap(gax, 2), swap(gby, 1)
        )
        near = scatter_near(parts, far)
        attend_to((0,), queries)
        g_all = join_rows(in_order((ga, gax, gay, gaxy), (gb, gbx, gby, gbxy)))
        near, parts[0], g_all = phase(near, parts[0], g_all)
        middle, inverse_mid, a, b = finish_middle(tokens, [parts[0], *near], held)
        n2_pieces = gather(a, b)

        act, slopes = activate(n2_pieces, gate_up)
        n2_all = join_rows(after(n2_pieces, act))
        part_down = over_reps(act, g_all)
        slopes, part_down, n2_all = phase(slopes, part_down, n2_all)
        down_sent = jnp.split(half_of(part_down, ctxs // 2, True), DOWN_STEPS, axis=1)
        down_come = []

        def send_down(*first):
            piece = after(down_sent[len(down_come)], *first)
            down_come.append(swap_ctx(piece, ctxs // 2))
            return down_come[-1]

        grad_act = activate_back(g_all, down, slopes)
        sent = over_reps_first(n2_all, grad_act)
        sent, down_come[-1] = phase(sent, send_down(down))
        parts = by_member(nt(after(grad_act, sent), gate_up).astype(bf16))
        parts, down_come[-1] = phase(parts, send_down(grad_act))
        far = scatter_far(parts)
        part_gate_up = over_reps_last(n2_all, after(grad_act, parts), sent)
        far, part_gate_up, down_come[-1] = phase(far, part_gate_up, send_down(sent))
        sum_gate_up = owned(part_gate_up)
        near = scatter_near(parts, far)
        forward = nn(after(act, far), down).astype(bf16)
        near, forward = phase(near, forward)
        grad_middle, a, b = finish_norm_back(
            out_grad, middle, inverse_mid, [(parts, 0), *near], natural, False
        )
        back_of = [None] * TP

        def attend_back_to(members, *grads):
            results = attend_back(
                members,
                orders,
                out,
                kv_pieces,
                [
                    (qt[k], mixed[k], logsum[k], *g, inverse[k], (cosine, k), (sine, k))
                    for k, g in zip(members, grads)
                ],
            )
            for k, back_of[k] in zip(members, results):
                pass

        attend_back_to((0,), (a, b))
        ax, by, ay, bx, back_of[0] = phase(
            swap(a, 1), swap(b, 2), swap(a, 2), swap(b, 1), back_of[0]
        )
        forward = by_member(forward)
        attend_back_to((1, 2), (ax, bx), (ay, by))
        axy, bxy, far, back_of[1], back_of[2] = phase(
            swap(ax, 2), swap(by, 1), scatter_far(forward), back_of[1], back_of[2]
        )
        keys_near = [
            swap_ctx(jnp.stack([back_of[k][3][(j - 1) * count : j * count] for k in range(3)]), j)
            for j in range(1, ctxs)
        ]
        db_pieces = in_order((a, ax, ay, axy), (b, bx, by, bxy))
        r = lax.axis_index("rep")
        if reps == 2:
            part_out = out_gradient(mixed, db_pieces, 2, 1 - r)
            part_out, axy, bxy = phase(part_out, axy, bxy)
            part_out = lax.ppermute(part_out, "rep", pair)
        attend_back_to((3,), (axy, bxy))
        forward_near = scatter_near(forward, far)
        keys_near, back_of[3], forward_near = phase(keys_near, back_of[3], forward_near)
        keys_last = [
            swap_ctx(back_of[3][3][None, (j - 1) * count : j * count], j) for j in range(1, ctxs)
        ]
        db_pieces = after(db_pieces, back_of[3])
        if reps == 2:
            part_out = out_gradient(mixed, db_pieces, 2, r, part_out)
        else:
            part_out = out_gradient(mixed, db_pieces, 1, jnp.zeros((), jnp.int32))
            part_out = lax.psum_scatter(part_out, "rep", scatter_dimension=0, tiled=True)
        raw_gate_up = collect(after(sum_gate_up, keys_near), t)
        keys_last, part_out, raw_gate_up = phase(keys_last, part_out, raw_gate_up)
        grad_proj, scaled_proj = finish_keys(
            [v[2] for v in back_of],
            keys_near,
            keys_last,
            [v[0] for v in back_of],
            [v[1] for v in back_of],
            inverse,
            cosine,
            sine,
        )
        parts = by_member(nt(grad_proj, qkv).astype(bf16))
        parts, down_come[-1] = phase(parts, send_down(keys_near))
        across = phase(*halves(parts[3]))
        far_back = swap(across[0], 2), swap(across[1], 1)
        sent = over_reps_first(x_all, after(scaled_proj, across))
        part_qkv = over_reps_last(x_all, after(scaled_proj, sent), sent)
        sum_out = owned(after(part_out, across))
        far_back, part_qkv, sum_out = phase(far_back, part_qkv, sum_out)
        sum_qkv = owned(part_qkv)
        near = scatter_near(parts, far_back)
        layer_out = finish_layer(after(middle, far_back), [(forward, 0), *forward_near])
        part_down = half_of(after(part_down, far_back), ctxs // 2, False).astype(f32)
        part_down = part_down + jnp.concatenate(down_come, axis=1).astype(f32)
        grad_gate, grad_up, grad_norm_mlp = merge_gate_up(
            t, after(raw_gate_up, far_back), w_gate, w_up, gain_mlp
        )
        near, layer_out, part_down, grad_norm_mlp = phase(
            near, layer_out, part_down, grad_norm_mlp
        )
        (input_grad,) = finish_norm_back(
            grad_middle, tokens, inverse[0], [(parts, 0), *near], natural, True
        )
        sum_qkv = after(sum_qkv, input_grad)
        grad_query, grad_key, grad_value, grad_norm_attn = merge_qkv(
            t, collect(sum_qkv, t), w_query, w_key, w_value, gain_attn
        )
        down_come = swap_ctx(
            half_of(part_down.astype(bf16), ctxs // 4, True), ctxs // 4
        )
        down_come = after(down_come, grad_query)
        sum_down = half_of(part_down, ctxs // 4, False) + down_come.astype(f32)
        return (
            layer_out,
            input_grad,
            grad_norm_attn[0],
            grad_query,
            grad_key,
            grad_value,
            after(sum_out, grad_query).astype(f32),
            grad_norm_mlp[0],
            grad_gate,
            grad_up,
            sum_down,
        )

    return body


def solution(mesh):
    sequences, ctxs = mesh.shape["dp"], mesh.shape["ctx"]
    reps = sequences // TP
    names = ("ty", "tx", "rep", "ctx")
    grid = Mesh(mesh.devices.reshape(2, 2, reps, ctxs), names)
    matrix, vector = P(names, None), P(names)
    order = P(("ty", "tx", "rep"), None)
    weights = [vector, matrix, matrix, matrix, matrix, vector, matrix, matrix, matrix]
    return jax.shard_map(
        make_body(reps, ctxs),
        mesh=grid,
        in_specs=(matrix, order, *weights, matrix),
        out_specs=(matrix, matrix, *weights),
        check_vma=False,
    )
```

```python
import jax
import jax.numpy as jnp
from jax import lax
from jax.experimental import pallas as pl
from jax.experimental.pallas import tpu as pltpu
from jax.sharding import Mesh, PartitionSpec as P

H = 32
KV = 4
HD = 64
TP = 4
GROUP = H // KV
LANES = 128
ROWS = 64
ROOM = 60 << 20
ATTEND_ROOM = 60 << 20
DOWN_STEPS = 4

epsilon = 1e-05
rope_base = 10000.0
masked_score = -1e30
bf16 = jnp.bfloat16
f32 = jnp.float32


def after(value, *others):
    return lax.optimization_barrier((value,) + others)[0]


def phase(*values):
    return lax.optimization_barrier(values)


def nn(left, right):
    return lax.dot_general(left, right, (((1,), (0,)), ((), ())), preferred_element_type=f32)


def nt(left, right):
    return lax.dot_general(left, right, (((1,), (1,)), ((), ())), preferred_element_type=f32)


def tn(left, right):
    return lax.dot_general(left, right, (((0,), (0,)), ((), ())), preferred_element_type=f32)


def like(shape, kind):
    return jax.ShapeDtypeStruct(shape, kind)


def size_of(values):
    return sum(v.size * v.dtype.itemsize for v in values)


def small_call(
    kernel, name, inputs, outputs, flops=0, scratch=(), scalars=0, transcendentals=0, room=ROOM
):
    specs, arrays = [pl.BlockSpec(memory_space=pltpu.SMEM)] * scalars, list(inputs[:scalars])
    for v in inputs[scalars:]:
        if isinstance(v, tuple):
            specs.append(row_block(*v))
            arrays.append(v[0])
        else:
            specs.append(whole_block(v.shape))
            arrays.append(v)
    size = size_of((*arrays, *outputs))
    return pl.pallas_call(
        kernel,
        grid=(1,),
        in_specs=specs,
        out_specs=[whole_block(v.shape) for v in outputs],
        out_shape=outputs,
        scratch_shapes=list(scratch),
        compiler_params=pltpu.CompilerParams(vmem_limit_bytes=room),
        cost_estimate=pl.CostEstimate(
            flops=max(flops, size), bytes_accessed=size, transcendentals=transcendentals
        ),
        name=name,
    )(*arrays)


def row_block(array, index):
    shape = array.shape[1:]
    return pl.BlockSpec((None,) + shape, lambda i: (index,) + (0,) * len(shape))


def whole_block(shape):
    return pl.BlockSpec(shape, lambda i: (0,) * len(shape))


def turn(vectors, cosine, sine):
    half = HD // 2
    out = []
    for at in range(0, vectors.shape[0], HD):
        first, second = vectors[at : at + half], vectors[at + half : at + HD]
        out += [first * cosine - second * sine, second * cosine + first * sine]
    return jnp.concatenate(out, axis=0)


def project(pieces, w, cosine, sine):
    half, width = pieces[0].shape
    rows, n, q = 2 * half, w.shape[1], GROUP * HD

    def kernel(*refs):
        x_refs, (w_ref, cos_ref, sin_ref, kv_ref), outs = refs[:8], refs[8:12], refs[12:]
        for k in range(TP):
            xb = jnp.concatenate([x_refs[2 * k][...], x_refs[2 * k + 1][...]], axis=0)
            x = xb.astype(f32)
            inverse = lax.rsqrt(jnp.mean(x * x, axis=1, keepdims=True) + epsilon)
            outs[TP + k][...] = inverse
            flat = (nn(xb, w_ref[...]) * inverse).T
            cosine, sine = cos_ref[k], sin_ref[k]
            outs[k][...] = (turn(flat[:q], cosine, sine) * HD**-0.5).astype(bf16)
            kv = jnp.concatenate([turn(flat[q : q + HD], cosine, sine), flat[q + HD :]], axis=0)
            kv_ref[k] = kv.T.astype(bf16)

    kv, *outs = small_call(
        kernel,
        "project",
        [*pieces, w, cosine, sine],
        [like((TP, rows, 2 * HD), bf16)]
        + [like((q, rows), bf16)] * TP
        + [like((rows, 1), f32)] * TP,
        flops=2 * TP * rows * width * n,
    )
    return outs[:TP], kv, outs[TP:]


def set_bias(order_ref, k, bias_ref):
    keys, rows = bias_ref.shape
    span = keys // order_ref.shape[1]
    lane = lax.broadcasted_iota(jnp.int32, (span, rows), 1)
    query = jnp.where(lane < span, order_ref[k, 0], order_ref[k, 1] - 1) * span + lane
    row = lax.broadcasted_iota(jnp.int32, (span, rows), 0)
    for b in range(keys // span):
        key = order_ref[k, b] * span + row
        bias_ref[b * span : (b + 1) * span, :] = jnp.where(query >= key, 0.0, masked_score)


def attend(members, orders, queries, kv_pieces, wo, kind):
    n, rows = queries[0].shape
    holders, width = len(kv_pieces), wo.shape[1]
    keys, count = holders * rows, len(members)

    def kernel(order_ref, wo_ref, *refs):
        for i, k in enumerate(members):
            qt_ref, *kv_refs = refs[i * (1 + holders) : (i + 1) * (1 + holders)]
            outs = refs[count * (1 + holders) :]
            ot_ref, lse_ref, part_ref = outs[3 * i : 3 * i + 3]
            bias_ref = outs[-1]
            set_bias(order_ref, k, bias_ref)
            kv = jnp.concatenate([ref[...] for ref in kv_refs], axis=0)
            vt = kv.astype(f32).T[HD:].astype(bf16)
            zero = jnp.zeros((HD, rows), bf16)
            for h in range(GROUP):
                at = slice(h * HD, (h + 1) * HD)
                scores = nn(kv, jnp.concatenate([qt_ref[at, :], zero], axis=0)) + bias_ref[...]
                top = jnp.max(scores, axis=0, keepdims=True)
                exponent = jnp.exp(scores - top)
                total = jnp.sum(exponent, axis=0, keepdims=True)
                ot_ref[at, :] = (nn(vt, exponent.astype(bf16)) / total).astype(bf16)
                lse_ref[h : h + 1, :] = top + jnp.log(total)
            part_ref[...] = tn(ot_ref[...], wo_ref[...]).astype(part_ref.dtype)

    inputs, outputs = [orders, wo], []
    for i, k in enumerate(members):
        inputs += [queries[i], *[(piece, k) for piece in kv_pieces]]
        outputs += [like((n, rows), bf16), like((GROUP, rows), f32), like((rows, width), kind)]
    results = small_call(
        kernel,
        "attend",
        inputs,
        outputs,
        flops=2 * rows * n * (keys * 2 * 4 + width) * count,
        scratch=[pltpu.VMEM((keys, rows), f32)],
        scalars=1,
        transcendentals=GROUP * rows * keys * count,
        room=ATTEND_ROOM,
    )
    return [results[3 * i : 3 * i + 3] for i in range(count)]


def attend_back(members, orders, wo, kv_pieces, details):
    n, rows = details[0][0].shape
    holders, width = len(kv_pieces), wo.shape[1]
    keys, half, count = holders * rows, rows // 2, len(members)
    step = 8 + holders

    def kernel(order_ref, wo_ref, *refs):
        outs, (bias_ref, dat_ref, dqt_ref, dkv_ref) = refs[count * step : -4], refs[-4:]
        for i, k in enumerate(members):
            own = refs[i * step : (i + 1) * step]
            kv_refs, (qt_ref, ot_ref, lse_ref, a_ref, b_ref) = own[:holders], own[holders:-3]
            inv_ref, cos_ref, sin_ref = own[-3:]
            dq_ref, dqs_ref, own_ref, far_ref = outs[4 * i : 4 * i + 4]
            set_bias(order_ref, k, bias_ref)
            kv = jnp.concatenate([ref[...] for ref in kv_refs], axis=0)
            kt = kv.astype(f32).T[:HD].astype(bf16)
            zero = jnp.zeros((HD, rows), bf16)
            dat_ref[:, :half] = nt(wo_ref[...], a_ref[...]).astype(bf16)
            dat_ref[:, half:] = nt(wo_ref[...], b_ref[...]).astype(bf16)
            for h in range(GROUP):
                at = slice(h * HD, (h + 1) * HD)
                q_low = jnp.concatenate([qt_ref[at, :], zero], axis=0)
                da_high = jnp.concatenate([zero, dat_ref[at, :]], axis=0)
                weights = jnp.exp(nn(kv, q_low) + bias_ref[...] - lse_ref[h : h + 1, :])
                delta = jnp.sum(
                    dat_ref[at, :].astype(f32) * ot_ref[at, :].astype(f32), axis=0, keepdims=True
                )
                ds = (weights * (nn(kv, da_high) - delta)).astype(bf16)
                dkv = nt(ds, q_low) + nt(weights.astype(bf16), da_high)
                if h == 0:
                    dkv_ref[...] = dkv
                else:
                    dkv_ref[...] += dkv
                dqt_ref[at, :] = nn(kt, ds)
            dq = (turn(dqt_ref[...], cos_ref[...], -sin_ref[...]) * HD**-0.5).T
            dq_ref[...] = dq.astype(bf16)
            dqs_ref[...] = (dq * inv_ref[...]).astype(bf16)
            own_ref[...] = dkv_ref[:rows, :]
            far_ref[...] = dkv_ref[rows:, :].astype(bf16)

    inputs, outputs = [orders, wo], []
    for k, detail in zip(members, details):
        inputs += [*[(piece, k) for piece in kv_pieces], *detail]
        outputs += [
            like((rows, n), bf16),
            like((rows, n), bf16),
            like((rows, 2 * HD), f32),
            like((keys - rows, 2 * HD), bf16),
        ]
    results = small_call(
        kernel,
        "attend_back",
        inputs,
        outputs,
        flops=2 * rows * n * (keys * 5 * 4 + width) * count,
        scratch=[
            pltpu.VMEM((keys, rows), f32),
            pltpu.VMEM((n, rows), bf16),
            pltpu.VMEM((n, rows), f32),
            pltpu.VMEM((keys, 2 * HD), f32),
        ],
        scalars=1,
        transcendentals=GROUP * rows * keys * count,
        room=ATTEND_ROOM,
    )
    return [results[4 * i : 4 * i + 4] for i in range(count)]


def out_gradient(mixed, grads, parts, index, come=None):
    n, width = mixed[0].shape[0] // parts, grads[0].shape[1]

    def kernel(index_ref, *refs):
        at = pl.ds(pl.multiple_of(index_ref[0] * n, n), n)
        total = 0.0 if come is None else refs[3 * TP][...].astype(f32)
        for k in range(TP):
            db = jnp.concatenate([refs[TP + 2 * k][...], refs[TP + 2 * k + 1][...]], axis=0)
            total = total + nn(refs[k][at, :], db)
        refs[-1][...] = total.astype(bf16)

    return small_call(
        kernel,
        "out_gradient",
        [index[None], *mixed, *grads] + ([] if come is None else [come]),
        [like((n, width), bf16)],
        flops=2 * TP * mixed[0].shape[1] * n * width,
        scalars=1,
    )[0]


def finish_keys(own, near, last, dq, dqs, inverse, cosine, sine):
    rows, n = dq[0].shape

    def kernel(*refs):
        own_refs, refs = refs[:TP], refs[TP:]
        near_refs, refs = refs[: len(near)], refs[len(near) :]
        last_refs, refs = refs[: len(last)], refs[len(last) :]
        dq_refs, dqs_refs, refs = refs[:TP], refs[TP : 2 * TP], refs[2 * TP :]
        inv_refs, (cos_ref, sin_ref, plain_ref, scaled_ref) = refs[:TP], refs[TP:]
        for k in range(TP):
            total = own_refs[k][...]
            for ref in near_refs if k < TP - 1 else last_refs:
                total = total + ref[k % (TP - 1)].astype(f32)
            total = total.T
            keys = turn(total[:HD], cos_ref[k], -sin_ref[k])
            total = jnp.concatenate([keys, total[HD:]], axis=0).T
            at = slice(k * rows, (k + 1) * rows)
            plain_ref[at, :n] = dq_refs[k][...]
            plain_ref[at, n:] = total.astype(bf16)
            scaled_ref[at, :n] = dqs_refs[k][...]
            scaled_ref[at, n:] = (total * inv_refs[k][...]).astype(bf16)

    shape = like((TP * rows, n + 2 * HD), bf16)
    return small_call(
        kernel,
        "finish_keys",
        [*own, *near, *last, *dq, *dqs, *inverse, cosine, sine],
        [shape, shape],
    )


def join_rows(pieces):
    rows, width = pieces[0].shape

    def kernel(*refs):
        for i, ref in enumerate(refs[:-1]):
            refs[-1][i * rows : (i + 1) * rows, :] = ref[...]

    return small_call(
        kernel, "join_rows", pieces, [like((len(pieces) * rows, width), pieces[0].dtype)]
    )[0]


def reorder_lanes(v, ordered):
    order, size = ordered
    return jnp.concatenate([v[:, i * size : (i + 1) * size] for i in order], axis=1)


def block_orders(width, holders):
    held = [m * holders + h for h in range(holders) for m in range(TP)]
    natural = [held.index(i) for i in range(len(held))]
    size = width // len(held)
    return (held, size), (natural, size)


def hold_tokens(tokens, held):
    half = tokens.shape[0] // 2

    def kernel(x_ref, a_ref, b_ref):
        a_ref[...] = reorder_lanes(x_ref[:half, :].astype(f32), held).astype(bf16)
        b_ref[...] = reorder_lanes(x_ref[half:, :].astype(f32), held).astype(bf16)

    shape = like((half, tokens.shape[1]), bf16)
    return small_call(kernel, "hold_tokens", [tokens], [shape, shape])


def summed(refs, at, half):
    own_ref, a2_ref, a1_ref, b1_ref, b2_ref = refs
    first, second = (a2_ref, a1_ref) if at < half else (b1_ref, b2_ref)
    come = slice(at % half, at % half + ROWS)
    total = own_ref[at : at + ROWS, :].astype(f32)
    return total + first[come, :].astype(f32) + second[come, :].astype(f32)


def finish_middle(tokens, pieces, held):
    rows, width = tokens.shape
    half = rows // 2

    def kernel(x_ref, *refs):
        sums, (mid_ref, inv_ref, a_ref, b_ref) = refs[:5], refs[5:]
        for at in range(0, rows, ROWS):
            here = slice(at, at + ROWS)
            middle = x_ref[here, :].astype(f32) + summed(sums, at, half)
            inverse = lax.rsqrt(jnp.mean(middle * middle, axis=1, keepdims=True) + epsilon)
            mid_ref[here, :] = middle
            inv_ref[here, :] = inverse
            out = a_ref if at < half else b_ref
            come = slice(at % half, at % half + ROWS)
            out[come, :] = reorder_lanes(middle * inverse, held).astype(bf16)

    return small_call(
        kernel,
        "finish_middle",
        [tokens, *pieces],
        [
            like((rows, width), f32),
            like((rows, 1), f32),
            like((half, width), bf16),
            like((half, width), bf16),
        ],
    )


def finish_norm_back(grad, normed_from, inverse, pieces, natural, last):
    rows, width = grad.shape
    half = rows // 2

    def kernel(g_ref, x_ref, inv_ref, *refs):
        sums, outs = refs[:5], refs[5:]
        for at in range(0, rows, ROWS):
            here = slice(at, at + ROWS)
            scaled = reorder_lanes(summed(sums, at, half), natural)
            inverse = inv_ref[here, :]
            normed = x_ref[here, :].astype(f32) * inverse
            mean = jnp.mean(scaled * normed, axis=1, keepdims=True)
            total = g_ref[here, :].astype(f32) + inverse * (scaled - normed * mean)
            outs[0][here, :] = total
            if not last:
                out = outs[1] if at < half else outs[2]
                out[at % half : at % half + ROWS, :] = total.astype(bf16)

    shapes = [like((rows, width), f32)]
    if not last:
        shapes += [like((half, width), bf16)] * 2
    return small_call(
        kernel, "finish_norm_back", [grad, normed_from, inverse, *pieces], shapes
    )


def finish_layer(middle, pieces):
    rows, width = middle.shape

    def kernel(mid_ref, *refs):
        for at in range(0, rows, ROWS):
            here = slice(at, at + ROWS)
            total = mid_ref[here, :] + summed(refs[:5], at, rows // 2)
            refs[5][here, :] = total.astype(bf16)

    return small_call(
        kernel, "finish_layer", [middle, *pieces], [like((rows, width), bf16)]
    )[0]


def interleaved(i):
    return slice(2 * i * LANES, (2 * i + 1) * LANES), slice((2 * i + 1) * LANES, (2 * i + 2) * LANES)


def activate(pieces, gate_up, tile=256):
    half, width = pieces[0].shape
    total, ff = half * len(pieces), gate_up.shape[1] // 2

    def kernel(*refs):
        n_refs, (w_ref, m_ref, slope_ref, n2_ref) = refs[: len(pieces)], refs[len(pieces) :]

        @pl.when(pl.program_id(0) == 0)
        def _():
            for i, ref in enumerate(n_refs):
                n2_ref[i * half : (i + 1) * half, :] = ref[...]

        both = nn(n2_ref[...], w_ref[...])
        for i in range(tile // LANES):
            gate_at, up_at = interleaved(i)
            gate, up = both[:, gate_at], both[:, up_at]
            sigmoid = jax.nn.sigmoid(gate)
            silu = gate * sigmoid
            m_ref[:, i * LANES : (i + 1) * LANES] = (silu * up).astype(bf16)
            slope_ref[:, gate_at] = (up * (sigmoid + silu * (1.0 - sigmoid))).astype(bf16)
            slope_ref[:, up_at] = silu.astype(bf16)

    return pl.pallas_call(
        kernel,
        grid=(pl.cdiv(ff, tile),),
        in_specs=[whole_block(v.shape) for v in pieces]
        + [pl.BlockSpec((width, 2 * tile), lambda j: (0, j))],
        out_specs=[
            pl.BlockSpec((total, tile), lambda j: (0, j)),
            pl.BlockSpec((total, 2 * tile), lambda j: (0, j)),
        ],
        out_shape=[like((total, ff), bf16), like((total, 2 * ff), bf16)],
        scratch_shapes=[pltpu.VMEM((total, width), bf16)],
        compiler_params=pltpu.CompilerParams(vmem_limit_bytes=ROOM),
        cost_estimate=pl.CostEstimate(
            flops=4 * total * width * ff,
            bytes_accessed=2 * (total * width + 2 * width * ff + 3 * total * ff),
            transcendentals=total * ff,
        ),
        name="activate",
    )(*pieces, gate_up)


def activate_back(g, down, slopes, tile=256):
    total, width = g.shape
    ff = down.shape[0]

    def kernel(g_ref, down_ref, slope_ref, d_ref):
        dm = nt(g_ref[...], down_ref[...])
        for i in range(tile // LANES):
            part = dm[:, i * LANES : (i + 1) * LANES]
            for at in interleaved(i):
                d_ref[:, at] = (part * slope_ref[:, at].astype(f32)).astype(bf16)

    return pl.pallas_call(
        kernel,
        grid=(pl.cdiv(ff, tile),),
        in_specs=[
            pl.BlockSpec((total, width), lambda j: (0, 0)),
            pl.BlockSpec((tile, width), lambda j: (j, 0)),
            pl.BlockSpec((total, 2 * tile), lambda j: (0, j)),
        ],
        out_specs=pl.BlockSpec((total, 2 * tile), lambda j: (0, j)),
        out_shape=like((total, 2 * ff), bf16),
        compiler_params=pltpu.CompilerParams(vmem_limit_bytes=ROOM),
        cost_estimate=pl.CostEstimate(
            flops=2 * total * width * ff,
            bytes_accessed=2 * (total * width + width * ff + 4 * total * ff),
            transcendentals=0,
        ),
        name="activate_back",
    )(g, down, slopes)


def weight_grad(left, right, index, come=None):
    total, width = left.shape
    n = right.shape[1]
    rows, columns = width // 4, n // 2 if n % (2 * LANES) == 0 else n

    def kernel(index_ref, left_ref, right_ref, *refs):
        part = tn(left_ref[...], right_ref[...])
        if come is not None:
            part = part + refs[0][...].astype(f32)
        refs[-1][...] = part.astype(bf16)

    out = pl.BlockSpec((rows, columns), lambda i, j, index: (i, j))
    more = [] if come is None else [come]
    return pl.pallas_call(
        kernel,
        grid_spec=pltpu.PrefetchScalarGridSpec(
            num_scalar_prefetch=1,
            grid=(2, n // columns),
            in_specs=[
                pl.BlockSpec((total, rows), lambda i, j, index: (0, 2 * index[0] + i)),
                pl.BlockSpec((total, columns), lambda i, j, index: (0, j)),
            ]
            + [out] * len(more),
            out_specs=out,
        ),
        out_shape=like((width // 2, n), bf16),
        compiler_params=pltpu.CompilerParams(vmem_limit_bytes=ROOM),
        cost_estimate=pl.CostEstimate(
            flops=total * width * n,
            bytes_accessed=total * width + 2 * total * n + 2 * width * n,
            transcendentals=0,
        ),
        name="weight_grad",
    )(index[None], left, right, *more)


def split_qkv(w_query, w_key, w_value, gain):
    own, n = w_query.shape[0], GROUP * HD

    def kernel(q_ref, k_ref, v_ref, gain_ref, out_ref):
        for g in range(TP):
            parts = [ref[:, g * HD : (g + 1) * HD].astype(f32) for ref in (k_ref, v_ref)]
            query = q_ref[:, g * n : (g + 1) * n].astype(f32)
            out_ref[g, :, :n] = (query * gain_ref[...]).astype(bf16)
            out_ref[g, :, n:] = (jnp.concatenate(parts, axis=1) * gain_ref[...]).astype(bf16)

    return small_call(
        kernel,
        "split_qkv",
        [w_query, w_key, w_value, gain],
        [like((TP, own, n + 2 * HD), bf16)],
    )[0]


def merge_qkv(t, pieces, w_query, w_key, w_value, gain):
    own, n = w_query.shape[0], GROUP * HD

    def kernel(t_ref, *refs):
        in_refs, (q_ref, k_ref, v_ref, gain_ref, dq_ref, dk_ref, dv_ref, dgain_ref) = (
            refs[:TP],
            refs[TP:],
        )
        slot = lax.broadcasted_iota(jnp.int32, (own, TP * HD), 1) // HD
        dgain = jnp.zeros((own, 1), f32)
        keys, values = 0.0, 0.0
        for k, ref in enumerate(in_refs):
            group = t_ref[0] ^ k
            here = pl.ds(pl.multiple_of(group * n, n), n)
            part = ref[:, :n].astype(f32)
            dgain += jnp.sum(part * q_ref[:, here].astype(f32), axis=1, keepdims=True)
            dq_ref[:, here] = part * gain_ref[...]
            part = ref[:, n:].astype(f32)
            mine = slot == group
            keys += jnp.where(mine, jnp.concatenate([part[:, :HD]] * TP, axis=1), 0.0)
            values += jnp.where(mine, jnp.concatenate([part[:, HD:]] * TP, axis=1), 0.0)
        for part, ref, out_ref in ((keys, k_ref, dk_ref), (values, v_ref, dv_ref)):
            dgain += jnp.sum(part * ref[...].astype(f32), axis=1, keepdims=True)
            out_ref[...] = part * gain_ref[...]
        dgain_ref[...] = dgain.T

    return small_call(
        kernel,
        "merge_qkv",
        [t[None], *pieces, w_query, w_key, w_value, gain],
        [like(w.shape, f32) for w in (w_query, w_key, w_value)] + [like((1, own), f32)],
        scalars=1,
    )


def split_gate_up(w_gate, w_up, gain):
    own, total = w_gate.shape
    ff = total // TP

    def kernel(gate_ref, up_ref, gain_ref, out_ref):
        for g in range(TP):
            for j in range(ff // LANES):
                here = slice(g * ff + j * LANES, g * ff + (j + 1) * LANES)
                for ref, at in zip((gate_ref, up_ref), interleaved(j)):
                    out_ref[g, :, at] = (ref[:, here].astype(f32) * gain_ref[...]).astype(bf16)

    return small_call(
        kernel,
        "split_gate_up",
        [w_gate, w_up, gain],
        [jax.ShapeDtypeStruct((TP, own, 2 * ff), bf16)],
    )[0]


def merge_gate_up(t, pieces, w_gate, w_up, gain):
    own, total = w_gate.shape
    ff = total // TP

    def kernel(t_ref, *refs):
        in_refs, (gate_ref, up_ref, gain_ref, dgate_ref, dup_ref, dgain_ref) = refs[:TP], refs[TP:]
        dgain = jnp.zeros((own, LANES), f32)
        for k, in_ref in enumerate(in_refs):
            base = (t_ref[0] ^ k) * ff
            for j in range(ff // LANES):
                here = pl.ds(pl.multiple_of(base + j * LANES, LANES), LANES)
                for ref, out_ref, at in zip(
                    (gate_ref, up_ref), (dgate_ref, dup_ref), interleaved(j)
                ):
                    part = in_ref[:, at].astype(f32)
                    dgain += part * ref[:, here].astype(f32)
                    out_ref[:, here] = part * gain_ref[...]
        dgain_ref[...] = jnp.sum(dgain, axis=1, keepdims=True).T

    return small_call(
        kernel,
        "merge_gate_up",
        [t[None], *pieces, w_gate, w_up, gain],
        [like((own, total), f32), like((own, total), f32), like((1, own), f32)],
        scalars=1,
    )


def make_body(reps, ctxs):
    pair = [(0, 1), (1, 0)]

    def swap(v, k):
        if k == 0:
            return v
        if k == 1:
            return lax.ppermute(v, "tx", pair)
        if k == 2:
            return lax.ppermute(v, "ty", pair)
        return lax.ppermute(v, ("ty", "tx"), [(i, i ^ 3) for i in range(TP)])

    def swap_ctx(v, j):
        return lax.ppermute(v, "ctx", [(i, i ^ j) for i in range(ctxs)]) if j else v

    def halves(v):
        half = v.shape[0] // 2
        return v[:half], v[half:]

    def in_order(a, b):
        return [p for k in range(TP) for p in (a[k], b[k])]

    def gather(a, b):
        ax, by = swap(a, 1), swap(b, 2)
        ay, bx = swap(a, 2), swap(b, 1)
        return in_order((a, ax, ay, swap(ax, 2)), (b, bx, by, swap(by, 1)))

    def scatter_far(parts):
        a, b = halves(parts[3])
        return swap(a, 2), swap(b, 1)

    def scatter_near(parts, far):
        a1, b1 = halves(parts[1])
        a2, b2 = halves(parts[2])
        a1 = (a1.astype(f32) + far[0].astype(f32)).astype(bf16)
        b2 = (b2.astype(f32) + far[1].astype(f32)).astype(bf16)
        return [swap(a2, 2), swap(a1, 1), swap(b1, 1), swap(b2, 2)]

    def by_member(v):
        return v.reshape(TP, -1, v.shape[1])

    def exchange(blocks, t, *first):
        out = jnp.zeros_like(blocks)
        for k in range(TP):
            come = swap(lax.dynamic_index_in_dim(blocks, t ^ k, 0, keepdims=True), k)
            come = after(come, *first) if first else come
            out = lax.dynamic_update_slice_in_dim(out, come, t ^ k, 0)
        return out

    def spread(blocks, t, *first):
        return exchange(blocks, t, *first).reshape(-1, blocks.shape[2])

    def collect(summed_rows, t):
        blocks = summed_rows.reshape(TP, -1, summed_rows.shape[1])
        return [swap(lax.dynamic_index_in_dim(blocks, t ^ k, 0, False), k) for k in range(TP)]

    def whole(v):
        return lax.all_gather(v, ("rep", "ctx"), axis=0, tiled=True)

    def over_reps_first(left, right):
        if reps != 2:
            return tn(left, right).astype(bf16)
        index = 1 - lax.axis_index("rep")
        half = left.shape[1] // 2
        if half % (2 * LANES) == 0:
            return weight_grad(left, right, index)
        return tn(lax.dynamic_slice_in_dim(left, index * half, half, 1), right).astype(bf16)

    def over_reps_last(left, right, first):
        if reps != 2:
            return lax.psum_scatter(first, "rep", scatter_dimension=0, tiled=True)
        index = lax.axis_index("rep")
        half = left.shape[1] // 2
        come = lax.ppermute(first, "rep", pair)
        if half % (2 * LANES) == 0:
            return weight_grad(left, right, index, come)
        mine = lax.dynamic_slice_in_dim(left, index * half, half, 1)
        return (tn(mine, right) + come.astype(f32)).astype(bf16)

    def over_reps(left, right):
        return over_reps_last(left, right, over_reps_first(left, right))

    def owned(part):
        return lax.psum_scatter(part, "ctx", scatter_dimension=0, tiled=True)

    def half_of(v, j, other):
        index = lax.axis_index("ctx") // j % 2
        v = v.reshape(2, -1, v.shape[1])
        return lax.dynamic_index_in_dim(v, 1 - index if other else index, 0, False)

    def body(
        tokens,
        span_order,
        norm_attn,
        w_query,
        w_key,
        w_value,
        w_out,
        norm_mlp,
        w_gate,
        w_up,
        w_down,
        out_grad,
    ):
        count, width = tokens.shape
        held, natural = block_orders(width, reps * ctxs)
        span = count * ctxs // span_order.shape[1]
        per = count // span
        t = 2 * lax.axis_index("ty") + lax.axis_index("tx")
        c = lax.axis_index("ctx")
        gain_attn = norm_attn.astype(f32)[:, None]
        gain_mlp = norm_mlp.astype(f32)[:, None]

        qkv_blocks = split_qkv(w_query, w_key, w_value, gain_attn)
        a, b = hold_tokens(after(tokens, qkv_blocks), held)
        qkv_mine, a, b = phase(spread(after(qkv_blocks, a), t), a, b)
        qkv = whole(qkv_mine)
        out = whole(after(w_out, qkv_mine))
        ax, by = swap(a, 1), swap(b, 2)
        ax, by, a, b = phase(ax, by, a, b)
        gate_up_blocks = split_gate_up(after(w_gate, ax), w_up, gain_mlp)
        orders = [swap(after(span_order, qkv_mine), k) for k in range(TP)]
        ay, bx, axy, bxy = swap(a, 2), swap(b, 1), swap(ax, 2), swap(by, 1)
        ay, bx, axy, bxy, gate_up_blocks = phase(ay, bx, axy, bxy, gate_up_blocks)
        x_pieces = in_order((a, ax, ay, axy), (b, bx, by, bxy))

        orders = jnp.concatenate(orders, axis=0).reshape(TP, ctxs, per)
        orders = jnp.concatenate(
            [lax.dynamic_slice_in_dim(orders, c ^ j, 1, 1) for j in range(ctxs)], axis=1
        ).reshape(TP, ctxs * per)
        positions = orders[:, :per, None] * span + jnp.arange(span, dtype=jnp.int32)
        half_dim = HD // 2
        frequency = jnp.power(rope_base, -jnp.arange(half_dim, dtype=f32) / half_dim)
        angles = frequency[:, None] * positions.reshape(TP, 1, count).astype(f32)
        cosine, sine = jnp.cos(angles), jnp.sin(angles)

        qt, kv, inverse = project(x_pieces, qkv, cosine, sine)
        gate_up_mine = spread(after(gate_up_blocks, axy, bxy), t, kv)
        kv_far = [swap_ctx(kv, j) for j in range(1, ctxs)]
        ga, gb = halves(after(out_grad, kv))
        kv, kv_far, gate_up_mine, gax, gby, x_all = phase(
            kv, kv_far, gate_up_mine, swap(ga, 1), swap(gb, 2), join_rows(after(x_pieces, kv))
        )
        kv_pieces = [kv, *kv_far]
        gate_up = whole(gate_up_mine)
        down = whole(after(w_down, gate_up_mine))
        mixed, logsum, parts = [None] * TP, [None] * TP, [None] * TP

        def attend_to(members, queries):
            results = attend(
                members,
                orders,
                [queries[k] for k in members],
                kv_pieces,
                out,
                f32 if 0 in members else bf16,
            )
            for k, (mixed[k], logsum[k], parts[k]) in zip(members, results):
                pass

        attend_to((3,), qt)
        queries, gay, gbx = phase(qt, swap(ga, 2), swap(gb, 1), parts[3])[:3]
        far = scatter_far(parts)
        attend_to((2, 1), queries)
        far, parts[1], parts[2], queries, gaxy, gbxy = phase(
            far, parts[1], parts[2], queries, swap(gax, 2), swap(gby, 1)
        )
        near = scatter_near(parts, far)
        attend_to((0,), queries)
        g_all = join_rows(in_order((ga, gax, gay, gaxy), (gb, gbx, gby, gbxy)))
        near, parts[0], g_all = phase(near, parts[0], g_all)
        middle, inverse_mid, a, b = finish_middle(tokens, [parts[0], *near], held)
        n2_pieces = gather(a, b)

        act, slopes = activate(n2_pieces, gate_up)
        n2_all = join_rows(after(n2_pieces, act))
        part_down = over_reps(act, g_all)
        slopes, part_down, n2_all = phase(slopes, part_down, n2_all)
        down_sent = jnp.split(half_of(part_down, ctxs // 2, True), DOWN_STEPS, axis=1)
        down_come = []

        def send_down(*first):
            piece = after(down_sent[len(down_come)], *first)
            down_come.append(swap_ctx(piece, ctxs // 2))
            return down_come[-1]

        grad_act = activate_back(g_all, down, slopes)
        sent = over_reps_first(n2_all, grad_act)
        sent, down_come[-1] = phase(sent, send_down(down))
        parts = by_member(nt(after(grad_act, sent), gate_up).astype(bf16))
        parts, down_come[-1] = phase(parts, send_down(grad_act))
        far = scatter_far(parts)
        part_gate_up = over_reps_last(n2_all, after(grad_act, parts), sent)
        far, part_gate_up, down_come[-1] = phase(far, part_gate_up, send_down(sent))
        sum_gate_up = owned(part_gate_up)
        near = scatter_near(parts, far)
        forward = nn(after(act, far), down).astype(bf16)
        near, forward = phase(near, forward)
        grad_middle, a, b = finish_norm_back(
            out_grad, middle, inverse_mid, [(parts, 0), *near], natural, False
        )
        back_of = [None] * TP

        def attend_back_to(members, *grads):
            results = attend_back(
                members,
                orders,
                out,
                kv_pieces,
                [
                    (qt[k], mixed[k], logsum[k], *g, inverse[k], (cosine, k), (sine, k))
                    for k, g in zip(members, grads)
                ],
            )
            for k, back_of[k] in zip(members, results):
                pass

        attend_back_to((0,), (a, b))
        ax, by, ay, bx, back_of[0] = phase(
            swap(a, 1), swap(b, 2), swap(a, 2), swap(b, 1), back_of[0]
        )
        forward = by_member(forward)
        attend_back_to((1, 2), (ax, bx), (ay, by))
        axy, bxy, far, back_of[1], back_of[2] = phase(
            swap(ax, 2), swap(by, 1), scatter_far(forward), back_of[1], back_of[2]
        )
        keys_near = [
            swap_ctx(jnp.stack([back_of[k][3][(j - 1) * count : j * count] for k in range(3)]), j)
            for j in range(1, ctxs)
        ]
        db_pieces = in_order((a, ax, ay, axy), (b, bx, by, bxy))
        r = lax.axis_index("rep")
        if reps == 2:
            part_out = out_gradient(mixed, db_pieces, 2, 1 - r)
            part_out, axy, bxy = phase(part_out, axy, bxy)
            part_out = lax.ppermute(part_out, "rep", pair)
        attend_back_to((3,), (axy, bxy))
        forward_near = scatter_near(forward, far)
        keys_near, back_of[3], forward_near = phase(keys_near, back_of[3], forward_near)
        keys_last = [
            swap_ctx(back_of[3][3][None, (j - 1) * count : j * count], j) for j in range(1, ctxs)
        ]
        db_pieces = after(db_pieces, back_of[3])
        if reps == 2:
            part_out = out_gradient(mixed, db_pieces, 2, r, part_out)
        else:
            part_out = out_gradient(mixed, db_pieces, 1, jnp.zeros((), jnp.int32))
            part_out = lax.psum_scatter(part_out, "rep", scatter_dimension=0, tiled=True)
        raw_gate_up = collect(after(sum_gate_up, keys_near), t)
        come = send_down(keys_near)
        keys_last, part_out, raw_gate_up, down_come[-1] = phase(
            keys_last, part_out, raw_gate_up, come
        )
        grad_proj, scaled_proj = finish_keys(
            [v[2] for v in back_of],
            keys_near,
            keys_last,
            [v[0] for v in back_of],
            [v[1] for v in back_of],
            inverse,
            cosine,
            sine,
        )
        parts = by_member(nt(grad_proj, qkv).astype(bf16))
        across = phase(*halves(parts[3]))
        far_back = swap(across[0], 2), swap(across[1], 1)
        sent = over_reps_first(x_all, after(scaled_proj, across))
        part_qkv = over_reps_last(x_all, after(scaled_proj, sent), sent)
        sum_out = owned(after(part_out, keys_last))
        far_back, part_qkv, sum_out = phase(far_back, part_qkv, sum_out)
        sum_qkv = owned(part_qkv)
        near = scatter_near(parts, far_back)
        layer_out = finish_layer(after(middle, far_back), [(forward, 0), *forward_near])
        part_down = half_of(after(part_down, far_back), ctxs // 2, False).astype(f32)
        part_down = part_down + jnp.concatenate(down_come, axis=1).astype(f32)
        grad_gate, grad_up, grad_norm_mlp = merge_gate_up(
            t, after(raw_gate_up, far_back), w_gate, w_up, gain_mlp
        )
        near, layer_out, part_down, grad_norm_mlp = phase(
            near, layer_out, part_down, grad_norm_mlp
        )
        (input_grad,) = finish_norm_back(
            grad_middle, tokens, inverse[0], [(parts, 0), *near], natural, True
        )
        sum_qkv = after(sum_qkv, input_grad)
        grad_query, grad_key, grad_value, grad_norm_attn = merge_qkv(
            t, collect(sum_qkv, t), w_query, w_key, w_value, gain_attn
        )
        down_come = swap_ctx(
            half_of(part_down.astype(bf16), ctxs // 4, True), ctxs // 4
        )
        down_come = after(down_come, grad_query)
        sum_down = half_of(part_down, ctxs // 4, False) + down_come.astype(f32)
        return (
            layer_out,
            input_grad,
            grad_norm_attn[0],
            grad_query,
            grad_key,
            grad_value,
            after(sum_out, grad_query).astype(f32),
            grad_norm_mlp[0],
            grad_gate,
            grad_up,
            sum_down,
        )

    return body


def solution(mesh):
    sequences, ctxs = mesh.shape["dp"], mesh.shape["ctx"]
    reps = sequences // TP
    names = ("ty", "tx", "rep", "ctx")
    grid = Mesh(mesh.devices.reshape(2, 2, reps, ctxs), names)
    matrix, vector = P(names, None), P(names)
    order = P(("ty", "tx", "rep"), None)
    weights = [vector, matrix, matrix, matrix, matrix, vector, matrix, matrix, matrix]
    return jax.shard_map(
        make_body(reps, ctxs),
        mesh=grid,
        in_specs=(matrix, order, *weights, matrix),
        out_specs=(matrix, matrix, *weights),
        check_vma=False,
    )
```

```python
import jax
import jax.numpy as jnp
from jax import lax
from jax.experimental import pallas as pl
from jax.experimental.pallas import tpu as pltpu
from jax.sharding import Mesh, PartitionSpec as P

H = 32
KV = 4
HD = 64
TP = 4
GROUP = H // KV
LANES = 128
ROWS = 64
ROOM = 60 << 20
ATTEND_ROOM = 60 << 20
DOWN_STEPS = 4

epsilon = 1e-05
rope_base = 10000.0
masked_score = -1e30
bf16 = jnp.bfloat16
f32 = jnp.float32


def after(value, *others):
    return lax.optimization_barrier((value,) + others)[0]


def phase(*values):
    return lax.optimization_barrier(values)


def nn(left, right):
    return lax.dot_general(left, right, (((1,), (0,)), ((), ())), preferred_element_type=f32)


def nt(left, right):
    return lax.dot_general(left, right, (((1,), (1,)), ((), ())), preferred_element_type=f32)


def tn(left, right):
    return lax.dot_general(left, right, (((0,), (0,)), ((), ())), preferred_element_type=f32)


def like(shape, kind):
    return jax.ShapeDtypeStruct(shape, kind)


def size_of(values):
    return sum(v.size * v.dtype.itemsize for v in values)


def small_call(
    kernel, name, inputs, outputs, flops=0, scratch=(), scalars=0, transcendentals=0, room=ROOM
):
    specs, arrays = [pl.BlockSpec(memory_space=pltpu.SMEM)] * scalars, list(inputs[:scalars])
    for v in inputs[scalars:]:
        if isinstance(v, tuple):
            specs.append(row_block(*v))
            arrays.append(v[0])
        else:
            specs.append(whole_block(v.shape))
            arrays.append(v)
    size = size_of((*arrays, *outputs))
    return pl.pallas_call(
        kernel,
        grid=(1,),
        in_specs=specs,
        out_specs=[whole_block(v.shape) for v in outputs],
        out_shape=outputs,
        scratch_shapes=list(scratch),
        compiler_params=pltpu.CompilerParams(vmem_limit_bytes=room),
        cost_estimate=pl.CostEstimate(
            flops=max(flops, size), bytes_accessed=size, transcendentals=transcendentals
        ),
        name=name,
    )(*arrays)


def row_block(array, index):
    shape = array.shape[1:]
    return pl.BlockSpec((None,) + shape, lambda i: (index,) + (0,) * len(shape))


def whole_block(shape):
    return pl.BlockSpec(shape, lambda i: (0,) * len(shape))


def turn(vectors, cosine, sine):
    half = HD // 2
    out = []
    for at in range(0, vectors.shape[0], HD):
        first, second = vectors[at : at + half], vectors[at + half : at + HD]
        out += [first * cosine - second * sine, second * cosine + first * sine]
    return jnp.concatenate(out, axis=0)


def project(pieces, w, cosine, sine):
    half, width = pieces[0].shape
    rows, n, q = 2 * half, w.shape[1], GROUP * HD

    def kernel(*refs):
        x_refs, (w_ref, cos_ref, sin_ref, kv_ref), outs = refs[:8], refs[8:12], refs[12:]
        for k in range(TP):
            xb = jnp.concatenate([x_refs[2 * k][...], x_refs[2 * k + 1][...]], axis=0)
            x = xb.astype(f32)
            inverse = lax.rsqrt(jnp.mean(x * x, axis=1, keepdims=True) + epsilon)
            outs[TP + k][...] = inverse
            flat = (nn(xb, w_ref[...]) * inverse).T
            cosine, sine = cos_ref[k], sin_ref[k]
            outs[k][...] = (turn(flat[:q], cosine, sine) * HD**-0.5).astype(bf16)
            kv = jnp.concatenate([turn(flat[q : q + HD], cosine, sine), flat[q + HD :]], axis=0)
            kv_ref[k] = kv.T.astype(bf16)

    kv, *outs = small_call(
        kernel,
        "project",
        [*pieces, w, cosine, sine],
        [like((TP, rows, 2 * HD), bf16)]
        + [like((q, rows), bf16)] * TP
        + [like((rows, 1), f32)] * TP,
        flops=2 * TP * rows * width * n,
    )
    return outs[:TP], kv, outs[TP:]


def set_bias(order_ref, k, bias_ref):
    keys, rows = bias_ref.shape
    span = keys // order_ref.shape[1]
    lane = lax.broadcasted_iota(jnp.int32, (span, rows), 1)
    query = jnp.where(lane < span, order_ref[k, 0], order_ref[k, 1] - 1) * span + lane
    row = lax.broadcasted_iota(jnp.int32, (span, rows), 0)
    for b in range(keys // span):
        key = order_ref[k, b] * span + row
        bias_ref[b * span : (b + 1) * span, :] = jnp.where(query >= key, 0.0, masked_score)


def attend(members, orders, queries, kv_pieces, wo, kind):
    n, rows = queries[0].shape
    holders, width = len(kv_pieces), wo.shape[1]
    keys, count = holders * rows, len(members)

    def kernel(order_ref, wo_ref, *refs):
        for i, k in enumerate(members):
            qt_ref, *kv_refs = refs[i * (1 + holders) : (i + 1) * (1 + holders)]
            outs = refs[count * (1 + holders) :]
            ot_ref, lse_ref, part_ref = outs[3 * i : 3 * i + 3]
            bias_ref = outs[-1]
            set_bias(order_ref, k, bias_ref)
            kv = jnp.concatenate([ref[...] for ref in kv_refs], axis=0)
            vt = kv.astype(f32).T[HD:].astype(bf16)
            zero = jnp.zeros((HD, rows), bf16)
            for h in range(GROUP):
                at = slice(h * HD, (h + 1) * HD)
                scores = nn(kv, jnp.concatenate([qt_ref[at, :], zero], axis=0)) + bias_ref[...]
                top = jnp.max(scores, axis=0, keepdims=True)
                exponent = jnp.exp(scores - top)
                total = jnp.sum(exponent, axis=0, keepdims=True)
                ot_ref[at, :] = (nn(vt, exponent.astype(bf16)) / total).astype(bf16)
                lse_ref[h : h + 1, :] = top + jnp.log(total)
            part_ref[...] = tn(ot_ref[...], wo_ref[...]).astype(part_ref.dtype)

    inputs, outputs = [orders, wo], []
    for i, k in enumerate(members):
        inputs += [queries[i], *[(piece, k) for piece in kv_pieces]]
        outputs += [like((n, rows), bf16), like((GROUP, rows), f32), like((rows, width), kind)]
    results = small_call(
        kernel,
        "attend",
        inputs,
        outputs,
        flops=2 * rows * n * (keys * 2 * 4 + width) * count,
        scratch=[pltpu.VMEM((keys, rows), f32)],
        scalars=1,
        transcendentals=GROUP * rows * keys * count,
        room=ATTEND_ROOM,
    )
    return [results[3 * i : 3 * i + 3] for i in range(count)]


def attend_back(members, orders, wo, kv_pieces, details):
    n, rows = details[0][0].shape
    holders, width = len(kv_pieces), wo.shape[1]
    keys, half, count = holders * rows, rows // 2, len(members)
    step = 8 + holders

    def kernel(order_ref, wo_ref, *refs):
        outs, (bias_ref, dat_ref, dqt_ref, dkv_ref) = refs[count * step : -4], refs[-4:]
        for i, k in enumerate(members):
            own = refs[i * step : (i + 1) * step]
            kv_refs, (qt_ref, ot_ref, lse_ref, a_ref, b_ref) = own[:holders], own[holders:-3]
            inv_ref, cos_ref, sin_ref = own[-3:]
            dq_ref, dqs_ref, own_ref, far_ref = outs[4 * i : 4 * i + 4]
            set_bias(order_ref, k, bias_ref)
            kv = jnp.concatenate([ref[...] for ref in kv_refs], axis=0)
            kt = kv.astype(f32).T[:HD].astype(bf16)
            zero = jnp.zeros((HD, rows), bf16)
            dat_ref[:, :half] = nt(wo_ref[...], a_ref[...]).astype(bf16)
            dat_ref[:, half:] = nt(wo_ref[...], b_ref[...]).astype(bf16)
            for h in range(GROUP):
                at = slice(h * HD, (h + 1) * HD)
                q_low = jnp.concatenate([qt_ref[at, :], zero], axis=0)
                da_high = jnp.concatenate([zero, dat_ref[at, :]], axis=0)
                weights = jnp.exp(nn(kv, q_low) + bias_ref[...] - lse_ref[h : h + 1, :])
                delta = jnp.sum(
                    dat_ref[at, :].astype(f32) * ot_ref[at, :].astype(f32), axis=0, keepdims=True
                )
                ds = (weights * (nn(kv, da_high) - delta)).astype(bf16)
                dkv = nt(ds, q_low) + nt(weights.astype(bf16), da_high)
                if h == 0:
                    dkv_ref[...] = dkv
                else:
                    dkv_ref[...] += dkv
                dqt_ref[at, :] = nn(kt, ds)
            dq = (turn(dqt_ref[...], cos_ref[...], -sin_ref[...]) * HD**-0.5).T
            dq_ref[...] = dq.astype(bf16)
            dqs_ref[...] = (dq * inv_ref[...]).astype(bf16)
            own_ref[...] = dkv_ref[:rows, :]
            far_ref[...] = dkv_ref[rows:, :].astype(bf16)

    inputs, outputs = [orders, wo], []
    for k, detail in zip(members, details):
        inputs += [*[(piece, k) for piece in kv_pieces], *detail]
        outputs += [
            like((rows, n), bf16),
            like((rows, n), bf16),
            like((rows, 2 * HD), f32),
            like((keys - rows, 2 * HD), bf16),
        ]
    results = small_call(
        kernel,
        "attend_back",
        inputs,
        outputs,
        flops=2 * rows * n * (keys * 5 * 4 + width) * count,
        scratch=[
            pltpu.VMEM((keys, rows), f32),
            pltpu.VMEM((n, rows), bf16),
            pltpu.VMEM((n, rows), f32),
            pltpu.VMEM((keys, 2 * HD), f32),
        ],
        scalars=1,
        transcendentals=GROUP * rows * keys * count,
        room=ATTEND_ROOM,
    )
    return [results[4 * i : 4 * i + 4] for i in range(count)]


def out_gradient(mixed, grads, parts, index, come=None):
    n, width = mixed[0].shape[0] // parts, grads[0].shape[1]

    def kernel(index_ref, *refs):
        at = pl.ds(pl.multiple_of(index_ref[0] * n, n), n)
        total = 0.0 if come is None else refs[3 * TP][...].astype(f32)
        for k in range(TP):
            db = jnp.concatenate([refs[TP + 2 * k][...], refs[TP + 2 * k + 1][...]], axis=0)
            total = total + nn(refs[k][at, :], db)
        refs[-1][...] = total.astype(bf16)

    return small_call(
        kernel,
        "out_gradient",
        [index[None], *mixed, *grads] + ([] if come is None else [come]),
        [like((n, width), bf16)],
        flops=2 * TP * mixed[0].shape[1] * n * width,
        scalars=1,
    )[0]


def finish_keys(own, near, last, dq, dqs, inverse, cosine, sine):
    rows, n = dq[0].shape

    def kernel(*refs):
        own_refs, refs = refs[:TP], refs[TP:]
        near_refs, refs = refs[: len(near)], refs[len(near) :]
        last_refs, refs = refs[: len(last)], refs[len(last) :]
        dq_refs, dqs_refs, refs = refs[:TP], refs[TP : 2 * TP], refs[2 * TP :]
        inv_refs, (cos_ref, sin_ref, plain_ref, scaled_ref) = refs[:TP], refs[TP:]
        for k in range(TP):
            total = own_refs[k][...]
            for ref in near_refs if k < TP - 1 else last_refs:
                total = total + ref[k % (TP - 1)].astype(f32)
            total = total.T
            keys = turn(total[:HD], cos_ref[k], -sin_ref[k])
            total = jnp.concatenate([keys, total[HD:]], axis=0).T
            at = slice(k * rows, (k + 1) * rows)
            plain_ref[at, :n] = dq_refs[k][...]
            plain_ref[at, n:] = total.astype(bf16)
            scaled_ref[at, :n] = dqs_refs[k][...]
            scaled_ref[at, n:] = (total * inv_refs[k][...]).astype(bf16)

    shape = like((TP * rows, n + 2 * HD), bf16)
    return small_call(
        kernel,
        "finish_keys",
        [*own, *near, *last, *dq, *dqs, *inverse, cosine, sine],
        [shape, shape],
    )


def join_rows(pieces):
    rows, width = pieces[0].shape

    def kernel(*refs):
        for i, ref in enumerate(refs[:-1]):
            refs[-1][i * rows : (i + 1) * rows, :] = ref[...]

    return small_call(
        kernel, "join_rows", pieces, [like((len(pieces) * rows, width), pieces[0].dtype)]
    )[0]


def reorder_lanes(v, ordered):
    order, size = ordered
    return jnp.concatenate([v[:, i * size : (i + 1) * size] for i in order], axis=1)


def block_orders(width, holders):
    held = [m * holders + h for h in range(holders) for m in range(TP)]
    natural = [held.index(i) for i in range(len(held))]
    size = width // len(held)
    return (held, size), (natural, size)


def hold_tokens(tokens, held):
    half = tokens.shape[0] // 2

    def kernel(x_ref, a_ref, b_ref):
        a_ref[...] = reorder_lanes(x_ref[:half, :].astype(f32), held).astype(bf16)
        b_ref[...] = reorder_lanes(x_ref[half:, :].astype(f32), held).astype(bf16)

    shape = like((half, tokens.shape[1]), bf16)
    return small_call(kernel, "hold_tokens", [tokens], [shape, shape])


def summed(refs, at, half):
    own_ref, a2_ref, a1_ref, b1_ref, b2_ref = refs
    first, second = (a2_ref, a1_ref) if at < half else (b1_ref, b2_ref)
    come = slice(at % half, at % half + ROWS)
    total = own_ref[at : at + ROWS, :].astype(f32)
    return total + first[come, :].astype(f32) + second[come, :].astype(f32)


def finish_middle(tokens, pieces, held):
    rows, width = tokens.shape
    half = rows // 2

    def kernel(x_ref, *refs):
        sums, (mid_ref, inv_ref, a_ref, b_ref) = refs[:5], refs[5:]
        for at in range(0, rows, ROWS):
            here = slice(at, at + ROWS)
            middle = x_ref[here, :].astype(f32) + summed(sums, at, half)
            inverse = lax.rsqrt(jnp.mean(middle * middle, axis=1, keepdims=True) + epsilon)
            mid_ref[here, :] = middle
            inv_ref[here, :] = inverse
            out = a_ref if at < half else b_ref
            come = slice(at % half, at % half + ROWS)
            out[come, :] = reorder_lanes(middle * inverse, held).astype(bf16)

    return small_call(
        kernel,
        "finish_middle",
        [tokens, *pieces],
        [
            like((rows, width), f32),
            like((rows, 1), f32),
            like((half, width), bf16),
            like((half, width), bf16),
        ],
    )


def finish_norm_back(grad, normed_from, inverse, pieces, natural, last):
    rows, width = grad.shape
    half = rows // 2

    def kernel(g_ref, x_ref, inv_ref, *refs):
        sums, outs = refs[:5], refs[5:]
        for at in range(0, rows, ROWS):
            here = slice(at, at + ROWS)
            scaled = reorder_lanes(summed(sums, at, half), natural)
            inverse = inv_ref[here, :]
            normed = x_ref[here, :].astype(f32) * inverse
            mean = jnp.mean(scaled * normed, axis=1, keepdims=True)
            total = g_ref[here, :].astype(f32) + inverse * (scaled - normed * mean)
            outs[0][here, :] = total
            if not last:
                out = outs[1] if at < half else outs[2]
                out[at % half : at % half + ROWS, :] = total.astype(bf16)

    shapes = [like((rows, width), f32)]
    if not last:
        shapes += [like((half, width), bf16)] * 2
    return small_call(
        kernel, "finish_norm_back", [grad, normed_from, inverse, *pieces], shapes
    )


def finish_layer(middle, pieces):
    rows, width = middle.shape

    def kernel(mid_ref, *refs):
        for at in range(0, rows, ROWS):
            here = slice(at, at + ROWS)
            total = mid_ref[here, :] + summed(refs[:5], at, rows // 2)
            refs[5][here, :] = total.astype(bf16)

    return small_call(
        kernel, "finish_layer", [middle, *pieces], [like((rows, width), bf16)]
    )[0]


def interleaved(i):
    return slice(2 * i * LANES, (2 * i + 1) * LANES), slice((2 * i + 1) * LANES, (2 * i + 2) * LANES)


def activate(pieces, gate_up, tile=256):
    half, width = pieces[0].shape
    total, ff = half * len(pieces), gate_up.shape[1] // 2

    def kernel(*refs):
        n_refs, (w_ref, m_ref, slope_ref, n2_ref) = refs[: len(pieces)], refs[len(pieces) :]

        @pl.when(pl.program_id(0) == 0)
        def _():
            for i, ref in enumerate(n_refs):
                n2_ref[i * half : (i + 1) * half, :] = ref[...]

        both = nn(n2_ref[...], w_ref[...])
        for i in range(tile // LANES):
            gate_at, up_at = interleaved(i)
            gate, up = both[:, gate_at], both[:, up_at]
            sigmoid = jax.nn.sigmoid(gate)
            silu = gate * sigmoid
            m_ref[:, i * LANES : (i + 1) * LANES] = (silu * up).astype(bf16)
            slope_ref[:, gate_at] = (up * (sigmoid + silu * (1.0 - sigmoid))).astype(bf16)
            slope_ref[:, up_at] = silu.astype(bf16)

    return pl.pallas_call(
        kernel,
        grid=(pl.cdiv(ff, tile),),
        in_specs=[whole_block(v.shape) for v in pieces]
        + [pl.BlockSpec((width, 2 * tile), lambda j: (0, j))],
        out_specs=[
            pl.BlockSpec((total, tile), lambda j: (0, j)),
            pl.BlockSpec((total, 2 * tile), lambda j: (0, j)),
        ],
        out_shape=[like((total, ff), bf16), like((total, 2 * ff), bf16)],
        scratch_shapes=[pltpu.VMEM((total, width), bf16)],
        compiler_params=pltpu.CompilerParams(vmem_limit_bytes=ROOM),
        cost_estimate=pl.CostEstimate(
            flops=4 * total * width * ff,
            bytes_accessed=2 * (total * width + 2 * width * ff + 3 * total * ff),
            transcendentals=total * ff,
        ),
        name="activate",
    )(*pieces, gate_up)


def activate_back(g, down, slopes, tile=256):
    total, width = g.shape
    ff = down.shape[0]

    def kernel(g_ref, down_ref, slope_ref, d_ref):
        dm = nt(g_ref[...], down_ref[...])
        for i in range(tile // LANES):
            part = dm[:, i * LANES : (i + 1) * LANES]
            for at in interleaved(i):
                d_ref[:, at] = (part * slope_ref[:, at].astype(f32)).astype(bf16)

    return pl.pallas_call(
        kernel,
        grid=(pl.cdiv(ff, tile),),
        in_specs=[
            pl.BlockSpec((total, width), lambda j: (0, 0)),
            pl.BlockSpec((tile, width), lambda j: (j, 0)),
            pl.BlockSpec((total, 2 * tile), lambda j: (0, j)),
        ],
        out_specs=pl.BlockSpec((total, 2 * tile), lambda j: (0, j)),
        out_shape=like((total, 2 * ff), bf16),
        compiler_params=pltpu.CompilerParams(vmem_limit_bytes=ROOM),
        cost_estimate=pl.CostEstimate(
            flops=2 * total * width * ff,
            bytes_accessed=2 * (total * width + width * ff + 4 * total * ff),
            transcendentals=0,
        ),
        name="activate_back",
    )(g, down, slopes)


def weight_grad(left, right, index, come=None):
    total, width = left.shape
    n = right.shape[1]
    rows, columns = width // 4, n // 2 if n % (2 * LANES) == 0 else n

    def kernel(index_ref, left_ref, right_ref, *refs):
        part = tn(left_ref[...], right_ref[...])
        if come is not None:
            part = part + refs[0][...].astype(f32)
        refs[-1][...] = part.astype(bf16)

    out = pl.BlockSpec((rows, columns), lambda i, j, index: (i, j))
    more = [] if come is None else [come]
    return pl.pallas_call(
        kernel,
        grid_spec=pltpu.PrefetchScalarGridSpec(
            num_scalar_prefetch=1,
            grid=(2, n // columns),
            in_specs=[
                pl.BlockSpec((total, rows), lambda i, j, index: (0, 2 * index[0] + i)),
                pl.BlockSpec((total, columns), lambda i, j, index: (0, j)),
            ]
            + [out] * len(more),
            out_specs=out,
        ),
        out_shape=like((width // 2, n), bf16),
        compiler_params=pltpu.CompilerParams(vmem_limit_bytes=ROOM),
        cost_estimate=pl.CostEstimate(
            flops=total * width * n,
            bytes_accessed=total * width + 2 * total * n + 2 * width * n,
            transcendentals=0,
        ),
        name="weight_grad",
    )(index[None], left, right, *more)


def split_qkv(w_query, w_key, w_value, gain):
    own, n = w_query.shape[0], GROUP * HD

    def kernel(q_ref, k_ref, v_ref, gain_ref, out_ref):
        for g in range(TP):
            parts = [ref[:, g * HD : (g + 1) * HD].astype(f32) for ref in (k_ref, v_ref)]
            query = q_ref[:, g * n : (g + 1) * n].astype(f32)
            out_ref[g, :, :n] = (query * gain_ref[...]).astype(bf16)
            out_ref[g, :, n:] = (jnp.concatenate(parts, axis=1) * gain_ref[...]).astype(bf16)

    return small_call(
        kernel,
        "split_qkv",
        [w_query, w_key, w_value, gain],
        [like((TP, own, n + 2 * HD), bf16)],
    )[0]


def merge_qkv(t, pieces, w_query, w_key, w_value, gain):
    own, n = w_query.shape[0], GROUP * HD

    def kernel(t_ref, *refs):
        in_refs, (q_ref, k_ref, v_ref, gain_ref, dq_ref, dk_ref, dv_ref, dgain_ref) = (
            refs[:TP],
            refs[TP:],
        )
        slot = lax.broadcasted_iota(jnp.int32, (own, TP * HD), 1) // HD
        dgain = jnp.zeros((own, 1), f32)
        keys, values = 0.0, 0.0
        for k, ref in enumerate(in_refs):
            group = t_ref[0] ^ k
            here = pl.ds(pl.multiple_of(group * n, n), n)
            part = ref[:, :n].astype(f32)
            dgain += jnp.sum(part * q_ref[:, here].astype(f32), axis=1, keepdims=True)
            dq_ref[:, here] = part * gain_ref[...]
            part = ref[:, n:].astype(f32)
            mine = slot == group
            keys += jnp.where(mine, jnp.concatenate([part[:, :HD]] * TP, axis=1), 0.0)
            values += jnp.where(mine, jnp.concatenate([part[:, HD:]] * TP, axis=1), 0.0)
        for part, ref, out_ref in ((keys, k_ref, dk_ref), (values, v_ref, dv_ref)):
            dgain += jnp.sum(part * ref[...].astype(f32), axis=1, keepdims=True)
            out_ref[...] = part * gain_ref[...]
        dgain_ref[...] = dgain.T

    return small_call(
        kernel,
        "merge_qkv",
        [t[None], *pieces, w_query, w_key, w_value, gain],
        [like(w.shape, f32) for w in (w_query, w_key, w_value)] + [like((1, own), f32)],
        scalars=1,
    )


def split_gate_up(w_gate, w_up, gain):
    own, total = w_gate.shape
    ff = total // TP

    def kernel(gate_ref, up_ref, gain_ref, out_ref):
        for g in range(TP):
            for j in range(ff // LANES):
                here = slice(g * ff + j * LANES, g * ff + (j + 1) * LANES)
                for ref, at in zip((gate_ref, up_ref), interleaved(j)):
                    out_ref[g, :, at] = (ref[:, here].astype(f32) * gain_ref[...]).astype(bf16)

    return small_call(
        kernel,
        "split_gate_up",
        [w_gate, w_up, gain],
        [jax.ShapeDtypeStruct((TP, own, 2 * ff), bf16)],
    )[0]


def merge_gate_up(t, pieces, w_gate, w_up, gain):
    own, total = w_gate.shape
    ff = total // TP

    def kernel(t_ref, *refs):
        in_refs, (gate_ref, up_ref, gain_ref, dgate_ref, dup_ref, dgain_ref) = refs[:TP], refs[TP:]
        dgain = jnp.zeros((own, LANES), f32)
        for k, in_ref in enumerate(in_refs):
            base = (t_ref[0] ^ k) * ff
            for j in range(ff // LANES):
                here = pl.ds(pl.multiple_of(base + j * LANES, LANES), LANES)
                for ref, out_ref, at in zip(
                    (gate_ref, up_ref), (dgate_ref, dup_ref), interleaved(j)
                ):
                    part = in_ref[:, at].astype(f32)
                    dgain += part * ref[:, here].astype(f32)
                    out_ref[:, here] = part * gain_ref[...]
        dgain_ref[...] = jnp.sum(dgain, axis=1, keepdims=True).T

    return small_call(
        kernel,
        "merge_gate_up",
        [t[None], *pieces, w_gate, w_up, gain],
        [like((own, total), f32), like((own, total), f32), like((1, own), f32)],
        scalars=1,
    )


def make_body(reps, ctxs):
    pair = [(0, 1), (1, 0)]

    def swap(v, k):
        if k == 0:
            return v
        if k == 1:
            return lax.ppermute(v, "tx", pair)
        if k == 2:
            return lax.ppermute(v, "ty", pair)
        return lax.ppermute(v, ("ty", "tx"), [(i, i ^ 3) for i in range(TP)])

    def swap_ctx(v, j):
        return lax.ppermute(v, "ctx", [(i, i ^ j) for i in range(ctxs)]) if j else v

    def halves(v):
        half = v.shape[0] // 2
        return v[:half], v[half:]

    def in_order(a, b):
        return [p for k in range(TP) for p in (a[k], b[k])]

    def gather(a, b):
        ax, by = swap(a, 1), swap(b, 2)
        ay, bx = swap(a, 2), swap(b, 1)
        return in_order((a, ax, ay, swap(ax, 2)), (b, bx, by, swap(by, 1)))

    def scatter_far(parts):
        a, b = halves(parts[3])
        return swap(a, 2), swap(b, 1)

    def scatter_near(parts, far):
        a1, b1 = halves(parts[1])
        a2, b2 = halves(parts[2])
        a1 = (a1.astype(f32) + far[0].astype(f32)).astype(bf16)
        b2 = (b2.astype(f32) + far[1].astype(f32)).astype(bf16)
        return [swap(a2, 2), swap(a1, 1), swap(b1, 1), swap(b2, 2)]

    def by_member(v):
        return v.reshape(TP, -1, v.shape[1])

    def exchange(blocks, t, *first):
        out = jnp.zeros_like(blocks)
        for k in range(TP):
            come = swap(lax.dynamic_index_in_dim(blocks, t ^ k, 0, keepdims=True), k)
            come = after(come, *first) if first else come
            out = lax.dynamic_update_slice_in_dim(out, come, t ^ k, 0)
        return out

    def spread(blocks, t, *first):
        return exchange(blocks, t, *first).reshape(-1, blocks.shape[2])

    def collect(summed_rows, t):
        blocks = summed_rows.reshape(TP, -1, summed_rows.shape[1])
        return [swap(lax.dynamic_index_in_dim(blocks, t ^ k, 0, False), k) for k in range(TP)]

    def whole(v):
        return lax.all_gather(v, ("rep", "ctx"), axis=0, tiled=True)

    def over_reps_first(left, right):
        if reps != 2:
            return tn(left, right).astype(bf16)
        index = 1 - lax.axis_index("rep")
        half = left.shape[1] // 2
        if half % (2 * LANES) == 0:
            return weight_grad(left, right, index)
        return tn(lax.dynamic_slice_in_dim(left, index * half, half, 1), right).astype(bf16)

    def over_reps_last(left, right, first):
        if reps != 2:
            return lax.psum_scatter(first, "rep", scatter_dimension=0, tiled=True)
        index = lax.axis_index("rep")
        half = left.shape[1] // 2
        come = lax.ppermute(first, "rep", pair)
        if half % (2 * LANES) == 0:
            return weight_grad(left, right, index, come)
        mine = lax.dynamic_slice_in_dim(left, index * half, half, 1)
        return (tn(mine, right) + come.astype(f32)).astype(bf16)

    def over_reps(left, right):
        return over_reps_last(left, right, over_reps_first(left, right))

    def owned(part):
        return lax.psum_scatter(part, "ctx", scatter_dimension=0, tiled=True)

    def half_of(v, j, other):
        index = lax.axis_index("ctx") // j % 2
        v = v.reshape(2, -1, v.shape[1])
        return lax.dynamic_index_in_dim(v, 1 - index if other else index, 0, False)

    def body(
        tokens,
        span_order,
        norm_attn,
        w_query,
        w_key,
        w_value,
        w_out,
        norm_mlp,
        w_gate,
        w_up,
        w_down,
        out_grad,
    ):
        count, width = tokens.shape
        held, natural = block_orders(width, reps * ctxs)
        span = count * ctxs // span_order.shape[1]
        per = count // span
        t = 2 * lax.axis_index("ty") + lax.axis_index("tx")
        c = lax.axis_index("ctx")
        gain_attn = norm_attn.astype(f32)[:, None]
        gain_mlp = norm_mlp.astype(f32)[:, None]

        qkv_blocks = split_qkv(w_query, w_key, w_value, gain_attn)
        a, b = hold_tokens(after(tokens, qkv_blocks), held)
        qkv_mine, a, b = phase(spread(after(qkv_blocks, a), t), a, b)
        qkv = whole(qkv_mine)
        out = whole(after(w_out, qkv_mine))
        ax, by = swap(a, 1), swap(b, 2)
        ax, by, a, b = phase(ax, by, a, b)
        gate_up_blocks = split_gate_up(after(w_gate, ax), w_up, gain_mlp)
        orders = [swap(after(span_order, qkv_mine), k) for k in range(TP)]
        ay, bx, axy, bxy = swap(a, 2), swap(b, 1), swap(ax, 2), swap(by, 1)
        ay, bx, axy, bxy, gate_up_blocks = phase(ay, bx, axy, bxy, gate_up_blocks)
        x_pieces = in_order((a, ax, ay, axy), (b, bx, by, bxy))

        orders = jnp.concatenate(orders, axis=0).reshape(TP, ctxs, per)
        orders = jnp.concatenate(
            [lax.dynamic_slice_in_dim(orders, c ^ j, 1, 1) for j in range(ctxs)], axis=1
        ).reshape(TP, ctxs * per)
        positions = orders[:, :per, None] * span + jnp.arange(span, dtype=jnp.int32)
        half_dim = HD // 2
        frequency = jnp.power(rope_base, -jnp.arange(half_dim, dtype=f32) / half_dim)
        angles = frequency[:, None] * positions.reshape(TP, 1, count).astype(f32)
        cosine, sine = jnp.cos(angles), jnp.sin(angles)

        qt, kv, inverse = project(x_pieces, qkv, cosine, sine)
        gate_up_mine = spread(after(gate_up_blocks, axy, bxy), t, kv)
        kv_far = [swap_ctx(kv, j) for j in range(1, ctxs)]
        ga, gb = halves(after(out_grad, kv))
        kv, kv_far, gate_up_mine, gax, gby, x_all = phase(
            kv, kv_far, gate_up_mine, swap(ga, 1), swap(gb, 2), join_rows(after(x_pieces, kv))
        )
        kv_pieces = [kv, *kv_far]
        gate_up = whole(gate_up_mine)
        down = whole(after(w_down, gate_up_mine))
        mixed, logsum, parts = [None] * TP, [None] * TP, [None] * TP

        def attend_to(members, queries):
            results = attend(
                members,
                orders,
                [queries[k] for k in members],
                kv_pieces,
                out,
                f32 if 0 in members else bf16,
            )
            for k, (mixed[k], logsum[k], parts[k]) in zip(members, results):
                pass

        attend_to((3,), qt)
        queries, gay, gbx = phase(qt, swap(ga, 2), swap(gb, 1), parts[3])[:3]
        far = scatter_far(parts)
        attend_to((2, 1), queries)
        far, parts[1], parts[2], queries, gaxy, gbxy = phase(
            far, parts[1], parts[2], queries, swap(gax, 2), swap(gby, 1)
        )
        near = scatter_near(parts, far)
        attend_to((0,), queries)
        g_all = join_rows(in_order((ga, gax, gay, gaxy), (gb, gbx, gby, gbxy)))
        near, parts[0], g_all = phase(near, parts[0], g_all)
        middle, inverse_mid, a, b = finish_middle(tokens, [parts[0], *near], held)
        n2_pieces = gather(a, b)

        act, slopes = activate(n2_pieces, gate_up)
        n2_all = join_rows(after(n2_pieces, act))
        part_down = over_reps(act, g_all)
        slopes, part_down, n2_all = phase(slopes, part_down, n2_all)
        down_sent = jnp.split(half_of(part_down, ctxs // 2, True), DOWN_STEPS, axis=1)
        down_come = []

        def send_down(*first):
            piece = after(down_sent[len(down_come)], *first)
            down_come.append(swap_ctx(piece, ctxs // 2))
            return down_come[-1]

        grad_act = activate_back(g_all, down, slopes)
        sent = over_reps_first(n2_all, grad_act)
        sent, down_come[-1] = phase(sent, send_down(down))
        parts = by_member(nt(after(grad_act, sent), gate_up).astype(bf16))
        come = send_down(grad_act)
        far = scatter_far(parts)
        part_gate_up = over_reps_last(n2_all, after(grad_act, parts), sent)
        far, part_gate_up, down_come[1], down_come[2] = phase(
            far, part_gate_up, come, send_down(parts)
        )
        sum_gate_up = owned(part_gate_up)
        near = scatter_near(parts, far)
        forward = nn(after(act, far), down).astype(bf16)
        near, forward = phase(near, forward)
        grad_middle, a, b = finish_norm_back(
            out_grad, middle, inverse_mid, [(parts, 0), *near], natural, False
        )
        back_of = [None] * TP

        def attend_back_to(members, *grads):
            results = attend_back(
                members,
                orders,
                out,
                kv_pieces,
                [
                    (qt[k], mixed[k], logsum[k], *g, inverse[k], (cosine, k), (sine, k))
                    for k, g in zip(members, grads)
                ],
            )
            for k, back_of[k] in zip(members, results):
                pass

        attend_back_to((0,), (a, b))
        ax, by, ay, bx, back_of[0] = phase(
            swap(a, 1), swap(b, 2), swap(a, 2), swap(b, 1), back_of[0]
        )
        forward = by_member(forward)
        attend_back_to((1, 2), (ax, bx), (ay, by))
        axy, bxy, far, back_of[1], back_of[2] = phase(
            swap(ax, 2), swap(by, 1), scatter_far(forward), back_of[1], back_of[2]
        )
        keys_near = [
            swap_ctx(jnp.stack([back_of[k][3][(j - 1) * count : j * count] for k in range(3)]), j)
            for j in range(1, ctxs)
        ]
        db_pieces = in_order((a, ax, ay, axy), (b, bx, by, bxy))
        r = lax.axis_index("rep")
        if reps == 2:
            part_out = out_gradient(mixed, db_pieces, 2, 1 - r)
            part_out, axy, bxy = phase(part_out, axy, bxy)
            part_out = lax.ppermute(part_out, "rep", pair)
        attend_back_to((3,), (axy, bxy))
        forward_near = scatter_near(forward, far)
        keys_near, back_of[3], forward_near = phase(keys_near, back_of[3], forward_near)
        keys_last = [
            swap_ctx(back_of[3][3][None, (j - 1) * count : j * count], j) for j in range(1, ctxs)
        ]
        db_pieces = after(db_pieces, back_of[3])
        if reps == 2:
            part_out = out_gradient(mixed, db_pieces, 2, r, part_out)
        else:
            part_out = out_gradient(mixed, db_pieces, 1, jnp.zeros((), jnp.int32))
            part_out = lax.psum_scatter(part_out, "rep", scatter_dimension=0, tiled=True)
        raw_gate_up = collect(after(sum_gate_up, keys_near), t)
        come = send_down(keys_near)
        keys_last, part_out, raw_gate_up, down_come[-1] = phase(
            keys_last, part_out, raw_gate_up, come
        )
        grad_proj, scaled_proj = finish_keys(
            [v[2] for v in back_of],
            keys_near,
            keys_last,
            [v[0] for v in back_of],
            [v[1] for v in back_of],
            inverse,
            cosine,
            sine,
        )
        parts = by_member(nt(grad_proj, qkv).astype(bf16))
        across = phase(*halves(parts[3]))
        far_back = swap(across[0], 2), swap(across[1], 1)
        sent = over_reps_first(x_all, after(scaled_proj, across))
        part_qkv = over_reps_last(x_all, after(scaled_proj, sent), sent)
        sum_out = owned(after(part_out, keys_last))
        far_back, part_qkv, sum_out = phase(far_back, part_qkv, sum_out)
        sum_qkv = owned(part_qkv)
        near = scatter_near(parts, far_back)
        layer_out = finish_layer(after(middle, far_back), [(forward, 0), *forward_near])
        part_down = half_of(after(part_down, far_back), ctxs // 2, False).astype(f32)
        part_down = part_down + jnp.concatenate(down_come, axis=1).astype(f32)
        grad_gate, grad_up, grad_norm_mlp = merge_gate_up(
            t, after(raw_gate_up, far_back), w_gate, w_up, gain_mlp
        )
        near, layer_out, part_down, grad_norm_mlp = phase(
            near, layer_out, part_down, grad_norm_mlp
        )
        (input_grad,) = finish_norm_back(
            grad_middle, tokens, inverse[0], [(parts, 0), *near], natural, True
        )
        sum_qkv = after(sum_qkv, input_grad)
        grad_query, grad_key, grad_value, grad_norm_attn = merge_qkv(
            t, collect(sum_qkv, t), w_query, w_key, w_value, gain_attn
        )
        down_come = swap_ctx(
            half_of(part_down.astype(bf16), ctxs // 4, True), ctxs // 4
        )
        down_come = after(down_come, grad_query)
        sum_down = half_of(part_down, ctxs // 4, False) + down_come.astype(f32)
        return (
            layer_out,
            input_grad,
            grad_norm_attn[0],
            grad_query,
            grad_key,
            grad_value,
            after(sum_out, grad_query).astype(f32),
            grad_norm_mlp[0],
            grad_gate,
            grad_up,
            sum_down,
        )

    return body


def solution(mesh):
    sequences, ctxs = mesh.shape["dp"], mesh.shape["ctx"]
    reps = sequences // TP
    names = ("ty", "tx", "rep", "ctx")
    grid = Mesh(mesh.devices.reshape(2, 2, reps, ctxs), names)
    matrix, vector = P(names, None), P(names)
    order = P(("ty", "tx", "rep"), None)
    weights = [vector, matrix, matrix, matrix, matrix, vector, matrix, matrix, matrix]
    return jax.shard_map(
        make_body(reps, ctxs),
        mesh=grid,
        in_specs=(matrix, order, *weights, matrix),
        out_specs=(matrix, matrix, *weights),
        check_vma=False,
    )
```

```python
import jax
import jax.numpy as jnp
from jax import lax
from jax.experimental import pallas as pl
from jax.experimental.pallas import tpu as pltpu
from jax.sharding import Mesh, PartitionSpec as P

H = 32
KV = 4
HD = 64
TP = 4
GROUP = H // KV
LANES = 128
ROWS = 64
ROOM = 60 << 20
ATTEND_ROOM = 32 << 20
DOWN_STEPS = 4

epsilon = 1e-05
rope_base = 10000.0
masked_score = -1e30
bf16 = jnp.bfloat16
f32 = jnp.float32


def after(value, *others):
    return lax.optimization_barrier((value,) + others)[0]


def phase(*values):
    return lax.optimization_barrier(values)


def nn(left, right):
    return lax.dot_general(left, right, (((1,), (0,)), ((), ())), preferred_element_type=f32)


def nt(left, right):
    return lax.dot_general(left, right, (((1,), (1,)), ((), ())), preferred_element_type=f32)


def tn(left, right):
    return lax.dot_general(left, right, (((0,), (0,)), ((), ())), preferred_element_type=f32)


def like(shape, kind):
    return jax.ShapeDtypeStruct(shape, kind)


def size_of(values):
    return sum(v.size * v.dtype.itemsize for v in values)


def small_call(
    kernel, name, inputs, outputs, flops=0, scratch=(), scalars=0, transcendentals=0, room=ROOM
):
    specs, arrays = [pl.BlockSpec(memory_space=pltpu.SMEM)] * scalars, list(inputs[:scalars])
    for v in inputs[scalars:]:
        if isinstance(v, tuple):
            specs.append(row_block(*v))
            arrays.append(v[0])
        else:
            specs.append(whole_block(v.shape))
            arrays.append(v)
    size = size_of((*arrays, *outputs))
    return pl.pallas_call(
        kernel,
        grid=(1,),
        in_specs=specs,
        out_specs=[whole_block(v.shape) for v in outputs],
        out_shape=outputs,
        scratch_shapes=list(scratch),
        compiler_params=pltpu.CompilerParams(vmem_limit_bytes=room),
        cost_estimate=pl.CostEstimate(
            flops=max(flops, size), bytes_accessed=size, transcendentals=transcendentals
        ),
        name=name,
    )(*arrays)


def row_block(array, index):
    shape = array.shape[1:]
    return pl.BlockSpec((None,) + shape, lambda i: (index,) + (0,) * len(shape))


def whole_block(shape):
    return pl.BlockSpec(shape, lambda i: (0,) * len(shape))


def turn(vectors, cosine, sine):
    half = HD // 2
    out = []
    for at in range(0, vectors.shape[0], HD):
        first, second = vectors[at : at + half], vectors[at + half : at + HD]
        out += [first * cosine - second * sine, second * cosine + first * sine]
    return jnp.concatenate(out, axis=0)


def project(pieces, w, cosine, sine):
    half, width = pieces[0].shape
    rows, n, q = 2 * half, w.shape[1], GROUP * HD

    def kernel(*refs):
        x_refs, (w_ref, cos_ref, sin_ref, kv_ref), outs = refs[:8], refs[8:12], refs[12:]
        for k in range(TP):
            xb = jnp.concatenate([x_refs[2 * k][...], x_refs[2 * k + 1][...]], axis=0)
            x = xb.astype(f32)
            inverse = lax.rsqrt(jnp.mean(x * x, axis=1, keepdims=True) + epsilon)
            outs[TP + k][...] = inverse
            flat = (nn(xb, w_ref[...]) * inverse).T
            cosine, sine = cos_ref[k], sin_ref[k]
            outs[k][...] = (turn(flat[:q], cosine, sine) * HD**-0.5).astype(bf16)
            kv = jnp.concatenate([turn(flat[q : q + HD], cosine, sine), flat[q + HD :]], axis=0)
            kv_ref[k] = kv.T.astype(bf16)

    kv, *outs = small_call(
        kernel,
        "project",
        [*pieces, w, cosine, sine],
        [like((TP, rows, 2 * HD), bf16)]
        + [like((q, rows), bf16)] * TP
        + [like((rows, 1), f32)] * TP,
        flops=2 * TP * rows * width * n,
    )
    return outs[:TP], kv, outs[TP:]


def set_bias(order_ref, k, bias_ref):
    keys, rows = bias_ref.shape
    span = keys // order_ref.shape[1]
    lane = lax.broadcasted_iota(jnp.int32, (span, rows), 1)
    query = jnp.where(lane < span, order_ref[k, 0], order_ref[k, 1] - 1) * span + lane
    row = lax.broadcasted_iota(jnp.int32, (span, rows), 0)
    for b in range(keys // span):
        key = order_ref[k, b] * span + row
        bias_ref[b * span : (b + 1) * span, :] = jnp.where(query >= key, 0.0, masked_score)


def attend(members, orders, queries, kv_pieces, wo, kind):
    n, rows = queries[0].shape
    holders, width = len(kv_pieces), wo.shape[1]
    keys, count = holders * rows, len(members)

    def kernel(order_ref, wo_ref, *refs):
        for i, k in enumerate(members):
            qt_ref, *kv_refs = refs[i * (1 + holders) : (i + 1) * (1 + holders)]
            outs = refs[count * (1 + holders) :]
            ot_ref, lse_ref, part_ref = outs[3 * i : 3 * i + 3]
            bias_ref = outs[-1]
            set_bias(order_ref, k, bias_ref)
            kv = jnp.concatenate([ref[...] for ref in kv_refs], axis=0)
            vt = kv.astype(f32).T[HD:].astype(bf16)
            zero = jnp.zeros((HD, rows), bf16)
            for h in range(GROUP):
                at = slice(h * HD, (h + 1) * HD)
                scores = nn(kv, jnp.concatenate([qt_ref[at, :], zero], axis=0)) + bias_ref[...]
                top = jnp.max(scores, axis=0, keepdims=True)
                exponent = jnp.exp(scores - top)
                total = jnp.sum(exponent, axis=0, keepdims=True)
                ot_ref[at, :] = (nn(vt, exponent.astype(bf16)) / total).astype(bf16)
                lse_ref[h : h + 1, :] = top + jnp.log(total)
            part_ref[...] = tn(ot_ref[...], wo_ref[...]).astype(part_ref.dtype)

    inputs, outputs = [orders, wo], []
    for i, k in enumerate(members):
        inputs += [queries[i], *[(piece, k) for piece in kv_pieces]]
        outputs += [like((n, rows), bf16), like((GROUP, rows), f32), like((rows, width), kind)]
    results = small_call(
        kernel,
        "attend",
        inputs,
        outputs,
        flops=2 * rows * n * (keys * 2 * 4 + width) * count,
        scratch=[pltpu.VMEM((keys, rows), f32)],
        scalars=1,
        transcendentals=GROUP * rows * keys * count,
        room=ATTEND_ROOM,
    )
    return [results[3 * i : 3 * i + 3] for i in range(count)]


def attend_back(members, orders, wo, kv_pieces, details):
    n, rows = details[0][0].shape
    holders, width = len(kv_pieces), wo.shape[1]
    keys, half, count = holders * rows, rows // 2, len(members)
    step = 8 + holders

    def kernel(order_ref, wo_ref, *refs):
        outs, (bias_ref, dat_ref, dqt_ref, dkv_ref) = refs[count * step : -4], refs[-4:]
        for i, k in enumerate(members):
            own = refs[i * step : (i + 1) * step]
            kv_refs, (qt_ref, ot_ref, lse_ref, a_ref, b_ref) = own[:holders], own[holders:-3]
            inv_ref, cos_ref, sin_ref = own[-3:]
            dq_ref, dqs_ref, own_ref, far_ref = outs[4 * i : 4 * i + 4]
            set_bias(order_ref, k, bias_ref)
            kv = jnp.concatenate([ref[...] for ref in kv_refs], axis=0)
            kt = kv.astype(f32).T[:HD].astype(bf16)
            zero = jnp.zeros((HD, rows), bf16)
            dat_ref[:, :half] = nt(wo_ref[...], a_ref[...]).astype(bf16)
            dat_ref[:, half:] = nt(wo_ref[...], b_ref[...]).astype(bf16)
            for h in range(GROUP):
                at = slice(h * HD, (h + 1) * HD)
                q_low = jnp.concatenate([qt_ref[at, :], zero], axis=0)
                da_high = jnp.concatenate([zero, dat_ref[at, :]], axis=0)
                weights = jnp.exp(nn(kv, q_low) + bias_ref[...] - lse_ref[h : h + 1, :])
                delta = jnp.sum(
                    dat_ref[at, :].astype(f32) * ot_ref[at, :].astype(f32), axis=0, keepdims=True
                )
                ds = (weights * (nn(kv, da_high) - delta)).astype(bf16)
                dkv = nt(ds, q_low) + nt(weights.astype(bf16), da_high)
                if h == 0:
                    dkv_ref[...] = dkv
                else:
                    dkv_ref[...] += dkv
                dqt_ref[at, :] = nn(kt, ds)
            dq = (turn(dqt_ref[...], cos_ref[...], -sin_ref[...]) * HD**-0.5).T
            dq_ref[...] = dq.astype(bf16)
            dqs_ref[...] = (dq * inv_ref[...]).astype(bf16)
            own_ref[...] = dkv_ref[:rows, :]
            far_ref[...] = dkv_ref[rows:, :].astype(bf16)

    inputs, outputs = [orders, wo], []
    for k, detail in zip(members, details):
        inputs += [*[(piece, k) for piece in kv_pieces], *detail]
        outputs += [
            like((rows, n), bf16),
            like((rows, n), bf16),
            like((rows, 2 * HD), f32),
            like((keys - rows, 2 * HD), bf16),
        ]
    results = small_call(
        kernel,
        "attend_back",
        inputs,
        outputs,
        flops=2 * rows * n * (keys * 5 * 4 + width) * count,
        scratch=[
            pltpu.VMEM((keys, rows), f32),
            pltpu.VMEM((n, rows), bf16),
            pltpu.VMEM((n, rows), f32),
            pltpu.VMEM((keys, 2 * HD), f32),
        ],
        scalars=1,
        transcendentals=GROUP * rows * keys * count,
        room=ATTEND_ROOM,
    )
    return [results[4 * i : 4 * i + 4] for i in range(count)]


def out_gradient(mixed, grads, parts, index, come=None):
    n, width = mixed[0].shape[0] // parts, grads[0].shape[1]

    def kernel(index_ref, *refs):
        at = pl.ds(pl.multiple_of(index_ref[0] * n, n), n)
        total = 0.0 if come is None else refs[3 * TP][...].astype(f32)
        for k in range(TP):
            db = jnp.concatenate([refs[TP + 2 * k][...], refs[TP + 2 * k + 1][...]], axis=0)
            total = total + nn(refs[k][at, :], db)
        refs[-1][...] = total.astype(bf16)

    return small_call(
        kernel,
        "out_gradient",
        [index[None], *mixed, *grads] + ([] if come is None else [come]),
        [like((n, width), bf16)],
        flops=2 * TP * mixed[0].shape[1] * n * width,
        scalars=1,
    )[0]


def finish_keys(own, near, last, dq, dqs, inverse, cosine, sine):
    rows, n = dq[0].shape

    def kernel(*refs):
        own_refs, refs = refs[:TP], refs[TP:]
        near_refs, refs = refs[: len(near)], refs[len(near) :]
        last_refs, refs = refs[: len(last)], refs[len(last) :]
        dq_refs, dqs_refs, refs = refs[:TP], refs[TP : 2 * TP], refs[2 * TP :]
        inv_refs, (cos_ref, sin_ref, plain_ref, scaled_ref) = refs[:TP], refs[TP:]
        for k in range(TP):
            total = own_refs[k][...]
            for ref in near_refs if k < TP - 1 else last_refs:
                total = total + ref[k % (TP - 1)].astype(f32)
            total = total.T
            keys = turn(total[:HD], cos_ref[k], -sin_ref[k])
            total = jnp.concatenate([keys, total[HD:]], axis=0).T
            at = slice(k * rows, (k + 1) * rows)
            plain_ref[at, :n] = dq_refs[k][...]
            plain_ref[at, n:] = total.astype(bf16)
            scaled_ref[at, :n] = dqs_refs[k][...]
            scaled_ref[at, n:] = (total * inv_refs[k][...]).astype(bf16)

    shape = like((TP * rows, n + 2 * HD), bf16)
    return small_call(
        kernel,
        "finish_keys",
        [*own, *near, *last, *dq, *dqs, *inverse, cosine, sine],
        [shape, shape],
    )


def join_rows(pieces):
    rows, width = pieces[0].shape

    def kernel(*refs):
        for i, ref in enumerate(refs[:-1]):
            refs[-1][i * rows : (i + 1) * rows, :] = ref[...]

    return small_call(
        kernel, "join_rows", pieces, [like((len(pieces) * rows, width), pieces[0].dtype)]
    )[0]


def reorder_lanes(v, ordered):
    order, size = ordered
    return jnp.concatenate([v[:, i * size : (i + 1) * size] for i in order], axis=1)


def block_orders(width, holders):
    held = [m * holders + h for h in range(holders) for m in range(TP)]
    natural = [held.index(i) for i in range(len(held))]
    size = width // len(held)
    return (held, size), (natural, size)


def hold_tokens(tokens, held):
    half = tokens.shape[0] // 2

    def kernel(x_ref, a_ref, b_ref):
        a_ref[...] = reorder_lanes(x_ref[:half, :].astype(f32), held).astype(bf16)
        b_ref[...] = reorder_lanes(x_ref[half:, :].astype(f32), held).astype(bf16)

    shape = like((half, tokens.shape[1]), bf16)
    return small_call(kernel, "hold_tokens", [tokens], [shape, shape])


def summed(refs, at, half):
    own_ref, a2_ref, a1_ref, b1_ref, b2_ref = refs
    first, second = (a2_ref, a1_ref) if at < half else (b1_ref, b2_ref)
    come = slice(at % half, at % half + ROWS)
    total = own_ref[at : at + ROWS, :].astype(f32)
    return total + first[come, :].astype(f32) + second[come, :].astype(f32)


def finish_middle(tokens, pieces, held):
    rows, width = tokens.shape
    half = rows // 2

    def kernel(x_ref, *refs):
        sums, (mid_ref, inv_ref, a_ref, b_ref) = refs[:5], refs[5:]
        for at in range(0, rows, ROWS):
            here = slice(at, at + ROWS)
            middle = x_ref[here, :].astype(f32) + summed(sums, at, half)
            inverse = lax.rsqrt(jnp.mean(middle * middle, axis=1, keepdims=True) + epsilon)
            mid_ref[here, :] = middle
            inv_ref[here, :] = inverse
            out = a_ref if at < half else b_ref
            come = slice(at % half, at % half + ROWS)
            out[come, :] = reorder_lanes(middle * inverse, held).astype(bf16)

    return small_call(
        kernel,
        "finish_middle",
        [tokens, *pieces],
        [
            like((rows, width), f32),
            like((rows, 1), f32),
            like((half, width), bf16),
            like((half, width), bf16),
        ],
    )


def finish_norm_back(grad, normed_from, inverse, pieces, natural, last):
    rows, width = grad.shape
    half = rows // 2

    def kernel(g_ref, x_ref, inv_ref, *refs):
        sums, outs = refs[:5], refs[5:]
        for at in range(0, rows, ROWS):
            here = slice(at, at + ROWS)
            scaled = reorder_lanes(summed(sums, at, half), natural)
            inverse = inv_ref[here, :]
            normed = x_ref[here, :].astype(f32) * inverse
            mean = jnp.mean(scaled * normed, axis=1, keepdims=True)
            total = g_ref[here, :].astype(f32) + inverse * (scaled - normed * mean)
            outs[0][here, :] = total
            if not last:
                out = outs[1] if at < half else outs[2]
                out[at % half : at % half + ROWS, :] = total.astype(bf16)

    shapes = [like((rows, width), f32)]
    if not last:
        shapes += [like((half, width), bf16)] * 2
    return small_call(
        kernel, "finish_norm_back", [grad, normed_from, inverse, *pieces], shapes
    )


def finish_layer(middle, pieces):
    rows, width = middle.shape

    def kernel(mid_ref, *refs):
        for at in range(0, rows, ROWS):
            here = slice(at, at + ROWS)
            total = mid_ref[here, :] + summed(refs[:5], at, rows // 2)
            refs[5][here, :] = total.astype(bf16)

    return small_call(
        kernel, "finish_layer", [middle, *pieces], [like((rows, width), bf16)]
    )[0]


def interleaved(i):
    return slice(2 * i * LANES, (2 * i + 1) * LANES), slice((2 * i + 1) * LANES, (2 * i + 2) * LANES)


def activate(pieces, gate_up, tile=256):
    half, width = pieces[0].shape
    total, ff = half * len(pieces), gate_up.shape[1] // 2

    def kernel(*refs):
        n_refs, (w_ref, m_ref, slope_ref, n2_ref) = refs[: len(pieces)], refs[len(pieces) :]

        @pl.when(pl.program_id(0) == 0)
        def _():
            for i, ref in enumerate(n_refs):
                n2_ref[i * half : (i + 1) * half, :] = ref[...]

        both = nn(n2_ref[...], w_ref[...])
        for i in range(tile // LANES):
            gate_at, up_at = interleaved(i)
            gate, up = both[:, gate_at], both[:, up_at]
            sigmoid = jax.nn.sigmoid(gate)
            silu = gate * sigmoid
            m_ref[:, i * LANES : (i + 1) * LANES] = (silu * up).astype(bf16)
            slope_ref[:, gate_at] = (up * (sigmoid + silu * (1.0 - sigmoid))).astype(bf16)
            slope_ref[:, up_at] = silu.astype(bf16)

    return pl.pallas_call(
        kernel,
        grid=(pl.cdiv(ff, tile),),
        in_specs=[whole_block(v.shape) for v in pieces]
        + [pl.BlockSpec((width, 2 * tile), lambda j: (0, j))],
        out_specs=[
            pl.BlockSpec((total, tile), lambda j: (0, j)),
            pl.BlockSpec((total, 2 * tile), lambda j: (0, j)),
        ],
        out_shape=[like((total, ff), bf16), like((total, 2 * ff), bf16)],
        scratch_shapes=[pltpu.VMEM((total, width), bf16)],
        compiler_params=pltpu.CompilerParams(vmem_limit_bytes=ROOM),
        cost_estimate=pl.CostEstimate(
            flops=4 * total * width * ff,
            bytes_accessed=2 * (total * width + 2 * width * ff + 3 * total * ff),
            transcendentals=total * ff,
        ),
        name="activate",
    )(*pieces, gate_up)


def activate_back(g, down, slopes, tile=256):
    total, width = g.shape
    ff = down.shape[0]

    def kernel(g_ref, down_ref, slope_ref, d_ref):
        dm = nt(g_ref[...], down_ref[...])
        for i in range(tile // LANES):
            part = dm[:, i * LANES : (i + 1) * LANES]
            for at in interleaved(i):
                d_ref[:, at] = (part * slope_ref[:, at].astype(f32)).astype(bf16)

    return pl.pallas_call(
        kernel,
        grid=(pl.cdiv(ff, tile),),
        in_specs=[
            pl.BlockSpec((total, width), lambda j: (0, 0)),
            pl.BlockSpec((tile, width), lambda j: (j, 0)),
            pl.BlockSpec((total, 2 * tile), lambda j: (0, j)),
        ],
        out_specs=pl.BlockSpec((total, 2 * tile), lambda j: (0, j)),
        out_shape=like((total, 2 * ff), bf16),
        compiler_params=pltpu.CompilerParams(vmem_limit_bytes=ROOM),
        cost_estimate=pl.CostEstimate(
            flops=2 * total * width * ff,
            bytes_accessed=2 * (total * width + width * ff + 4 * total * ff),
            transcendentals=0,
        ),
        name="activate_back",
    )(g, down, slopes)


def weight_grad(left, right, index, come=None):
    total, width = left.shape
    n = right.shape[1]
    rows, columns = width // 4, n // 2 if n % (2 * LANES) == 0 else n

    def kernel(index_ref, left_ref, right_ref, *refs):
        part = tn(left_ref[...], right_ref[...])
        if come is not None:
            part = part + refs[0][...].astype(f32)
        refs[-1][...] = part.astype(bf16)

    out = pl.BlockSpec((rows, columns), lambda i, j, index: (i, j))
    more = [] if come is None else [come]
    return pl.pallas_call(
        kernel,
        grid_spec=pltpu.PrefetchScalarGridSpec(
            num_scalar_prefetch=1,
            grid=(2, n // columns),
            in_specs=[
                pl.BlockSpec((total, rows), lambda i, j, index: (0, 2 * index[0] + i)),
                pl.BlockSpec((total, columns), lambda i, j, index: (0, j)),
            ]
            + [out] * len(more),
            out_specs=out,
        ),
        out_shape=like((width // 2, n), bf16),
        compiler_params=pltpu.CompilerParams(vmem_limit_bytes=ROOM),
        cost_estimate=pl.CostEstimate(
            flops=total * width * n,
            bytes_accessed=total * width + 2 * total * n + 2 * width * n,
            transcendentals=0,
        ),
        name="weight_grad",
    )(index[None], left, right, *more)


def split_qkv(w_query, w_key, w_value, gain):
    own, n = w_query.shape[0], GROUP * HD

    def kernel(q_ref, k_ref, v_ref, gain_ref, out_ref):
        for g in range(TP):
            parts = [ref[:, g * HD : (g + 1) * HD].astype(f32) for ref in (k_ref, v_ref)]
            query = q_ref[:, g * n : (g + 1) * n].astype(f32)
            out_ref[g, :, :n] = (query * gain_ref[...]).astype(bf16)
            out_ref[g, :, n:] = (jnp.concatenate(parts, axis=1) * gain_ref[...]).astype(bf16)

    return small_call(
        kernel,
        "split_qkv",
        [w_query, w_key, w_value, gain],
        [like((TP, own, n + 2 * HD), bf16)],
    )[0]


def merge_qkv(t, pieces, w_query, w_key, w_value, gain):
    own, n = w_query.shape[0], GROUP * HD

    def kernel(t_ref, *refs):
        in_refs, (q_ref, k_ref, v_ref, gain_ref, dq_ref, dk_ref, dv_ref, dgain_ref) = (
            refs[:TP],
            refs[TP:],
        )
        slot = lax.broadcasted_iota(jnp.int32, (own, TP * HD), 1) // HD
        dgain = jnp.zeros((own, 1), f32)
        keys, values = 0.0, 0.0
        for k, ref in enumerate(in_refs):
            group = t_ref[0] ^ k
            here = pl.ds(pl.multiple_of(group * n, n), n)
            part = ref[:, :n].astype(f32)
            dgain += jnp.sum(part * q_ref[:, here].astype(f32), axis=1, keepdims=True)
            dq_ref[:, here] = part * gain_ref[...]
            part = ref[:, n:].astype(f32)
            mine = slot == group
            keys += jnp.where(mine, jnp.concatenate([part[:, :HD]] * TP, axis=1), 0.0)
            values += jnp.where(mine, jnp.concatenate([part[:, HD:]] * TP, axis=1), 0.0)
        for part, ref, out_ref in ((keys, k_ref, dk_ref), (values, v_ref, dv_ref)):
            dgain += jnp.sum(part * ref[...].astype(f32), axis=1, keepdims=True)
            out_ref[...] = part * gain_ref[...]
        dgain_ref[...] = dgain.T

    return small_call(
        kernel,
        "merge_qkv",
        [t[None], *pieces, w_query, w_key, w_value, gain],
        [like(w.shape, f32) for w in (w_query, w_key, w_value)] + [like((1, own), f32)],
        scalars=1,
    )


def split_gate_up(w_gate, w_up, gain):
    own, total = w_gate.shape
    ff = total // TP

    def kernel(gate_ref, up_ref, gain_ref, out_ref):
        for g in range(TP):
            for j in range(ff // LANES):
                here = slice(g * ff + j * LANES, g * ff + (j + 1) * LANES)
                for ref, at in zip((gate_ref, up_ref), interleaved(j)):
                    out_ref[g, :, at] = (ref[:, here].astype(f32) * gain_ref[...]).astype(bf16)

    return small_call(
        kernel,
        "split_gate_up",
        [w_gate, w_up, gain],
        [jax.ShapeDtypeStruct((TP, own, 2 * ff), bf16)],
    )[0]


def merge_gate_up(t, pieces, w_gate, w_up, gain):
    own, total = w_gate.shape
    ff = total // TP

    def kernel(t_ref, *refs):
        in_refs, (gate_ref, up_ref, gain_ref, dgate_ref, dup_ref, dgain_ref) = refs[:TP], refs[TP:]
        dgain = jnp.zeros((own, LANES), f32)
        for k, in_ref in enumerate(in_refs):
            base = (t_ref[0] ^ k) * ff
            for j in range(ff // LANES):
                here = pl.ds(pl.multiple_of(base + j * LANES, LANES), LANES)
                for ref, out_ref, at in zip(
                    (gate_ref, up_ref), (dgate_ref, dup_ref), interleaved(j)
                ):
                    part = in_ref[:, at].astype(f32)
                    dgain += part * ref[:, here].astype(f32)
                    out_ref[:, here] = part * gain_ref[...]
        dgain_ref[...] = jnp.sum(dgain, axis=1, keepdims=True).T

    return small_call(
        kernel,
        "merge_gate_up",
        [t[None], *pieces, w_gate, w_up, gain],
        [like((own, total), f32), like((own, total), f32), like((1, own), f32)],
        scalars=1,
    )


def make_body(reps, ctxs):
    pair = [(0, 1), (1, 0)]

    def swap(v, k):
        if k == 0:
            return v
        if k == 1:
            return lax.ppermute(v, "tx", pair)
        if k == 2:
            return lax.ppermute(v, "ty", pair)
        return lax.ppermute(v, ("ty", "tx"), [(i, i ^ 3) for i in range(TP)])

    def swap_ctx(v, j):
        return lax.ppermute(v, "ctx", [(i, i ^ j) for i in range(ctxs)]) if j else v

    def halves(v):
        half = v.shape[0] // 2
        return v[:half], v[half:]

    def in_order(a, b):
        return [p for k in range(TP) for p in (a[k], b[k])]

    def gather(a, b):
        ax, by = swap(a, 1), swap(b, 2)
        ay, bx = swap(a, 2), swap(b, 1)
        return in_order((a, ax, ay, swap(ax, 2)), (b, bx, by, swap(by, 1)))

    def scatter_far(parts):
        a, b = halves(parts[3])
        return swap(a, 2), swap(b, 1)

    def scatter_near(parts, far):
        a1, b1 = halves(parts[1])
        a2, b2 = halves(parts[2])
        a1 = (a1.astype(f32) + far[0].astype(f32)).astype(bf16)
        b2 = (b2.astype(f32) + far[1].astype(f32)).astype(bf16)
        return [swap(a2, 2), swap(a1, 1), swap(b1, 1), swap(b2, 2)]

    def by_member(v):
        return v.reshape(TP, -1, v.shape[1])

    def exchange(blocks, t, *first):
        out = jnp.zeros_like(blocks)
        for k in range(TP):
            come = swap(lax.dynamic_index_in_dim(blocks, t ^ k, 0, keepdims=True), k)
            come = after(come, *first) if first else come
            out = lax.dynamic_update_slice_in_dim(out, come, t ^ k, 0)
        return out

    def spread(blocks, t, *first):
        return exchange(blocks, t, *first).reshape(-1, blocks.shape[2])

    def collect(summed_rows, t):
        blocks = summed_rows.reshape(TP, -1, summed_rows.shape[1])
        return [swap(lax.dynamic_index_in_dim(blocks, t ^ k, 0, False), k) for k in range(TP)]

    def whole(v):
        return lax.all_gather(v, ("rep", "ctx"), axis=0, tiled=True)

    def over_reps_first(left, right):
        if reps != 2:
            return tn(left, right).astype(bf16)
        index = 1 - lax.axis_index("rep")
        half = left.shape[1] // 2
        if half % (2 * LANES) == 0:
            return weight_grad(left, right, index)
        return tn(lax.dynamic_slice_in_dim(left, index * half, half, 1), right).astype(bf16)

    def over_reps_last(left, right, first):
        if reps != 2:
            return lax.psum_scatter(first, "rep", scatter_dimension=0, tiled=True)
        index = lax.axis_index("rep")
        half = left.shape[1] // 2
        come = lax.ppermute(first, "rep", pair)
        if half % (2 * LANES) == 0:
            return weight_grad(left, right, index, come)
        mine = lax.dynamic_slice_in_dim(left, index * half, half, 1)
        return (tn(mine, right) + come.astype(f32)).astype(bf16)

    def over_reps(left, right):
        return over_reps_last(left, right, over_reps_first(left, right))

    def owned(part):
        return lax.psum_scatter(part, "ctx", scatter_dimension=0, tiled=True)

    def half_of(v, j, other):
        index = lax.axis_index("ctx") // j % 2
        v = v.reshape(2, -1, v.shape[1])
        return lax.dynamic_index_in_dim(v, 1 - index if other else index, 0, False)

    def body(
        tokens,
        span_order,
        norm_attn,
        w_query,
        w_key,
        w_value,
        w_out,
        norm_mlp,
        w_gate,
        w_up,
        w_down,
        out_grad,
    ):
        count, width = tokens.shape
        held, natural = block_orders(width, reps * ctxs)
        span = count * ctxs // span_order.shape[1]
        per = count // span
        t = 2 * lax.axis_index("ty") + lax.axis_index("tx")
        c = lax.axis_index("ctx")
        gain_attn = norm_attn.astype(f32)[:, None]
        gain_mlp = norm_mlp.astype(f32)[:, None]

        qkv_blocks = split_qkv(w_query, w_key, w_value, gain_attn)
        a, b = hold_tokens(after(tokens, qkv_blocks), held)
        qkv_mine, a, b = phase(spread(after(qkv_blocks, a), t), a, b)
        qkv = whole(qkv_mine)
        out = whole(after(w_out, qkv_mine))
        ax, by = swap(a, 1), swap(b, 2)
        ax, by, a, b = phase(ax, by, a, b)
        gate_up_blocks = split_gate_up(after(w_gate, ax), w_up, gain_mlp)
        orders = [swap(after(span_order, qkv_mine), k) for k in range(TP)]
        ay, bx, axy, bxy = swap(a, 2), swap(b, 1), swap(ax, 2), swap(by, 1)
        ay, bx, axy, bxy, gate_up_blocks = phase(ay, bx, axy, bxy, gate_up_blocks)
        x_pieces = in_order((a, ax, ay, axy), (b, bx, by, bxy))

        orders = jnp.concatenate(orders, axis=0).reshape(TP, ctxs, per)
        orders = jnp.concatenate(
            [lax.dynamic_slice_in_dim(orders, c ^ j, 1, 1) for j in range(ctxs)], axis=1
        ).reshape(TP, ctxs * per)
        positions = orders[:, :per, None] * span + jnp.arange(span, dtype=jnp.int32)
        half_dim = HD // 2
        frequency = jnp.power(rope_base, -jnp.arange(half_dim, dtype=f32) / half_dim)
        angles = frequency[:, None] * positions.reshape(TP, 1, count).astype(f32)
        cosine, sine = jnp.cos(angles), jnp.sin(angles)

        qt, kv, inverse = project(x_pieces, qkv, cosine, sine)
        gate_up_mine = spread(after(gate_up_blocks, axy, bxy), t, kv)
        kv_far = [swap_ctx(kv, j) for j in range(1, ctxs)]
        ga, gb = halves(after(out_grad, kv))
        kv, kv_far, gate_up_mine, gax, gby, x_all = phase(
            kv, kv_far, gate_up_mine, swap(ga, 1), swap(gb, 2), join_rows(after(x_pieces, kv))
        )
        kv_pieces = [kv, *kv_far]
        gate_up = whole(gate_up_mine)
        down = whole(after(w_down, gate_up_mine))
        mixed, logsum, parts = [None] * TP, [None] * TP, [None] * TP

        def attend_to(members, queries):
            results = attend(
                members,
                orders,
                [queries[k] for k in members],
                kv_pieces,
                out,
                f32 if 0 in members else bf16,
            )
            for k, (mixed[k], logsum[k], parts[k]) in zip(members, results):
                pass

        attend_to((3,), qt)
        queries, gay, gbx = phase(qt, swap(ga, 2), swap(gb, 1), parts[3])[:3]
        far = scatter_far(parts)
        attend_to((2, 1), queries)
        far, parts[1], parts[2], queries, gaxy, gbxy = phase(
            far, parts[1], parts[2], queries, swap(gax, 2), swap(gby, 1)
        )
        near = scatter_near(parts, far)
        attend_to((0,), queries)
        g_all = join_rows(in_order((ga, gax, gay, gaxy), (gb, gbx, gby, gbxy)))
        near, parts[0], g_all = phase(near, parts[0], g_all)
        middle, inverse_mid, a, b = finish_middle(tokens, [parts[0], *near], held)
        n2_pieces = gather(a, b)

        act, slopes = activate(n2_pieces, gate_up)
        n2_all = join_rows(after(n2_pieces, act))
        part_down = over_reps(act, g_all)
        slopes, part_down, n2_all = phase(slopes, part_down, n2_all)
        down_sent = jnp.split(half_of(part_down, ctxs // 2, True), DOWN_STEPS, axis=1)
        down_come = []

        def send_down(*first):
            piece = after(down_sent[len(down_come)], *first)
            down_come.append(swap_ctx(piece, ctxs // 2))
            return down_come[-1]

        grad_act = activate_back(g_all, down, slopes)
        sent = over_reps_first(n2_all, grad_act)
        sent, down_come[-1] = phase(sent, send_down(down))
        parts = by_member(nt(after(grad_act, sent), gate_up).astype(bf16))
        come = send_down(grad_act)
        far = scatter_far(parts)
        part_gate_up = over_reps_last(n2_all, after(grad_act, parts), sent)
        far, part_gate_up, down_come[1], down_come[2] = phase(
            far, part_gate_up, come, send_down(parts)
        )
        sum_gate_up = owned(part_gate_up)
        near = scatter_near(parts, far)
        forward = nn(after(act, far), down).astype(bf16)
        near, forward = phase(near, forward)
        grad_middle, a, b = finish_norm_back(
            out_grad, middle, inverse_mid, [(parts, 0), *near], natural, False
        )
        back_of = [None] * TP

        def attend_back_to(members, *grads):
            results = attend_back(
                members,
                orders,
                out,
                kv_pieces,
                [
                    (qt[k], mixed[k], logsum[k], *g, inverse[k], (cosine, k), (sine, k))
                    for k, g in zip(members, grads)
                ],
            )
            for k, back_of[k] in zip(members, results):
                pass

        attend_back_to((0,), (a, b))
        ax, by, ay, bx, back_of[0] = phase(
            swap(a, 1), swap(b, 2), swap(a, 2), swap(b, 1), back_of[0]
        )
        forward = by_member(forward)
        attend_back_to((1, 2), (ax, bx), (ay, by))
        axy, bxy, far, back_of[1], back_of[2] = phase(
            swap(ax, 2), swap(by, 1), scatter_far(forward), back_of[1], back_of[2]
        )
        keys_near = [
            swap_ctx(jnp.stack([back_of[k][3][(j - 1) * count : j * count] for k in range(3)]), j)
            for j in range(1, ctxs)
        ]
        db_pieces = in_order((a, ax, ay, axy), (b, bx, by, bxy))
        r = lax.axis_index("rep")
        if reps == 2:
            part_out = out_gradient(mixed, db_pieces, 2, 1 - r)
            part_out, axy, bxy = phase(part_out, axy, bxy)
            part_out = lax.ppermute(part_out, "rep", pair)
        attend_back_to((3,), (axy, bxy))
        forward_near = scatter_near(forward, far)
        keys_near, back_of[3], forward_near = phase(keys_near, back_of[3], forward_near)
        keys_last = [
            swap_ctx(back_of[3][3][None, (j - 1) * count : j * count], j) for j in range(1, ctxs)
        ]
        db_pieces = after(db_pieces, back_of[3])
        if reps == 2:
            part_out = out_gradient(mixed, db_pieces, 2, r, part_out)
        else:
            part_out = out_gradient(mixed, db_pieces, 1, jnp.zeros((), jnp.int32))
            part_out = lax.psum_scatter(part_out, "rep", scatter_dimension=0, tiled=True)
        raw_gate_up = collect(after(sum_gate_up, keys_near), t)
        come = send_down(keys_near)
        keys_last, part_out, raw_gate_up, down_come[-1] = phase(
            keys_last, part_out, raw_gate_up, come
        )
        grad_proj, scaled_proj = finish_keys(
            [v[2] for v in back_of],
            keys_near,
            keys_last,
            [v[0] for v in back_of],
            [v[1] for v in back_of],
            inverse,
            cosine,
            sine,
        )
        parts = by_member(nt(grad_proj, qkv).astype(bf16))
        across = phase(*halves(parts[3]))
        far_back = swap(across[0], 2), swap(across[1], 1)
        sent = over_reps_first(x_all, after(scaled_proj, across))
        part_qkv = over_reps_last(x_all, after(scaled_proj, sent), sent)
        sum_out = owned(after(part_out, keys_last))
        far_back, part_qkv, sum_out = phase(far_back, part_qkv, sum_out)
        sum_qkv = owned(part_qkv)
        near = scatter_near(parts, far_back)
        layer_out = finish_layer(after(middle, far_back), [(forward, 0), *forward_near])
        part_down = half_of(after(part_down, far_back), ctxs // 2, False).astype(f32)
        part_down = part_down + jnp.concatenate(down_come, axis=1).astype(f32)
        grad_gate, grad_up, grad_norm_mlp = merge_gate_up(
            t, after(raw_gate_up, far_back), w_gate, w_up, gain_mlp
        )
        near, layer_out, part_down, grad_norm_mlp = phase(
            near, layer_out, part_down, grad_norm_mlp
        )
        (input_grad,) = finish_norm_back(
            grad_middle, tokens, inverse[0], [(parts, 0), *near], natural, True
        )
        sum_qkv = after(sum_qkv, input_grad)
        grad_query, grad_key, grad_value, grad_norm_attn = merge_qkv(
            t, collect(sum_qkv, t), w_query, w_key, w_value, gain_attn
        )
        down_come = swap_ctx(
            half_of(part_down.astype(bf16), ctxs // 4, True), ctxs // 4
        )
        down_come = after(down_come, grad_query)
        sum_down = half_of(part_down, ctxs // 4, False) + down_come.astype(f32)
        return (
            layer_out,
            input_grad,
            grad_norm_attn[0],
            grad_query,
            grad_key,
            grad_value,
            after(sum_out, grad_query).astype(f32),
            grad_norm_mlp[0],
            grad_gate,
            grad_up,
            sum_down,
        )

    return body


def solution(mesh):
    sequences, ctxs = mesh.shape["dp"], mesh.shape["ctx"]
    reps = sequences // TP
    names = ("ty", "tx", "rep", "ctx")
    grid = Mesh(mesh.devices.reshape(2, 2, reps, ctxs), names)
    matrix, vector = P(names, None), P(names)
    order = P(("ty", "tx", "rep"), None)
    weights = [vector, matrix, matrix, matrix, matrix, vector, matrix, matrix, matrix]
    return jax.shard_map(
        make_body(reps, ctxs),
        mesh=grid,
        in_specs=(matrix, order, *weights, matrix),
        out_specs=(matrix, matrix, *weights),
        check_vma=False,
    )
```
